32 devices in a mesh: box: 8 (over z, x), col: 4 (over y, core).
Axes of the slice: x: 2, y: 2, z: 4, core: 2. Of those that a mesh axis runs over, the one named last changes fastest.
Arguments:
- density: bfloat16 [1024, 16, 456], P('box'), may hold values from -6 to 6
- export_ids: int32 [8, 8, 4], P('box'), may hold values from -1 to 127, as said below
- list_slot: int32 [1024, 64], P('box'), may hold values from -1 to 31, as said below
- translations: bfloat16 [64, 456, 456], P('col'), may hold values from -0.046875 to 0.046875
- patch_points: int32 [64, 1024], P('box'), may hold values from 0 to 466943, as said below
- inverses: bfloat16 [64, 1024, 1024], P('box'), may hold values from -0.1875 to 0.1875
Outputs:
- field: bfloat16 [1024, 16, 456], P('box', 'col')
- corrected: bfloat16 [1024, 16, 456], P('box', 'col')
The draws below stay inside these ranges and needn't reach their ends.
Inputs may be any that keep to these rules, and one draw needn't show every extreme that they name: export_ids[s, d, c] is one of device s's boxes (an index below 128 within s's boxes) or -1 for an empty slot; the boxes of one pair (s, d) are distinct; a device's slots from itself and from the devices just before and after it are all filled. list_slot[b, o] is -1 where box b has no translation o, else an import slot of b's device whose export entry is not -1. `patch_points`: a patch of device d's patches has distinct points within 8 consecutive boxes that begin no more than 2 boxes before d's first box and end no more than 2 boxes after its last.
All inputs are finite; a program needn't handle non-finite values.
Results may differ from the reference program's by a relative error of at most 0.0045.
Values may be sent and summed in bfloat16 or wider, within the bound.
No kernel may reach another device: no remote copies, remote signals or barrier semaphores. Data moves between devices by JAX's collectives and lax.ppermute only.
A program may use at most 128 MiB of HBM per device.

```python
import jax
import jax.numpy as jnp
from jax import lax

POINTS = 456
COLS = 16
OPS = 64
PATCH_PTS = 1024
BOX_DEV = 128
CAPACITY = 4
PATCH_DEV = 8
RIM = 2
SPAN = 8
BOXES = 1024
SOURCES = 8
PATCHES = 64


def shared_counts(key):
    count_key = jax.random.fold_in(key, 11)
    counts = jax.random.randint(count_key, (SOURCES, SOURCES), 0, CAPACITY + 1)
    target = jnp.arange(SOURCES)[:, None]
    anchor = jnp.arange(SOURCES)[None, :]
    nearby = jnp.abs(target - anchor) <= 1
    return jnp.where(nearby, CAPACITY, counts).astype(jnp.int32)


def draw_export_ids(key, part):
    counts = shared_counts(key)
    pick_key = jax.random.fold_in(key, 12)
    sub_keys = jax.random.split(pick_key, SOURCES * SOURCES)
    chosen = jax.vmap(lambda sub_key: jax.random.permutation(sub_key, BOX_DEV)[:CAPACITY])(sub_keys)
    chosen = chosen.reshape(SOURCES, SOURCES, CAPACITY)
    filled = jnp.arange(CAPACITY)[None, None, :] < counts.T[:, :, None]
    return jnp.where(filled, chosen, -1).astype(jnp.int32)


def draw_list_slot(key, part):
    counts = shared_counts(key)
    level_key = jax.random.fold_in(key, 13)
    present_key = jax.random.fold_in(key, 14)
    choose_key = jax.random.fold_in(key, 15)
    device = jnp.arange(BOXES) // BOX_DEV
    level = jax.random.randint(level_key, (SOURCES,), 0, 4)
    present = jax.random.randint(present_key, (BOXES, OPS), 0, 4) <= level[device][:, None]
    inclusive = jnp.cumsum(counts, axis=1)
    box_inclusive = inclusive[device]
    totals = box_inclusive[:, -1]
    drawn = jax.random.randint(choose_key, (BOXES, OPS), 0, totals[:, None])
    source = jnp.sum((box_inclusive[:, None, :] <= drawn[:, :, None]).astype(jnp.int32), axis=2)
    exclusive = box_inclusive - counts[device]
    base_slot = jnp.take_along_axis(exclusive, source, axis=1)
    slot_index = source * CAPACITY + (drawn - base_slot)
    return jnp.where(present, slot_index, -1).astype(jnp.int32)


def draw_patch_points(key, part):
    start_key = jax.random.fold_in(key, 21)
    point_key = jax.random.fold_in(key, 22)
    device = jnp.arange(PATCHES) // PATCH_DEV
    within = jnp.arange(PATCHES) % PATCH_DEV
    lowest = jnp.where(device == 0, 0, -RIM)
    highest = jnp.where(device == SOURCES - 1, BOX_DEV - SPAN, BOX_DEV + RIM - SPAN)
    random_start = jax.random.randint(start_key, (PATCHES,), lowest, highest + 1)
    start_box = jnp.where(within == 0, lowest, jnp.where(within == 1, highest, random_start))
    sub_keys = jax.random.split(point_key, PATCHES)
    offsets = jax.vmap(lambda sub_key: jax.random.permutation(sub_key, SPAN * POINTS)[:PATCH_PTS])(sub_keys)
    first_point = (device * BOX_DEV + start_box) * POINTS
    return (first_point[:, None] + offsets).astype(jnp.int32)


def steps_of(own_key, shape, cuts, smallest, largest):
    def one(axis_at, shards_of):
        heights = jax.random.uniform(jax.random.fold_in(jax.random.fold_in(own_key, 6), axis_at), (shards_of,), jnp.float32, smallest / len(cuts), largest / len(cuts))
        return jnp.repeat(jnp.exp(heights), shape[axis_at] // shards_of).reshape((-1,) + (1,) * (len(shape) - axis_at - 1))

    loudness = one(*cuts[0])
    for cut in cuts[1:]:
        loudness = loudness * one(*cut)
    return loudness


def scatter_about(key, dims, width, most, cuts=(), kind=jnp.bfloat16):
    level = steps_of(key, dims, cuts, -0.22, 0.18) if cuts else 1.0
    entries = jax.random.normal(key, dims, jnp.float32) * width * level
    return jnp.minimum(jnp.maximum(entries, -most), most).astype(kind)


def setup_inputs(seed: int = 0) -> dict:
    key_of = jax.random.split(jax.random.key(seed), 7)
    return {
        "density": scatter_about(key_of[0], (BOXES, COLS, POINTS), 1.0, 6.0, ((0, 8),)),
        "export_ids": draw_export_ids(jax.random.fold_in(key_of[6], 71), 0),
        "list_slot": draw_list_slot(jax.random.fold_in(key_of[6], 71), 0),
        "translations": scatter_about(key_of[3], (OPS, POINTS, POINTS), (POINTS * OPS // 2) ** -0.5, 0.046875, ((0, 4),)),
        "patch_points": draw_patch_points(jax.random.fold_in(key_of[6], 71), 0),
        "inverses": scatter_about(key_of[5], (PATCHES, PATCH_PTS, PATCH_PTS), PATCH_PTS ** -0.5, 0.1875, ((0, 8),)),
    }


def reference(density, export_ids, list_slot, translations, patch_points, inverses):
    device = (jnp.arange(BOXES) // BOX_DEV).astype(jnp.int32)
    live_slot = list_slot >= 0
    safe_slot = jnp.maximum(list_slot, 0)
    source = (safe_slot // CAPACITY).astype(jnp.int32)
    within = (safe_slot % CAPACITY).astype(jnp.int32)
    exported = export_ids[source, device[:, None], within]
    usable = live_slot & (exported >= 0)
    peer_box = jnp.where(usable, source * BOX_DEV + exported, 0).astype(jnp.int32)

    def add_operator(totals, pieces):
        peer_col, usable_col, operator = pieces
        gathered = jnp.take(density, peer_col, axis=0).astype(jnp.float32)
        gathered = jnp.where(usable_col[:, None, None], gathered, jnp.float32(0.0))
        term = jnp.dot(gathered.reshape(BOXES * COLS, POINTS), operator.astype(jnp.float32),
                       preferred_element_type=jnp.float32)
        return totals + term.reshape(BOXES, COLS, POINTS), None

    start_sum = jnp.zeros((BOXES, COLS, POINTS), jnp.float32)
    field_sum, _ = lax.scan(add_operator, start_sum, (peer_box.T, usable.T, translations))
    field = field_sum.astype(jnp.bfloat16)

    by_column = jnp.transpose(field, (1, 0, 2)).reshape(COLS, BOXES * POINTS)
    values = jnp.take(by_column, patch_points, axis=1)
    values = jnp.transpose(values, (1, 0, 2))

    def one_patch(pieces):
        patch_values, patch_inverse = pieces
        return jnp.dot(patch_values.astype(jnp.float32), patch_inverse.astype(jnp.float32),
                       preferred_element_type=jnp.float32)

    products = lax.map(one_patch, (values, inverses)).astype(jnp.bfloat16)
    flat_products = jnp.transpose(products, (1, 0, 2)).reshape(COLS, PATCHES * PATCH_PTS)
    correction = jnp.zeros((COLS, BOXES * POINTS), jnp.float32)
    correction = correction.at[:, patch_points.reshape(-1)].add(flat_products.astype(jnp.float32))
    correction = jnp.transpose(correction.reshape(COLS, BOXES, POINTS), (1, 0, 2))
    corrected = (field.astype(jnp.float32) + correction).astype(jnp.bfloat16)
    return (field, corrected)
```

```python
import functools

import jax
import jax.numpy as jnp
from jax import lax
from jax.experimental import pallas as pl
from jax.experimental.pallas import tpu as pltpu
from jax.sharding import PartitionSpec as P

RIM = 2
SPAN = 8
LANES = 128
NT = (((1,), (1,)), ((), ()))
ANY = pl.BlockSpec(memory_space=pl.ANY)
VMEM = pl.BlockSpec(memory_space=pltpu.VMEM)
SMEM = pl.BlockSpec(memory_space=pltpu.SMEM)


def round_up(n, m):
    return -(-n // m) * m


def params(limit):
    return pltpu.CompilerParams(vmem_limit_bytes=limit << 20)


def iota(shape, dim):
    return lax.broadcasted_iota(jnp.int32, shape, dim)


def div(x, n):
    if n & (n - 1) == 0:
        return x >> (n.bit_length() - 1)
    return lax.div(x, jnp.int32(n))


def mod(x, n):
    if n & (n - 1) == 0:
        return x & (n - 1)
    return lax.rem(x, jnp.int32(n))


def pick_kernel(share, groups_ref, ids_ref, density_ref, out_ref, block, sems):
    capacity, dests = ids_ref.shape
    cols, width, boxes = block.shape
    copies = []
    for j in range(cols // share):
        copy = pltpu.make_async_copy(
            density_ref.at[pl.ds(groups_ref[j] * share, share)],
            block.at[pl.ds(j * share, share)],
            sems.at[j],
        )
        copy.start()
        copies.append(copy)
    rows = dests * cols * capacity
    row = iota((rows, boxes), 0)
    pair = div(row, cols * capacity) * capacity + mod(row, capacity)
    column = mod(div(row, capacity), cols)

    def place(k, wanted):
        return jnp.where(pair == k, ids_ref[mod(k, capacity), div(k, capacity)], wanted)

    wanted = jnp.full((rows, boxes), -1, jnp.int32)
    if dests * capacity <= 64:
        for k in range(dests * capacity):
            wanted = place(jnp.int32(k), wanted)
    else:
        wanted = lax.fori_loop(0, dests * capacity, place, wanted)
    hit = wanted == iota((rows, boxes), 1)
    for copy in copies:
        copy.wait()
    total = jnp.zeros((rows, width), jnp.float32)
    for c in range(cols):
        chosen = jnp.where(hit & (column == c), 1.0, 0.0).astype(jnp.bfloat16)
        total = total + lax.dot_general(
            chosen, block[c], NT, preferred_element_type=jnp.float32
        )
    out_ref[...] = total.astype(out_ref.dtype).reshape(out_ref.shape)


def field_kernel(
    share, capacity, group, ops_at_ref, imported_ref, slots_ref, *rest
):
    operator_refs, (out_ref, edge_ref, weights, terms, hot, sems) = rest[:-6], rest[-6:]
    sources, per_source, width = imported_ref.shape
    local_ops = operator_refs[0].shape[0]
    boxes = slots_ref.shape[1]
    slots = sources * capacity
    stride = terms.shape[1] // share
    chunk = local_ops
    for size in (4, 2, 1):
        if local_ops % size == 0:
            chunk = size
            break
    copies = []
    for half, ref in enumerate(operator_refs):
        for at in range(0, local_ops, chunk):
            copy = pltpu.make_async_copy(
                ref.at[pl.ds(at, chunk)],
                weights.at[pl.ds(half * local_ops + at, chunk)],
                sems.at[len(copies)],
            )
            copy.start()
            copies.append(copy)
    arrived = sources * per_source
    shape = (share * slots, arrived)
    row = iota(shape, 0)
    slot = mod(row, slots)
    origin = (
        div(slot, capacity) * per_source
        + (group * share + div(row, slots)) * capacity
        + mod(slot, capacity)
    )
    order = jnp.where(origin == iota(shape, 1), 1.0, 0.0).astype(jnp.bfloat16)
    flat = imported_ref[...].reshape(arrived, width)
    ordered = jnp.dot(order, flat, preferred_element_type=jnp.float32).astype(jnp.bfloat16)
    for half in range(len(operator_refs)):
        wanted = slots_ref[pl.ds(ops_at_ref[half], local_ops), :]
        for o in range(local_ops):
            picked = iota((slots, boxes), 0) == wanted[o : o + 1, :]
            at = (half * local_ops + o) * slots
            hot[at : at + slots, :] = jnp.where(picked, 1.0, 0.0).astype(jnp.bfloat16)
    picks = hot[...].T
    for i, copy in enumerate(copies):
        copy.wait()
        for o in range(i * chunk, (i + 1) * chunk):
            term = jnp.dot(ordered, weights[o], preferred_element_type=jnp.float32)
            term = term.astype(jnp.bfloat16)
            for c in range(share):
                terms[o * slots : (o + 1) * slots, c * stride : c * stride + width] = term[
                    c * slots : (c + 1) * slots
                ]
    total = jnp.dot(picks, terms[...], preferred_element_type=jnp.float32)
    tiles = stride // LANES
    for c in range(share):
        out_ref[c] = total[:, c * stride : (c + 1) * stride].astype(out_ref.dtype)
    for c in range(share):
        for t in range(tiles):
            part = total[:, (c * tiles + t) * LANES : (c * tiles + t + 1) * LANES]
            for b in range(RIM):
                at = (b * share + c) * tiles + t
                edge_ref[0, at : at + 1, :] = part[b : b + 1]
                edge_ref[1, at : at + 1, :] = part[boxes - RIM + b : boxes - RIM + b + 1]


def field_call(imported, slots_t, operators, ops_at, share, capacity, group, dtype):
    sources = imported.shape[0]
    width = imported.shape[2]
    boxes = slots_t.shape[1]
    slots = sources * capacity
    all_ops = sum(o.shape[0] for o in operators)
    stride = round_up(width, LANES)
    return pl.pallas_call(
        functools.partial(field_kernel, share, capacity, group),
        out_shape=[
            jax.ShapeDtypeStruct((share, boxes, stride), dtype),
            jax.ShapeDtypeStruct((2, RIM * share * (stride // LANES), LANES), jnp.float32),
        ],
        in_specs=[SMEM, VMEM, VMEM] + [ANY] * len(operators),
        out_specs=[VMEM, VMEM],
        scratch_shapes=[
            pltpu.VMEM((all_ops, width, width), jnp.bfloat16),
            pltpu.VMEM((all_ops * slots, share * stride), jnp.bfloat16),
            pltpu.VMEM((all_ops * slots, boxes), jnp.bfloat16),
            pltpu.SemaphoreType.DMA((all_ops,)),
        ],
        compiler_params=params(56),
        cost_estimate=pl.CostEstimate(
            flops=2 * all_ops * share * slots * width * (width + boxes),
            bytes_accessed=all_ops * width * stride * 2,
            transcendentals=0,
        ),
    )(ops_at, imported, slots_t, *operators)


def patch_kernel(
    info_ref, starts_ref, code_ref, lane_ref, own_ref, received_ref, low_ref, high_ref,
    inverses_ref, field_ref, corrected_ref, side_ref, rows_ref, ext, spread, values, blocks, sems,
):
    share, boxes, stride = own_ref.shape
    width = field_ref.shape[1]
    patches, points = code_ref.shape
    tiles = stride // LANES
    per_box = share * tiles
    window = SPAN * per_box
    rim = RIM * per_box
    copies = []
    for p in range(patches):
        copy = pltpu.make_async_copy(inverses_ref.at[p], blocks.at[p], sems.at[p])
        copy.start()
        copies.append(copy)
    spread[...] = jnp.zeros_like(spread)
    ext[:rim, :] = low_ref[...]
    ext[rim + boxes * per_box :, :] = high_ref[...]
    for c in range(share):
        for t in range(tiles):
            part = own_ref[c, :, t * LANES : (t + 1) * LANES]
            for r in range(received_ref.shape[0]):
                part = part + received_ref[r, c, :, t * LANES : (t + 1) * LANES].astype(jnp.float32)
            part = part.astype(jnp.bfloat16).astype(jnp.float32)
            ext[pl.ds(rim + c * tiles + t, boxes, stride=per_box), :] = part
            last = min(width - t * LANES, LANES)
            field_ref[c, t * LANES : t * LANES + last, :] = part.T[:last].astype(field_ref.dtype)
    row = iota((window, LANES), 0)
    row_code = div(row, per_box) * tiles + mod(row, tiles)
    for p in range(patches):
        held = ext[pl.ds(pl.multiple_of(starts_ref[p] * per_box, 8), window), :]
        for at in range(0, points, LANES):
            code = code_ref[p : p + 1, at : at + LANES]
            lane = jnp.broadcast_to(lane_ref[p : p + 1, at : at + LANES], (window, LANES))
            found = jnp.take_along_axis(held, lane, axis=1)
            found = jnp.where(row_code == code, found, 0.0)
            found = jnp.sum(found.reshape(SPAN, per_box, LANES), axis=0)
            values[p, :, at : at + LANES] = jnp.sum(found.reshape(share, tiles, LANES), axis=1)
    row = iota((window, points), 0)
    row_code = div(row, per_box) * tiles + mod(row, tiles)
    for p in range(patches):
        copies[p].wait()
        product = jnp.dot(
            values[p].astype(jnp.bfloat16), blocks[p], preferred_element_type=jnp.float32
        )
        product = product.astype(jnp.bfloat16).astype(jnp.float32)
        product = jnp.concatenate(
            [jnp.broadcast_to(product[c : c + 1], (tiles, points)) for c in range(share)], axis=0
        )
        product = jnp.concatenate([product] * SPAN, axis=0)
        left = jnp.where(row_code == code_ref[p : p + 1, :], product, 0.0).astype(jnp.bfloat16)
        right = jnp.where(iota((LANES, points), 0) == lane_ref[p : p + 1, :], 1.0, 0.0)
        placed = lax.dot_general(
            left, right.astype(jnp.bfloat16), NT, preferred_element_type=jnp.float32
        )
        at = pl.ds(pl.multiple_of(starts_ref[p] * per_box, 8), window)
        spread[at, :] = spread[at, :] + placed
    for c in range(share):
        for t in range(tiles):
            at = pl.ds(rim + c * tiles + t, boxes, stride=per_box)
            total = ext[at, :] + spread[at, :]
            last = min(width - t * LANES, LANES)
            corrected_ref[c, t * LANES : t * LANES + last, :] = total.T[:last].astype(
                corrected_ref.dtype
            )
    end = rim + boxes * per_box
    rows_ref[0] = ext[rim : 2 * rim, :] + spread[rim : 2 * rim, :]
    rows_ref[1] = ext[end - rim : end, :] + spread[end - rim : end, :]
    even = info_ref[0] == 0
    low = spread[:rim, :]
    high = spread[end:, :]
    side_ref[0] = jnp.where(even, high, low)
    side_ref[1] = jnp.where(even, low, high)


def finish_kernel(info_ref, first_ref, second_ref, rows_ref, corrected_ref, out_ref, tall):
    share, width, boxes = corrected_ref.shape
    per_box = rows_ref.shape[1] // RIM
    tiles = per_box // share
    even = info_ref[0] == 0
    first = first_ref[...]
    second = second_ref[...]
    low = rows_ref[0] + jnp.where(even, second, first)
    high = rows_ref[1] + jnp.where(even, first, second)
    tall[...] = jnp.zeros_like(tall)
    for c in range(share):
        for t in range(tiles):
            for b in range(RIM):
                at = b * per_box + c * tiles + t
                tall[b : b + 1, :] = low[at : at + 1]
                tall[boxes - RIM + b : boxes - RIM + b + 1, :] = high[at : at + 1]
            turned = tall[...].T
            last = min(width - t * LANES, LANES)
            box = iota((last, boxes), 1)
            edge = (box < RIM) | (box >= boxes - RIM)
            kept = corrected_ref[c, t * LANES : t * LANES + last, :].astype(jnp.float32)
            out_ref[c, t * LANES : t * LANES + last, :] = jnp.where(
                edge, turned[:last], kept
            ).astype(out_ref.dtype)


def swap_sides(first, second, axis):
    count = lax.axis_size(axis)
    evens = [(i, i + 1) for i in range(0, count - 1, 2)]
    odds = [(i, i + 1) for i in range(1, count - 1, 2)]
    evens += [(b, a) for a, b in evens]
    odds += [(b, a) for a, b in odds]
    return lax.ppermute(first, axis, evens), lax.ppermute(second, axis, odds)


def body(density, export_ids, list_slot, translations, patch_points, inverses):
    boxes, total_cols, width = density.shape
    groups = lax.axis_size("col")
    share = total_cols // groups
    capacity = export_ids.shape[2]
    sources = export_ids.shape[1]
    local_ops = translations.shape[0]
    patches, points = patch_points.shape
    stride = round_up(width, LANES)
    tiles = stride // LANES
    inner = 2 if groups % 2 == 0 else 1
    outer = groups // inner
    col = lax.axis_index("col").astype(jnp.int32)
    box = lax.axis_index("box").astype(jnp.int32)
    core, half = col % inner, col // inner
    handled = jnp.stack([((half + j) % outer) * inner + core for j in range(outer)])
    ops_at = jnp.stack([(half * inner + (core + i) % inner) * local_ops for i in range(inner)])
    info = jnp.stack([box % 2])

    operators = [translations]
    for i in range(1, inner):
        moves = [(h * inner + (k + i) % inner, h * inner + k) for h in range(outer) for k in range(inner)]
        operators.append(lax.ppermute(translations, "col", moves))

    cols = outer * share
    outgoing = pl.pallas_call(
        functools.partial(pick_kernel, share),
        out_shape=jax.ShapeDtypeStruct((sources, cols * capacity, width), jnp.bfloat16),
        in_specs=[SMEM, SMEM, ANY],
        out_specs=VMEM,
        scratch_shapes=[
            pltpu.VMEM((cols, width, boxes), jnp.bfloat16),
            pltpu.SemaphoreType.DMA((outer,)),
        ],
        compiler_params=params(32),
    )(handled, export_ids[0].T, jnp.transpose(density, (1, 2, 0)))
    imported = lax.all_to_all(outgoing, "box", split_axis=0, concat_axis=0, tiled=True)

    slots_t = list_slot.T
    parts = []
    edge_parts = []
    for j in range(1, outer):
        part, edge = field_call(imported, slots_t, operators, ops_at, share, capacity, j, jnp.bfloat16)
        moves = [
            (h * inner + k, ((h + j) % outer) * inner + k) for h in range(outer) for k in range(inner)
        ]
        edge_parts.append(lax.ppermute(edge, "col", moves))
        parts.append(lax.ppermute(part, "col", moves))
    own, edges = field_call(imported, slots_t, operators, ops_at, share, capacity, 0, jnp.float32)
    received = jnp.stack(parts)
    for edge in edge_parts:
        edges = edges + edge
    edges = edges.astype(jnp.bfloat16).astype(jnp.float32)
    low, high = edges[0], edges[1]
    even = box % 2 == 0
    first, second = swap_sides(jnp.where(even, high, low), jnp.where(even, low, high), "box")
    low_in = jnp.where(even, second, first)
    high_in = jnp.where(even, first, second)

    local = patch_points - (box * boxes - RIM) * width
    at_box = local // width
    at_point = local - at_box * width
    start = jnp.minimum(jnp.min(at_box, axis=1), boxes + 2 * RIM - SPAN)
    code = (at_box - start[:, None]) * tiles + at_point // LANES
    lane = at_point % LANES

    per_box = share * tiles
    ext_rows = (boxes + 2 * RIM) * per_box
    field_t, corrected_t, sides, rows = pl.pallas_call(
        patch_kernel,
        out_shape=[
            jax.ShapeDtypeStruct((share, width, boxes), jnp.bfloat16),
            jax.ShapeDtypeStruct((share, width, boxes), jnp.bfloat16),
            jax.ShapeDtypeStruct((2, RIM * per_box, LANES), jnp.float32),
            jax.ShapeDtypeStruct((2, RIM * per_box, LANES), jnp.float32),
        ],
        in_specs=[SMEM, SMEM] + [VMEM] * 6 + [ANY],
        out_specs=[VMEM] * 4,
        scratch_shapes=[
            pltpu.VMEM((ext_rows, LANES), jnp.float32),
            pltpu.VMEM((ext_rows, LANES), jnp.float32),
            pltpu.VMEM((patches, share, points), jnp.float32),
            pltpu.VMEM((patches, points, points), jnp.bfloat16),
            pltpu.SemaphoreType.DMA((patches,)),
        ],
        compiler_params=params(48),
    )(info, start, code, lane, own, received, low_in, high_in, inverses)

    back_first, back_second = swap_sides(sides[0], sides[1], "box")
    corrected_t = pl.pallas_call(
        finish_kernel,
        out_shape=jax.ShapeDtypeStruct(corrected_t.shape, corrected_t.dtype),
        in_specs=[SMEM] + [VMEM] * 4,
        out_specs=VMEM,
        scratch_shapes=[pltpu.VMEM((boxes, LANES), jnp.float32)],
        input_output_aliases={4: 0},
        compiler_params=params(32),
    )(info, back_first, back_second, rows, corrected_t)
    return jnp.transpose(field_t, (2, 0, 1)), jnp.transpose(corrected_t, (2, 0, 1))


def solution(mesh):
    return jax.shard_map(
        body,
        mesh=mesh,
        in_specs=(
            P("box", None, None),
            P("box", None, None),
            P("box", None),
            P("col", None, None),
            P("box", None),
            P("box", None, None),
        ),
        out_specs=(P("box", "col", None), P("box", "col", None)),
        check_vma=False,
    )
```

```python
import functools

import jax
import jax.numpy as jnp
from jax import lax
from jax.experimental import pallas as pl
from jax.experimental.pallas import tpu as pltpu
from jax.sharding import PartitionSpec as P

RIM = 2
SPAN = 8
LANES = 128
NT = (((1,), (1,)), ((), ()))
ANY = pl.BlockSpec(memory_space=pl.ANY)
VMEM = pl.BlockSpec(memory_space=pltpu.VMEM)
SMEM = pl.BlockSpec(memory_space=pltpu.SMEM)


def round_up(n, m):
    return -(-n // m) * m


def params(limit):
    return pltpu.CompilerParams(vmem_limit_bytes=limit << 20)


def iota(shape, dim):
    return lax.broadcasted_iota(jnp.int32, shape, dim)


def div(x, n):
    if n & (n - 1) == 0:
        return x >> (n.bit_length() - 1)
    return lax.div(x, jnp.int32(n))


def mod(x, n):
    if n & (n - 1) == 0:
        return x & (n - 1)
    return lax.rem(x, jnp.int32(n))


def handled_groups():
    groups = lax.axis_size("col")
    inner = 2 if groups % 2 == 0 else 1
    return inner, groups // inner


def pick_kernel(share, ids_hbm, density_ref, out_ref, ids_ref, block, sems):
    capacity, dests = ids_ref.shape
    cols, width, boxes = block.shape
    inner, outer = handled_groups()
    col = lax.axis_index("col")
    ids_copy = pltpu.make_async_copy(ids_hbm, ids_ref, sems.at[outer])
    ids_copy.start()
    copies = []
    for j in range(outer):
        group = mod(div(col, inner) + j, outer) * inner + mod(col, inner)
        copy = pltpu.make_async_copy(
            density_ref.at[pl.ds(group * share, share)],
            block.at[pl.ds(j * share, share)],
            sems.at[j],
        )
        copy.start()
        copies.append(copy)
    ids_copy.wait()
    rows = dests * cols * capacity
    row = iota((rows, boxes), 0)
    pair = div(row, cols * capacity) * capacity + mod(row, capacity)
    column = mod(div(row, capacity), cols)

    def place(k, wanted):
        return jnp.where(pair == k, ids_ref[mod(k, capacity), div(k, capacity)], wanted)

    wanted = jnp.full((rows, boxes), -1, jnp.int32)
    if dests * capacity <= 64:
        for k in range(dests * capacity):
            wanted = place(jnp.int32(k), wanted)
    else:
        wanted = lax.fori_loop(0, dests * capacity, place, wanted)
    hit = wanted == iota((rows, boxes), 1)
    for copy in copies:
        copy.wait()
    total = jnp.zeros((rows, width), jnp.float32)
    for c in range(cols):
        chosen = jnp.where(hit & (column == c), 1.0, 0.0).astype(jnp.bfloat16)
        total = total + lax.dot_general(
            chosen, block[c], NT, preferred_element_type=jnp.float32
        )
    out_ref[...] = total.astype(out_ref.dtype).reshape(out_ref.shape)


def prepare_kernel(
    slots, tiles, width, local_ops, slots_ref, points_ref, picks_ref, code_ref, lane_ref, spans_ref, hot
):
    boxes = slots_ref.shape[1]
    patches = code_ref.shape[0]
    inner, outer = handled_groups()
    col = lax.axis_index("col")
    for half in range(inner):
        first = (div(col, inner) * inner + mod(col + half, inner)) * local_ops
        wanted = slots_ref[pl.ds(first, local_ops), :]
        for o in range(local_ops):
            picked = iota((slots, boxes), 0) == wanted[o : o + 1, :]
            at = (half * local_ops + o) * slots
            hot[at : at + slots, :] = jnp.where(picked, 1.0, 0.0).astype(jnp.bfloat16)
    picks_ref[...] = hot[...].T
    local = points_ref[...] - (lax.axis_index("box") * boxes - RIM) * width
    at_box = ((local.astype(jnp.float32) + 0.5) * (1.0 / width)).astype(jnp.int32)
    at_point = local - at_box * width
    lowest = jnp.min(at_box, axis=1, keepdims=True)
    highest = jnp.max(at_box, axis=1, keepdims=True)
    start = jnp.minimum(lowest, boxes + 2 * RIM - SPAN)
    code = (at_box - start) * tiles + div(at_point, LANES)
    lane = mod(at_point, LANES)
    for p in range(patches):
        code_ref[p] = code[p : p + 1]
        lane_ref[p] = lane[p : p + 1]
        spans_ref[p] = jnp.min(lowest[p : p + 1])
        spans_ref[patches + p] = jnp.min(highest[p : p + 1])


def prepare_call(slots_t, patch_points, slots, tiles, width, local_ops):
    inner, _ = handled_groups()
    boxes = slots_t.shape[1]
    patches, points = patch_points.shape
    all_slots = inner * local_ops * slots
    return pl.pallas_call(
        functools.partial(prepare_kernel, slots, tiles, width, local_ops),
        out_shape=[
            jax.ShapeDtypeStruct((boxes, all_slots), jnp.bfloat16),
            jax.ShapeDtypeStruct((patches, 1, points), jnp.int32),
            jax.ShapeDtypeStruct((patches, 1, points), jnp.int32),
            jax.ShapeDtypeStruct((2 * patches,), jnp.int32),
        ],
        in_specs=[VMEM] * 2,
        out_specs=[VMEM] * 3 + [SMEM],
        scratch_shapes=[pltpu.VMEM((all_slots, boxes), jnp.bfloat16)],
        compiler_params=params(8),
    )(
        pltpu.with_memory_space_constraint(slots_t, pltpu.HBM),
        pltpu.with_memory_space_constraint(patch_points, pltpu.HBM),
    )


def field_kernel(share, capacity, group, fetch, imported_ref, picks_ref, *rest):
    if fetch:
        sources_refs, (out_ref, edge_ref, operators_ref, terms, sems) = rest[:-5], rest[-5:]
    else:
        sources_refs, (operators_ref, out_ref, edge_ref, terms) = (), rest
    sources, per_source, width = imported_ref.shape
    all_ops = operators_ref.shape[0]
    boxes = picks_ref.shape[0]
    slots = sources * capacity
    stride = terms.shape[1] // share
    tiles = stride // LANES
    copies, chunk = {}, 1
    for ref in sources_refs:
        local_ops = ref.shape[0]
        chunk = 4 if local_ops % 4 == 0 else 1
        for at in range(0, local_ops, chunk):
            to = len(copies) * chunk
            copy = pltpu.make_async_copy(
                ref.at[pl.ds(at, chunk)], operators_ref.at[pl.ds(to, chunk)], sems.at[len(copies)]
            )
            copy.start()
            copies[to] = copy
    arrived = sources * per_source
    shape = (share * slots, arrived)
    row = iota(shape, 0)
    slot = mod(row, slots)
    origin = (
        div(slot, capacity) * per_source
        + (group * share + div(row, slots)) * capacity
        + mod(slot, capacity)
    )
    order = jnp.where(origin == iota(shape, 1), 1.0, 0.0).astype(jnp.bfloat16)
    flat = imported_ref[...].reshape(arrived, width)
    ordered = jnp.dot(order, flat, preferred_element_type=jnp.float32).astype(jnp.bfloat16)
    for o in range(all_ops):
        if o in copies:
            copies[o].wait()
        term = jnp.dot(ordered, operators_ref[o], preferred_element_type=jnp.float32)
        term = term.astype(jnp.bfloat16)
        for c in range(share):
            terms[o * slots : (o + 1) * slots, c * stride : c * stride + width] = term[
                c * slots : (c + 1) * slots
            ]
    total = jnp.dot(picks_ref[...], terms[...], preferred_element_type=jnp.float32)
    total = total.astype(out_ref.dtype)
    for c in range(share):
        out_ref[c] = total[:, c * stride : (c + 1) * stride]
        for t in range(tiles):
            at = (c * tiles + t) * LANES
            to = pl.ds(c * tiles + t, RIM, stride=share * tiles)
            edge_ref[0, to, :] = total[:RIM, at : at + LANES].astype(jnp.float32)
            edge_ref[1, to, :] = total[boxes - RIM :, at : at + LANES].astype(jnp.float32)


def field_call(imported, picks, operators, share, capacity, group, dtype):
    sources, _, width = imported.shape
    boxes, all_slots = picks.shape
    all_ops = all_slots // (sources * capacity)
    stride = round_up(width, LANES)
    fetch = isinstance(operators, tuple)
    out_shape = [
        jax.ShapeDtypeStruct((share, boxes, stride), dtype),
        jax.ShapeDtypeStruct((2, RIM * share * (stride // LANES), LANES), jnp.float32),
    ]
    scratch = [pltpu.VMEM((all_slots, share * stride), jnp.bfloat16)]
    if fetch:
        out_shape.append(pltpu.VMEM((all_ops, width, width), operators[0].dtype))
        scratch.append(pltpu.SemaphoreType.DMA((all_ops,)))
        operators = [pltpu.with_memory_space_constraint(o, pltpu.HBM) for o in operators]
    else:
        operators = [pltpu.with_memory_space_constraint(operators, pltpu.VMEM)]
    return pl.pallas_call(
        functools.partial(field_kernel, share, capacity, group, fetch),
        out_shape=out_shape,
        in_specs=[VMEM] * 2 + [ANY if fetch else VMEM] * len(operators),
        out_specs=[VMEM] * len(out_shape),
        scratch_shapes=scratch,
        compiler_params=params(8 + all_slots * share * stride * 2 // (1 << 20)),
        cost_estimate=pl.CostEstimate(
            flops=2 * all_slots * share * width * (width + boxes),
            bytes_accessed=2 * all_ops * width * width,
            transcendentals=0,
        ),
    )(imported, picks, *operators)


def edge_kernel(*refs):
    edge_refs, (first_ref, second_ref) = refs[:-2], refs[-2:]
    total = edge_refs[0][...]
    for ref in edge_refs[1:]:
        total = total + ref[...]
    total = total.astype(jnp.bfloat16).astype(jnp.float32)
    even = mod(lax.axis_index("box"), 2) == 0
    first_ref[...] = jnp.where(even, total[1], total[0])
    second_ref[...] = jnp.where(even, total[0], total[1])


def edge_call(*edges):
    side = jax.ShapeDtypeStruct(edges[0].shape[1:], jnp.float32)
    return pl.pallas_call(
        edge_kernel,
        out_shape=[side, side],
        in_specs=[VMEM] * len(edges),
        out_specs=[VMEM, VMEM],
        compiler_params=params(2),
        cost_estimate=pl.CostEstimate(flops=10**10, bytes_accessed=0, transcendentals=0),
    )(*edges)


def order_patches(spans_ref, order_ref, boxes):
    patches = spans_ref.shape[0] // 2
    count = jnp.int32(0)
    for wanted in (True, False):
        for p in range(patches):
            reaches = (spans_ref[p] < RIM) | (spans_ref[patches + p] >= boxes + RIM)
            order_ref[count] = p
            count = count + jnp.where(reaches == wanted, 1, 0)
        if wanted:
            first = count
    return first


def patch_batch(chosen, spans_ref, code_ref, lane_ref, ext, inverses_ref, spread, share, boxes):
    points = code_ref.shape[2]
    per_box = ext.shape[0] // (boxes + 2 * RIM)
    tiles = per_box // share
    window = SPAN * per_box
    places, products = [], []
    row = iota((window, LANES), 0)
    row_code = div(row, per_box) * tiles + mod(row, tiles)
    for p in chosen:
        start = jnp.minimum(spans_ref[p], boxes + 2 * RIM - SPAN) * per_box
        places.append(pl.ds(pl.multiple_of(start, 8), window))
        held = ext[places[-1], :]
        values = []
        for at in range(0, points, LANES):
            code = code_ref[p, :, at : at + LANES]
            lane = jnp.broadcast_to(lane_ref[p, :, at : at + LANES], (window, LANES))
            found = jnp.take_along_axis(held, lane, axis=1)
            found = jnp.where(row_code == code, found, 0.0)
            found = jnp.sum(found.reshape(SPAN, per_box, LANES), axis=0)
            values.append(jnp.sum(found.reshape(share, tiles, LANES), axis=1))
        values = jnp.concatenate(values, axis=1).astype(jnp.bfloat16)
        product = jnp.dot(values, inverses_ref[p], preferred_element_type=jnp.float32)
        products.append(product.astype(jnp.bfloat16).astype(jnp.float32))
    row = iota((window, points), 0)
    row_code = div(row, per_box) * tiles + mod(row, tiles)
    for p, place, product in zip(chosen, places, products):
        product = jnp.concatenate(
            [jnp.broadcast_to(product[c : c + 1], (tiles, points)) for c in range(share)], axis=0
        )
        product = jnp.concatenate([product] * SPAN, axis=0)
        left = jnp.where(row_code == code_ref[p], product, 0.0).astype(jnp.bfloat16)
        right = jnp.where(iota((LANES, points), 0) == lane_ref[p], 1.0, 0.0)
        placed = lax.dot_general(
            left, right.astype(jnp.bfloat16), NT, preferred_element_type=jnp.float32
        )
        spread[place, :] = spread[place, :] + placed


def batch_size(patches):
    return 2 if patches % 2 == 0 else 1


def early_kernel(
    spans_ref, code_ref, lane_ref, own_ref, received_ref, inverses_ref, first_ref, second_ref,
    ext, spread, first_out, second_out, order_ref,
):
    share, boxes, stride = own_ref.shape
    tiles = stride // LANES
    per_box = share * tiles
    rim = RIM * per_box
    end = rim + boxes * per_box
    patches = code_ref.shape[0]
    even = mod(lax.axis_index("box"), 2) == 0
    first = first_ref[...]
    second = second_ref[...]
    spread[...] = jnp.zeros_like(spread)
    ext[:rim, :] = jnp.where(even, second, first)
    ext[end:, :] = jnp.where(even, first, second)
    for c in range(share):
        for t in range(tiles):
            part = own_ref[c, :, t * LANES : (t + 1) * LANES]
            for r in range(received_ref.shape[0]):
                part = part + received_ref[r, c, :, t * LANES : (t + 1) * LANES].astype(jnp.float32)
            part = part.astype(jnp.bfloat16).astype(jnp.float32)
            ext[pl.ds(rim + c * tiles + t, boxes, stride=per_box), :] = part
    batch = batch_size(patches)
    reaching = order_patches(spans_ref, order_ref, boxes)

    def step(i, carry):
        chosen = [order_ref[i * batch + k] for k in range(batch)]
        patch_batch(chosen, spans_ref, code_ref, lane_ref, ext, inverses_ref, spread, share, boxes)
        return carry

    lax.fori_loop(0, div(reaching + batch - 1, batch), step, 0)
    low = spread[:rim, :]
    high = spread[end:, :]
    first_out[...] = jnp.where(even, high, low)
    second_out[...] = jnp.where(even, low, high)


def late_kernel(
    spans_ref, code_ref, lane_ref, ext, early_ref, inverses_ref,
    field_ref, corrected_ref, rows_ref, spread, order_ref,
):
    share, width, boxes = field_ref.shape
    per_box = ext.shape[0] // (boxes + 2 * RIM)
    tiles = per_box // share
    rim = RIM * per_box
    end = rim + boxes * per_box
    patches = code_ref.shape[0]
    spread[...] = early_ref[...]
    batch = batch_size(patches)
    reaching = order_patches(spans_ref, order_ref, boxes)

    def step(i, carry):
        chosen = [order_ref[i * batch + k] for k in range(batch)]
        patch_batch(chosen, spans_ref, code_ref, lane_ref, ext, inverses_ref, spread, share, boxes)
        return carry

    lax.fori_loop(div(reaching + batch - 1, batch), patches // batch, step, 0)
    for c in range(share):
        for t in range(tiles):
            at = pl.ds(rim + c * tiles + t, boxes, stride=per_box)
            last = min(width - t * LANES, LANES)
            own = ext[at, :]
            total = own + spread[at, :]
            to = slice(t * LANES, t * LANES + last)
            field_ref[c, to, :] = own.T[:last].astype(field_ref.dtype)
            corrected_ref[c, to, :] = total.T[:last].astype(corrected_ref.dtype)
    rows_ref[:rim] = ext[rim : 2 * rim, :] + spread[rim : 2 * rim, :]
    rows_ref[rim:] = ext[end - rim : end, :] + spread[end - rim : end, :]


def finish_kernel(first_ref, second_ref, rows_ref, corrected_ref, out_ref):
    share, width, boxes = corrected_ref.shape
    rim = rows_ref.shape[0] // 2
    per_box = rim // RIM
    tiles = per_box // share
    even = mod(lax.axis_index("box"), 2) == 0
    first = first_ref[...]
    second = second_ref[...]
    low = rows_ref[:rim] + jnp.where(even, second, first)
    high = rows_ref[rim:] + jnp.where(even, first, second)
    rows = jnp.concatenate([low, high], axis=0)
    point = mod(iota(rows.shape, 0), tiles) * LANES + iota(rows.shape, 1)
    rows = jnp.where(point < width, rows, 0.0).T.astype(jnp.bfloat16)
    shape = (2 * rim, per_box * boxes)
    row = iota(shape, 0)
    box = div(mod(row, rim), per_box) + jnp.where(row < rim, 0, boxes - RIM)
    target = mod(row, per_box) * boxes + box
    place = jnp.where(target == iota(shape, 1), 1.0, 0.0).astype(jnp.bfloat16)
    placed = jnp.dot(rows, place, preferred_element_type=jnp.float32)
    box = iota((LANES, boxes), 1)
    edge = (box < RIM) | (box >= boxes - RIM)
    for c in range(share):
        for t in range(tiles):
            last = min(width - t * LANES, LANES)
            at = (c * tiles + t) * boxes
            to = slice(t * LANES, t * LANES + last)
            kept = corrected_ref[c, to, :].astype(jnp.float32)
            out_ref[c, to, :] = jnp.where(
                edge[:last], placed[:last, at : at + boxes], kept
            ).astype(out_ref.dtype)


def swap_sides(first, second):
    count = lax.axis_size("box")

    def moves(start):
        pairs = [(i, i + 1) for i in range(start, count - 1, 2)]
        return pairs + [(b, a) for a, b in pairs]

    return lax.ppermute(first, "box", moves(0)), lax.ppermute(second, "box", moves(1))


def body(density, export_ids, list_slot, translations, patch_points, inverses):
    boxes, total_cols, width = density.shape
    inner, outer = handled_groups()
    share = total_cols // (inner * outer)
    capacity = export_ids.shape[2]
    sources = export_ids.shape[1]
    patches, points = patch_points.shape
    stride = round_up(width, LANES)
    tiles = stride // LANES
    per_box = share * tiles
    places = [(h, k) for h in range(outer) for k in range(inner)]

    others = []
    for i in range(1, inner):
        moves = [(h * inner + (k + i) % inner, h * inner + k) for h, k in places]
        others.append(lax.ppermute(translations, "col", moves))

    cols = outer * share
    outgoing = pl.pallas_call(
        functools.partial(pick_kernel, share),
        out_shape=jax.ShapeDtypeStruct((sources, cols * capacity, width), jnp.bfloat16),
        in_specs=[ANY, ANY],
        out_specs=VMEM,
        scratch_shapes=[
            pltpu.SMEM((capacity, sources), jnp.int32),
            pltpu.VMEM((cols, width, boxes), jnp.bfloat16),
            pltpu.SemaphoreType.DMA((outer + 1,)),
        ],
        compiler_params=params(8),
    )(
        pltpu.with_memory_space_constraint(export_ids[0].T, pltpu.HBM),
        pltpu.with_memory_space_constraint(jnp.transpose(density, (1, 2, 0)), pltpu.HBM),
    )
    imported = lax.all_to_all(outgoing, "box", split_axis=0, concat_axis=0, tiled=True)

    _, *prepared = lax.optimization_barrier((outgoing, list_slot.T, patch_points))
    picks, code, lane, spans = prepare_call(
        *prepared, sources * capacity, tiles, width, translations.shape[0]
    )
    operators = (translations, *others)
    parts, edges = [], []
    for j in range(1, outer):
        part, edge, *loaded = field_call(
            imported, picks, operators, share, capacity, j, jnp.bfloat16
        )
        operators = loaded[0] if loaded else operators
        moves = [(h * inner + k, ((h + j) % outer) * inner + k) for h, k in places]
        edges.append(lax.ppermute(edge, "col", moves))
        parts.append(lax.ppermute(part, "col", moves))
    own, edge = field_call(imported, picks, operators, share, capacity, 0, jnp.float32)[:2]
    first, second = swap_sides(*edge_call(edge, *edges))
    received = jnp.stack(parts)

    ext_rows = (boxes + 2 * RIM) * per_box
    rim = RIM * per_box
    side = jax.ShapeDtypeStruct((rim, LANES), jnp.float32)
    ext, early, first, second = pl.pallas_call(
        early_kernel,
        out_shape=[
            pltpu.VMEM((ext_rows, LANES), jnp.float32),
            pltpu.VMEM((ext_rows, LANES), jnp.float32),
            side,
            side,
        ],
        in_specs=[SMEM] + [VMEM] * 7,
        out_specs=[VMEM] * 4,
        scratch_shapes=[pltpu.SMEM((patches + 1,), jnp.int32)],
        compiler_params=params(10),
    )(spans, code, lane, own, received, inverses, first, second)
    first, second = swap_sides(first, second)

    field_t, corrected_t, rows = pl.pallas_call(
        late_kernel,
        out_shape=[
            jax.ShapeDtypeStruct((share, width, boxes), jnp.bfloat16),
            pltpu.VMEM((share, width, boxes), jnp.bfloat16),
            pltpu.VMEM((2 * rim, LANES), jnp.float32),
        ],
        in_specs=[SMEM] + [VMEM] * 5,
        out_specs=[VMEM] * 3,
        scratch_shapes=[
            pltpu.VMEM((ext_rows, LANES), jnp.float32),
            pltpu.SMEM((patches + 1,), jnp.int32),
        ],
        compiler_params=params(10),
        cost_estimate=pl.CostEstimate(
            flops=2 * patches * share * points * points,
            bytes_accessed=patches * points * points * 2,
            transcendentals=0,
        ),
    )(spans, code, lane, ext, early, inverses)

    corrected_t = pl.pallas_call(
        finish_kernel,
        out_shape=jax.ShapeDtypeStruct(corrected_t.shape, corrected_t.dtype),
        in_specs=[VMEM] * 4,
        out_specs=VMEM,
        compiler_params=params(8),
    )(first, second, rows, corrected_t)
    return jnp.transpose(field_t, (2, 0, 1)), jnp.transpose(corrected_t, (2, 0, 1))


def solution(mesh):
    return jax.shard_map(
        body,
        mesh=mesh,
        in_specs=(
            P("box", None, None),
            P("box", None, None),
            P("box", None),
            P("col", None, None),
            P("box", None),
            P("box", None, None),
        ),
        out_specs=(P("box", "col", None), P("box", "col", None)),
        check_vma=False,
    )
```

```python
import functools

import jax
import jax.numpy as jnp
from jax import lax
from jax.experimental import pallas as pl
from jax.experimental.pallas import tpu as pltpu
from jax.sharding import PartitionSpec as P

RIM = 2
SPAN = 8
EARLY_OPS = 4
LANES = 128
NT = (((1,), (1,)), ((), ()))
ANY = pl.BlockSpec(memory_space=pl.ANY)
VMEM = pl.BlockSpec(memory_space=pltpu.VMEM)
SMEM = pl.BlockSpec(memory_space=pltpu.SMEM)


def round_up(n, m):
    return -(-n // m) * m


def params(limit):
    return pltpu.CompilerParams(vmem_limit_bytes=limit << 20)


def iota(shape, dim):
    return lax.broadcasted_iota(jnp.int32, shape, dim)


def div(x, n):
    if n & (n - 1) == 0:
        return x >> (n.bit_length() - 1)
    return lax.div(x, jnp.int32(n))


def mod(x, n):
    if n & (n - 1) == 0:
        return x & (n - 1)
    return lax.rem(x, jnp.int32(n))


def handled_groups():
    groups = lax.axis_size("col")
    inner = 2 if groups % 2 == 0 else 1
    return inner, groups // inner


def pick_kernel(share, swaps, load, ids_hbm, density_ref, operators_hbm, *rest):
    out_refs, (ids_ref, block, sems) = rest[:-3], rest[-3:]
    if load:
        *out_refs, operators_ref = out_refs
    capacity, dests = ids_ref.shape
    cols, width, boxes = block.shape
    inner, outer = handled_groups()
    col = lax.axis_index("col")
    ids_copy = pltpu.make_async_copy(ids_hbm, ids_ref, sems.at[outer])
    ids_copy.start()
    copies = []
    for j in range(outer):
        group = mod(div(col, inner) + j, outer) * inner + mod(col, inner)
        copy = pltpu.make_async_copy(
            density_ref.at[pl.ds(group * share, share)],
            block.at[pl.ds(j * share, share)],
            sems.at[j],
        )
        copy.start()
        copies.append(copy)
    if load:
        operators_copy = pltpu.make_async_copy(
            operators_hbm.at[pl.ds(0, load)], operators_ref, sems.at[outer + 1]
        )
        operators_copy.start()
    ids_copy.wait()
    rows = dests * cols * capacity
    row = iota((rows, boxes), 0)
    dest = div(row, cols * capacity)
    if swaps:
        dest = dest ^ lax.axis_index("box")
    pair = dest * capacity + mod(row, capacity)
    column = mod(div(row, capacity), cols)

    def place(k, wanted):
        return jnp.where(pair == k, ids_ref[mod(k, capacity), div(k, capacity)], wanted)

    wanted = jnp.full((rows, boxes), -1, jnp.int32)
    if dests * capacity <= 64:
        for k in range(dests * capacity):
            wanted = place(jnp.int32(k), wanted)
    else:
        wanted = lax.fori_loop(0, dests * capacity, place, wanted)
    hit = wanted == iota((rows, boxes), 1)
    for copy in copies:
        copy.wait()
    total = jnp.zeros((rows, width), jnp.float32)
    for c in range(cols):
        chosen = jnp.where(hit & (column == c), 1.0, 0.0).astype(jnp.bfloat16)
        total = total + lax.dot_general(
            chosen, block[c], NT, preferred_element_type=jnp.float32
        )
    total = total.astype(out_refs[0].dtype).reshape(dests, cols * capacity, width)
    if not swaps:
        out_refs[0][...] = total
        return
    for k, ref in enumerate(out_refs[:-1]):
        ref[...] = total[2 * k]
        out_refs[-1][k] = total[2 * k + 1]
    if load:
        operators_copy.wait()


def pick_call(export_ids, density, translations, share, swaps, load):
    boxes, _, width = density.shape
    _, sources, capacity = export_ids.shape
    _, outer = handled_groups()
    block = (outer * share * capacity, width)
    if swaps:
        shapes = [block] * (sources // 2) + [(sources // 2,) + block]
    else:
        shapes = [(sources,) + block]
    return pl.pallas_call(
        functools.partial(pick_kernel, share, swaps, load),
        out_shape=[jax.ShapeDtypeStruct(shape, density.dtype) for shape in shapes]
        + [pltpu.VMEM((load,) + translations.shape[1:], translations.dtype)] * (load > 0),
        in_specs=[ANY] * 3,
        out_specs=[VMEM] * (len(shapes) + (load > 0)),
        scratch_shapes=[
            pltpu.SMEM((capacity, sources), jnp.int32),
            pltpu.VMEM((outer * share, width, boxes), density.dtype),
            pltpu.SemaphoreType.DMA((outer + 2,)),
        ],
        compiler_params=params(8),
    )(
        pltpu.with_memory_space_constraint(export_ids[0].T, pltpu.HBM),
        pltpu.with_memory_space_constraint(jnp.transpose(density, (1, 2, 0)), pltpu.HBM),
        pltpu.with_memory_space_constraint(translations, pltpu.HBM),
    )


def swap_blocks(outgoing):
    *keeps, send = outgoing
    count = lax.axis_size("box")

    def swap(x, mask):
        return lax.ppermute(x, "box", [(i, i ^ mask) for i in range(count)])

    received = swap(send, 1)
    blocks = [keeps[0], received]
    for k in range(1, len(keeps)):
        blocks += [swap(keeps[k], 2 * k), swap(received[k], 2 * k)]
    return blocks


def prepare_kernel(
    slots, tiles, width, local_ops, slots_hbm, points_hbm, operators_hbm,
    picks_ref, code_ref, lane_ref, spans_ref, *rest
):
    *operators_refs, slots_ref, points_ref, hot, sems = rest
    copies = [
        pltpu.make_async_copy(slots_hbm, slots_ref, sems.at[0]),
        pltpu.make_async_copy(points_hbm, points_ref, sems.at[1]),
    ]
    for ref in operators_refs:
        part = operators_hbm.at[pl.ds(local_ops - ref.shape[0], ref.shape[0])]
        copies.append(pltpu.make_async_copy(part, ref, sems.at[2]))
    for copy in copies:
        copy.start()
    copies[0].wait()
    boxes = slots_ref.shape[1]
    patches = code_ref.shape[0]
    inner, outer = handled_groups()
    col = lax.axis_index("col")
    for half in range(inner):
        first = (div(col, inner) * inner + mod(col + half, inner)) * local_ops
        wanted = slots_ref[pl.ds(first, local_ops), :]
        for o in range(local_ops):
            picked = iota((slots, boxes), 0) == wanted[o : o + 1, :]
            at = (half * local_ops + o) * slots
            hot[at : at + slots, :] = jnp.where(picked, 1.0, 0.0).astype(jnp.bfloat16)
    picks_ref[...] = hot[...].T
    copies[1].wait()
    local = points_ref[...] - (lax.axis_index("box") * boxes - RIM) * width
    at_box = ((local.astype(jnp.float32) + 0.5) * (1.0 / width)).astype(jnp.int32)
    at_point = local - at_box * width
    lowest = jnp.min(at_box, axis=1, keepdims=True)
    highest = jnp.max(at_box, axis=1, keepdims=True)
    start = jnp.minimum(lowest, boxes + 2 * RIM - SPAN)
    code = (at_box - start) * tiles + div(at_point, LANES)
    lane = mod(at_point, LANES)
    for p in range(patches):
        code_ref[p] = code[p : p + 1]
        lane_ref[p] = lane[p : p + 1]
        spans_ref[p] = jnp.min(lowest[p : p + 1])
        spans_ref[patches + p] = jnp.min(highest[p : p + 1])
    for copy in copies[2:]:
        copy.wait()


def prepare_call(slots_t, patch_points, translations, load, slots, tiles):
    local_ops, width, _ = translations.shape
    inner, _ = handled_groups()
    boxes = slots_t.shape[1]
    patches, points = patch_points.shape
    all_slots = inner * local_ops * slots
    keep = pltpu.VMEM if load else jax.ShapeDtypeStruct
    return pl.pallas_call(
        functools.partial(prepare_kernel, slots, tiles, width, local_ops),
        out_shape=[
            keep((boxes, all_slots), jnp.bfloat16),
            keep((patches, 1, points), jnp.int32),
            keep((patches, 1, points), jnp.int32),
            jax.ShapeDtypeStruct((2 * patches,), jnp.int32),
        ]
        + [pltpu.VMEM((load, width, width), translations.dtype)] * (load > 0),
        in_specs=[ANY] * 3,
        out_specs=[VMEM] * 3 + [SMEM] + [VMEM] * (load > 0),
        scratch_shapes=[
            pltpu.VMEM(slots_t.shape, slots_t.dtype),
            pltpu.VMEM(patch_points.shape, patch_points.dtype),
            pltpu.VMEM((all_slots, boxes), jnp.bfloat16),
            pltpu.SemaphoreType.DMA((3,)),
        ],
        compiler_params=params(8),
    )(
        pltpu.with_memory_space_constraint(slots_t, pltpu.HBM),
        pltpu.with_memory_space_constraint(patch_points, pltpu.HBM),
        pltpu.with_memory_space_constraint(translations, pltpu.HBM),
    )


def field_kernel(share, capacity, group, arrivals, ready, pending, *refs):
    imported_refs, picks_ref, rest = refs[:arrivals], refs[arrivals], refs[arrivals + 1 :]
    *operator_refs, out_ref, edge_ref, terms, fetched, sems = rest
    ready_refs, pending_refs = operator_refs[: len(ready)], operator_refs[len(ready) :]
    work = [(at + i, ref, i, None) for at, ref in zip(ready, ready_refs) for i in range(ref.shape[0])]
    filled = 0
    for (start, count, at), ref in zip(pending, pending_refs):
        chunk = 4 if count % 4 == 0 else 1
        for i in range(0, count, chunk):
            copy = pltpu.make_async_copy(
                ref.at[pl.ds(start + i, chunk)], fetched.at[pl.ds(filled, chunk)], sems.at[filled]
            )
            copy.start()
            for k in range(chunk):
                work.append((at + i + k, fetched, filled + k, None if k else copy))
            filled += chunk
    if arrivals == 1:
        sources, per_source, width = imported_refs[0].shape
        flat = imported_refs[0][...].reshape(sources * per_source, width)
        swapped = 0
    else:
        sources = arrivals
        per_source, width = imported_refs[0].shape
        pieces = [ref[0] if i == 1 else ref[...] for i, ref in enumerate(imported_refs)]
        flat = jnp.concatenate(pieces, axis=0)
        swapped = lax.axis_index("box")
    boxes = picks_ref.shape[0]
    slots = sources * capacity
    stride = terms.shape[1] // share
    tiles = stride // LANES
    arrived = sources * per_source
    shape = (share * slots, arrived)
    row = iota(shape, 0)
    slot = mod(row, slots)
    origin = (
        (div(slot, capacity) ^ swapped) * per_source
        + (group * share + div(row, slots)) * capacity
        + mod(slot, capacity)
    )
    order = jnp.where(origin == iota(shape, 1), 1.0, 0.0).astype(jnp.bfloat16)
    ordered = jnp.dot(order, flat, preferred_element_type=jnp.float32).astype(jnp.bfloat16)
    for o, ref, i, copy in work:
        if copy is not None:
            copy.wait()
        term = jnp.dot(ordered, ref[i], preferred_element_type=jnp.float32)
        term = term.astype(jnp.bfloat16)
        for c in range(share):
            terms[o * slots : (o + 1) * slots, c * stride : c * stride + width] = term[
                c * slots : (c + 1) * slots
            ]
    total = jnp.dot(picks_ref[...], terms[...], preferred_element_type=jnp.float32)
    total = total.astype(out_ref.dtype)
    for c in range(share):
        out_ref[c] = total[:, c * stride : (c + 1) * stride]
        for t in range(tiles):
            at = (c * tiles + t) * LANES
            to = pl.ds(c * tiles + t, RIM, stride=share * tiles)
            edge_ref[0, to, :] = total[:RIM, at : at + LANES].astype(jnp.float32)
            edge_ref[1, to, :] = total[boxes - RIM :, at : at + LANES].astype(jnp.float32)


def field_call(imported, picks, ready, pending, share, capacity, group, dtype):
    width = imported[0].shape[-1]
    boxes, all_slots = picks.shape
    arrivals = len(imported)
    stride = round_up(width, LANES)
    fetched = sum(count for _, _, count, _ in pending)
    held = all_slots * share * stride * 2 + fetched * width * stride * 2
    return pl.pallas_call(
        functools.partial(
            field_kernel, share, capacity, group, arrivals,
            [at for _, at in ready], [entry[1:] for entry in pending],
        ),
        out_shape=[
            jax.ShapeDtypeStruct((share, boxes, stride), dtype),
            jax.ShapeDtypeStruct((2, RIM * share * (stride // LANES), LANES), jnp.float32),
        ],
        in_specs=[VMEM] * (arrivals + 1 + len(ready)) + [ANY] * len(pending),
        out_specs=[VMEM, VMEM],
        scratch_shapes=[
            pltpu.VMEM((all_slots, share * stride), jnp.bfloat16),
            pltpu.VMEM((max(fetched, 1), width, width), jnp.bfloat16),
            pltpu.SemaphoreType.DMA((max(fetched, 1),)),
        ],
        compiler_params=params(8 + held // (1 << 20)),
        cost_estimate=pl.CostEstimate(
            flops=2 * all_slots * share * width * (width + boxes),
            bytes_accessed=all_slots * share * stride * 2,
            transcendentals=0,
        ),
    )(
        *imported,
        picks,
        *[pltpu.with_memory_space_constraint(array, pltpu.VMEM) for array, _ in ready],
        *[pltpu.with_memory_space_constraint(array, pltpu.HBM) for array, *_ in pending],
    )


def edge_kernel(*refs):
    edge_refs, (first_ref, second_ref) = refs[:-2], refs[-2:]
    total = edge_refs[0][...]
    for ref in edge_refs[1:]:
        total = total + ref[...]
    total = total.astype(jnp.bfloat16).astype(jnp.float32)
    even = mod(lax.axis_index("box"), 2) == 0
    first_ref[...] = jnp.where(even, total[1], total[0])
    second_ref[...] = jnp.where(even, total[0], total[1])


def edge_call(*edges):
    side = jax.ShapeDtypeStruct(edges[0].shape[1:], jnp.float32)
    return pl.pallas_call(
        edge_kernel,
        out_shape=[side, side],
        in_specs=[VMEM] * len(edges),
        out_specs=[VMEM, VMEM],
        compiler_params=params(2),
        cost_estimate=pl.CostEstimate(flops=10**10, bytes_accessed=0, transcendentals=0),
    )(*edges)


def order_patches(spans_ref, order_ref, boxes):
    patches = spans_ref.shape[0] // 2
    count = jnp.int32(0)
    for wanted in (True, False):
        for p in range(patches):
            reaches = (spans_ref[p] < RIM) | (spans_ref[patches + p] >= boxes + RIM)
            order_ref[count] = p
            count = count + jnp.where(reaches == wanted, 1, 0)
        if wanted:
            first = count
    return first


def patch_batch(chosen, spans_ref, code_ref, lane_ref, ext, inverses_ref, spread, share, boxes):
    points = code_ref.shape[2]
    per_box = ext.shape[0] // (boxes + 2 * RIM)
    tiles = per_box // share
    window = SPAN * per_box
    places, products = [], []
    row = iota((window, LANES), 0)
    row_code = div(row, per_box) * tiles + mod(row, tiles)
    for p in chosen:
        start = jnp.minimum(spans_ref[p], boxes + 2 * RIM - SPAN) * per_box
        places.append(pl.ds(pl.multiple_of(start, 8), window))
        held = ext[places[-1], :]
        values = []
        for at in range(0, points, LANES):
            code = code_ref[p, :, at : at + LANES]
            lane = jnp.broadcast_to(lane_ref[p, :, at : at + LANES], (window, LANES))
            found = jnp.take_along_axis(held, lane, axis=1)
            found = jnp.where(row_code == code, found, 0.0)
            found = jnp.sum(found.reshape(SPAN, per_box, LANES), axis=0)
            values.append(jnp.sum(found.reshape(share, tiles, LANES), axis=1))
        values = jnp.concatenate(values, axis=1).astype(jnp.bfloat16)
        product = jnp.dot(values, inverses_ref[p], preferred_element_type=jnp.float32)
        products.append(product.astype(jnp.bfloat16).astype(jnp.float32))
    row = iota((window, points), 0)
    row_code = div(row, per_box) * tiles + mod(row, tiles)
    for p, place, product in zip(chosen, places, products):
        product = jnp.concatenate(
            [jnp.broadcast_to(product[c : c + 1], (tiles, points)) for c in range(share)], axis=0
        )
        product = jnp.concatenate([product] * SPAN, axis=0)
        left = jnp.where(row_code == code_ref[p], product, 0.0).astype(jnp.bfloat16)
        right = jnp.where(iota((LANES, points), 0) == lane_ref[p], 1.0, 0.0)
        placed = lax.dot_general(
            left, right.astype(jnp.bfloat16), NT, preferred_element_type=jnp.float32
        )
        spread[place, :] = spread[place, :] + placed


def batch_size(patches):
    return 2 if patches % 2 == 0 else 1


def early_kernel(
    spans_ref, code_ref, lane_ref, own_ref, received_ref, inverses_ref, first_ref, second_ref,
    ext, spread, first_out, second_out, order_ref,
):
    share, boxes, stride = own_ref.shape
    tiles = stride // LANES
    per_box = share * tiles
    rim = RIM * per_box
    end = rim + boxes * per_box
    patches = code_ref.shape[0]
    even = mod(lax.axis_index("box"), 2) == 0
    first = first_ref[...]
    second = second_ref[...]
    spread[...] = jnp.zeros_like(spread)
    ext[:rim, :] = jnp.where(even, second, first)
    ext[end:, :] = jnp.where(even, first, second)
    for c in range(share):
        for t in range(tiles):
            part = own_ref[c, :, t * LANES : (t + 1) * LANES]
            for r in range(received_ref.shape[0]):
                part = part + received_ref[r, c, :, t * LANES : (t + 1) * LANES].astype(jnp.float32)
            part = part.astype(jnp.bfloat16).astype(jnp.float32)
            ext[pl.ds(rim + c * tiles + t, boxes, stride=per_box), :] = part
    batch = batch_size(patches)
    reaching = order_patches(spans_ref, order_ref, boxes)

    def step(i, carry):
        chosen = [order_ref[i * batch + k] for k in range(batch)]
        patch_batch(chosen, spans_ref, code_ref, lane_ref, ext, inverses_ref, spread, share, boxes)
        return carry

    lax.fori_loop(0, div(reaching + batch - 1, batch), step, 0)
    low = spread[:rim, :]
    high = spread[end:, :]
    first_out[...] = jnp.where(even, high, low)
    second_out[...] = jnp.where(even, low, high)


def late_kernel(
    spans_ref, code_ref, lane_ref, ext, early_ref, inverses_ref,
    field_ref, corrected_ref, rows_ref, spread, order_ref,
):
    share, width, boxes = field_ref.shape
    per_box = ext.shape[0] // (boxes + 2 * RIM)
    tiles = per_box // share
    rim = RIM * per_box
    end = rim + boxes * per_box
    patches = code_ref.shape[0]
    spread[...] = early_ref[...]
    batch = batch_size(patches)
    reaching = order_patches(spans_ref, order_ref, boxes)

    def step(i, carry):
        chosen = [order_ref[i * batch + k] for k in range(batch)]
        patch_batch(chosen, spans_ref, code_ref, lane_ref, ext, inverses_ref, spread, share, boxes)
        return carry

    lax.fori_loop(div(reaching + batch - 1, batch), patches // batch, step, 0)
    for c in range(share):
        for t in range(tiles):
            at = pl.ds(rim + c * tiles + t, boxes, stride=per_box)
            last = min(width - t * LANES, LANES)
            own = ext[at, :]
            total = own + spread[at, :]
            to = slice(t * LANES, t * LANES + last)
            field_ref[c, to, :] = own.T[:last].astype(field_ref.dtype)
            corrected_ref[c, to, :] = total.T[:last].astype(corrected_ref.dtype)
    rows_ref[:rim] = ext[rim : 2 * rim, :] + spread[rim : 2 * rim, :]
    rows_ref[rim:] = ext[end - rim : end, :] + spread[end - rim : end, :]


def finish_kernel(first_ref, second_ref, rows_ref, corrected_ref, out_ref):
    share, width, boxes = corrected_ref.shape
    rim = rows_ref.shape[0] // 2
    per_box = rim // RIM
    tiles = per_box // share
    even = mod(lax.axis_index("box"), 2) == 0
    first = first_ref[...]
    second = second_ref[...]
    low = rows_ref[:rim] + jnp.where(even, second, first)
    high = rows_ref[rim:] + jnp.where(even, first, second)
    rows = jnp.concatenate([low, high], axis=0)
    point = mod(iota(rows.shape, 0), tiles) * LANES + iota(rows.shape, 1)
    rows = jnp.where(point < width, rows, 0.0).T.astype(jnp.bfloat16)
    shape = (2 * rim, per_box * boxes)
    row = iota(shape, 0)
    box = div(mod(row, rim), per_box) + jnp.where(row < rim, 0, boxes - RIM)
    target = mod(row, per_box) * boxes + box
    place = jnp.where(target == iota(shape, 1), 1.0, 0.0).astype(jnp.bfloat16)
    placed = jnp.dot(rows, place, preferred_element_type=jnp.float32)
    box = iota((LANES, boxes), 1)
    edge = (box < RIM) | (box >= boxes - RIM)
    for c in range(share):
        for t in range(tiles):
            last = min(width - t * LANES, LANES)
            at = (c * tiles + t) * boxes
            to = slice(t * LANES, t * LANES + last)
            kept = corrected_ref[c, to, :].astype(jnp.float32)
            out_ref[c, to, :] = jnp.where(
                edge[:last], placed[:last, at : at + boxes], kept
            ).astype(out_ref.dtype)


def swap_sides(first, second):
    count = lax.axis_size("box")

    def moves(start):
        pairs = [(i, i + 1) for i in range(start, count - 1, 2)]
        return pairs + [(b, a) for a, b in pairs]

    return lax.ppermute(first, "box", moves(0)), lax.ppermute(second, "box", moves(1))


def body(density, export_ids, list_slot, translations, patch_points, inverses):
    boxes, total_cols, width = density.shape
    inner, outer = handled_groups()
    share = total_cols // (inner * outer)
    capacity = export_ids.shape[2]
    sources = export_ids.shape[1]
    patches, points = patch_points.shape
    stride = round_up(width, LANES)
    tiles = stride // LANES
    per_box = share * tiles
    places = [(h, k) for h in range(outer) for k in range(inner)]

    others = []
    for i in range(1, inner):
        moves = [(h * inner + (k + i) % inner, h * inner + k) for h, k in places]
        others.append(lax.ppermute(translations, "col", moves))

    swaps = sources <= 16 and sources & (sources - 1) == 0
    local_ops = translations.shape[0]
    early = EARLY_OPS if swaps else 0
    load = local_ops - early if swaps else 0
    outgoing = pick_call(export_ids, density, translations, share, swaps, early)
    ready = []
    if early:
        *outgoing, first_ops = outgoing
        ready.append((first_ops, 0))
    if swaps:
        imported = swap_blocks(outgoing)
    else:
        imported = [lax.all_to_all(outgoing[0], "box", split_axis=0, concat_axis=0, tiled=True)]

    _, *later = lax.optimization_barrier(
        (outgoing[-1], list_slot.T, patch_points, translations)
    )
    picks, code, lane, spans, *loaded = prepare_call(*later, load, sources * capacity, tiles)
    arrived = [(other, (i + 1) * local_ops) for i, other in enumerate(others)]
    pending = []
    if swaps:
        ready += [(array, early) for array in loaded] + arrived
    else:
        pending = [(array, 0, local_ops, at) for array, at in [(translations, 0)] + arrived]
    parts, edges = [], []
    for j in range(1, outer):
        part, edge = field_call(
            imported, picks, ready, pending, share, capacity, j, jnp.bfloat16
        )
        moves = [(h * inner + k, ((h + j) % outer) * inner + k) for h, k in places]
        edges.append(lax.ppermute(edge, "col", moves))
        parts.append(lax.ppermute(part, "col", moves))
    own, edge = field_call(imported, picks, ready, pending, share, capacity, 0, jnp.float32)
    first, second = swap_sides(*edge_call(edge, *edges))
    received = jnp.stack(parts)

    ext_rows = (boxes + 2 * RIM) * per_box
    rim = RIM * per_box
    side = jax.ShapeDtypeStruct((rim, LANES), jnp.float32)
    ext, early, first, second = pl.pallas_call(
        early_kernel,
        out_shape=[
            pltpu.VMEM((ext_rows, LANES), jnp.float32),
            pltpu.VMEM((ext_rows, LANES), jnp.float32),
            side,
            side,
        ],
        in_specs=[SMEM] + [VMEM] * 7,
        out_specs=[VMEM] * 4,
        scratch_shapes=[pltpu.SMEM((patches + 1,), jnp.int32)],
        compiler_params=params(10),
    )(spans, code, lane, own, received, inverses, first, second)
    first, second = swap_sides(first, second)

    field_t, corrected_t, rows = pl.pallas_call(
        late_kernel,
        out_shape=[
            jax.ShapeDtypeStruct((share, width, boxes), jnp.bfloat16),
            pltpu.VMEM((share, width, boxes), jnp.bfloat16),
            pltpu.VMEM((2 * rim, LANES), jnp.float32),
        ],
        in_specs=[SMEM] + [VMEM] * 5,
        out_specs=[VMEM] * 3,
        scratch_shapes=[
            pltpu.VMEM((ext_rows, LANES), jnp.float32),
            pltpu.SMEM((patches + 1,), jnp.int32),
        ],
        compiler_params=params(10),
        cost_estimate=pl.CostEstimate(
            flops=2 * patches * share * points * points,
            bytes_accessed=patches * points * points * 2,
            transcendentals=0,
        ),
    )(spans, code, lane, ext, early, inverses)

    corrected_t = pl.pallas_call(
        finish_kernel,
        out_shape=jax.ShapeDtypeStruct(corrected_t.shape, corrected_t.dtype),
        in_specs=[VMEM] * 4,
        out_specs=VMEM,
        compiler_params=params(8),
    )(first, second, rows, corrected_t)
    return jnp.transpose(field_t, (2, 0, 1)), jnp.transpose(corrected_t, (2, 0, 1))


def solution(mesh):
    return jax.shard_map(
        body,
        mesh=mesh,
        in_specs=(
            P("box", None, None),
            P("box", None, None),
            P("box", None),
            P("col", None, None),
            P("box", None),
            P("box", None, None),
        ),
        out_specs=(P("box", "col", None), P("box", "col", None)),
        check_vma=False,
    )
```

```python
import functools

import jax
import jax.numpy as jnp
from jax import lax
from jax.experimental import pallas as pl
from jax.experimental.pallas import tpu as pltpu
from jax.sharding import PartitionSpec as P

RIM = 2
SPAN = 8
EARLY_OPS = 4
LANES = 128
NT = (((1,), (1,)), ((), ()))
ANY = pl.BlockSpec(memory_space=pl.ANY)
VMEM = pl.BlockSpec(memory_space=pltpu.VMEM)
SMEM = pl.BlockSpec(memory_space=pltpu.SMEM)


def round_up(n, m):
    return -(-n // m) * m


def params(limit):
    return pltpu.CompilerParams(vmem_limit_bytes=limit << 20)


def iota(shape, dim):
    return lax.broadcasted_iota(jnp.int32, shape, dim)


def div(x, n):
    if n & (n - 1) == 0:
        return x >> (n.bit_length() - 1)
    return lax.div(x, jnp.int32(n))


def mod(x, n):
    if n & (n - 1) == 0:
        return x & (n - 1)
    return lax.rem(x, jnp.int32(n))


def handled_groups():
    groups = lax.axis_size("col")
    inner = 2 if groups % 2 == 0 else 1
    return inner, groups // inner


def pick_kernel(share, swaps, load, ids_hbm, density_ref, operators_hbm, *rest):
    out_refs, (ids_ref, block, sems) = rest[:-3], rest[-3:]
    if load:
        *out_refs, operators_ref = out_refs
    capacity, dests = ids_ref.shape
    cols, width, boxes = block.shape
    inner, outer = handled_groups()
    col = lax.axis_index("col")
    ids_copy = pltpu.make_async_copy(ids_hbm, ids_ref, sems.at[outer])
    ids_copy.start()
    copies = []
    for j in range(outer):
        group = mod(div(col, inner) + j, outer) * inner + mod(col, inner)
        copy = pltpu.make_async_copy(
            density_ref.at[pl.ds(group * share, share)],
            block.at[pl.ds(j * share, share)],
            sems.at[j],
        )
        copy.start()
        copies.append(copy)
    if load:
        operators_copy = pltpu.make_async_copy(
            operators_hbm.at[pl.ds(0, load)], operators_ref, sems.at[outer + 1]
        )
        operators_copy.start()
    ids_copy.wait()
    rows = dests * cols * capacity
    row = iota((rows, boxes), 0)
    dest = div(row, cols * capacity)
    if swaps:
        dest = dest ^ lax.axis_index("box")
    pair = dest * capacity + mod(row, capacity)
    column = mod(div(row, capacity), cols)

    def place(k, wanted):
        return jnp.where(pair == k, ids_ref[mod(k, capacity), div(k, capacity)], wanted)

    wanted = jnp.full((rows, boxes), -1, jnp.int32)
    if dests * capacity <= 64:
        for k in range(dests * capacity):
            wanted = place(jnp.int32(k), wanted)
    else:
        wanted = lax.fori_loop(0, dests * capacity, place, wanted)
    hit = wanted == iota((rows, boxes), 1)
    for copy in copies:
        copy.wait()
    total = jnp.zeros((rows, width), jnp.float32)
    for c in range(cols):
        chosen = jnp.where(hit & (column == c), 1.0, 0.0).astype(jnp.bfloat16)
        total = total + lax.dot_general(
            chosen, block[c], NT, preferred_element_type=jnp.float32
        )
    total = total.astype(out_refs[0].dtype).reshape(dests, cols * capacity, width)
    if not swaps:
        out_refs[0][...] = total
        return
    for k, ref in enumerate(out_refs[:-1]):
        ref[...] = total[2 * k]
        out_refs[-1][k] = total[2 * k + 1]
    if load:
        operators_copy.wait()


def pick_call(export_ids, density, translations, share, swaps, load):
    boxes, _, width = density.shape
    _, sources, capacity = export_ids.shape
    _, outer = handled_groups()
    block = (outer * share * capacity, width)
    if swaps:
        shapes = [block] * (sources // 2) + [(sources // 2,) + block]
    else:
        shapes = [(sources,) + block]
    return pl.pallas_call(
        functools.partial(pick_kernel, share, swaps, load),
        out_shape=[jax.ShapeDtypeStruct(shape, density.dtype) for shape in shapes]
        + [pltpu.VMEM((load,) + translations.shape[1:], translations.dtype)] * (load > 0),
        in_specs=[ANY] * 3,
        out_specs=[VMEM] * (len(shapes) + (load > 0)),
        scratch_shapes=[
            pltpu.SMEM((capacity, sources), jnp.int32),
            pltpu.VMEM((outer * share, width, boxes), density.dtype),
            pltpu.SemaphoreType.DMA((outer + 2,)),
        ],
        compiler_params=params(8),
    )(
        pltpu.with_memory_space_constraint(export_ids[0].T, pltpu.HBM),
        pltpu.with_memory_space_constraint(jnp.transpose(density, (1, 2, 0)), pltpu.HBM),
        pltpu.with_memory_space_constraint(translations, pltpu.HBM),
    )


def swap_blocks(outgoing):
    *keeps, send = outgoing
    count = lax.axis_size("box")

    def swap(x, mask):
        return lax.ppermute(x, "box", [(i, i ^ mask) for i in range(count)])

    received = swap(send, 1)
    blocks = [keeps[0], received]
    for k in range(1, len(keeps)):
        blocks += [swap(keeps[k], 2 * k), swap(received[k], 2 * k)]
    return blocks


def prepare_kernel(
    slots, tiles, width, local_ops, slots_hbm, points_hbm, operators_hbm,
    picks_ref, code_ref, lane_ref, spans_ref, *rest
):
    *operators_refs, slots_ref, points_ref, hot, sems = rest
    copies = [
        pltpu.make_async_copy(slots_hbm, slots_ref, sems.at[0]),
        pltpu.make_async_copy(points_hbm, points_ref, sems.at[1]),
    ]
    for ref in operators_refs:
        part = operators_hbm.at[pl.ds(local_ops - ref.shape[0], ref.shape[0])]
        copies.append(pltpu.make_async_copy(part, ref, sems.at[2]))
    for copy in copies:
        copy.start()
    copies[0].wait()
    boxes = slots_ref.shape[1]
    patches = code_ref.shape[0]
    inner, outer = handled_groups()
    col = lax.axis_index("col")
    for half in range(inner):
        first = (div(col, inner) * inner + mod(col + half, inner)) * local_ops
        wanted = slots_ref[pl.ds(first, local_ops), :]
        for o in range(local_ops):
            picked = iota((slots, boxes), 0) == wanted[o : o + 1, :]
            at = (half * local_ops + o) * slots
            hot[at : at + slots, :] = jnp.where(picked, 1.0, 0.0).astype(jnp.bfloat16)
    picks_ref[...] = hot[...].T
    copies[1].wait()
    local = points_ref[...] - (lax.axis_index("box") * boxes - RIM) * width
    at_box = ((local.astype(jnp.float32) + 0.5) * (1.0 / width)).astype(jnp.int32)
    at_point = local - at_box * width
    lowest = jnp.min(at_box, axis=1, keepdims=True)
    highest = jnp.max(at_box, axis=1, keepdims=True)
    start = jnp.minimum(lowest, boxes + 2 * RIM - SPAN)
    code = (at_box - start) * tiles + div(at_point, LANES)
    lane = mod(at_point, LANES)
    for p in range(patches):
        code_ref[p] = code[p : p + 1]
        lane_ref[p] = lane[p : p + 1]
        spans_ref[p] = jnp.min(lowest[p : p + 1])
        spans_ref[patches + p] = jnp.min(highest[p : p + 1])
    for copy in copies[2:]:
        copy.wait()


def prepare_call(slots_t, patch_points, translations, load, slots, tiles):
    local_ops, width, _ = translations.shape
    inner, _ = handled_groups()
    boxes = slots_t.shape[1]
    patches, points = patch_points.shape
    all_slots = inner * local_ops * slots
    keep = pltpu.VMEM if load else jax.ShapeDtypeStruct
    return pl.pallas_call(
        functools.partial(prepare_kernel, slots, tiles, width, local_ops),
        out_shape=[
            keep((boxes, all_slots), jnp.bfloat16),
            keep((patches, 1, points), jnp.int32),
            keep((patches, 1, points), jnp.int32),
            jax.ShapeDtypeStruct((2 * patches,), jnp.int32),
        ]
        + [pltpu.VMEM((load, width, width), translations.dtype)] * (load > 0),
        in_specs=[ANY] * 3,
        out_specs=[VMEM] * 3 + [SMEM] + [VMEM] * (load > 0),
        scratch_shapes=[
            pltpu.VMEM(slots_t.shape, slots_t.dtype),
            pltpu.VMEM(patch_points.shape, patch_points.dtype),
            pltpu.VMEM((all_slots, boxes), jnp.bfloat16),
            pltpu.SemaphoreType.DMA((3,)),
        ],
        compiler_params=params(8),
    )(
        pltpu.with_memory_space_constraint(slots_t, pltpu.HBM),
        pltpu.with_memory_space_constraint(patch_points, pltpu.HBM),
        pltpu.with_memory_space_constraint(translations, pltpu.HBM),
    )


def field_kernel(share, capacity, group, arrivals, ready, pending, *refs):
    imported_refs, picks_ref, rest = refs[:arrivals], refs[arrivals], refs[arrivals + 1 :]
    *operator_refs, out_ref, edge_ref, terms, fetched, sems = rest
    ready_refs, pending_refs = operator_refs[: len(ready)], operator_refs[len(ready) :]
    work = [(at + i, ref, i, None) for at, ref in zip(ready, ready_refs) for i in range(ref.shape[0])]
    filled = 0
    for (start, count, at), ref in zip(pending, pending_refs):
        chunk = 4 if count % 4 == 0 else 1
        for i in range(0, count, chunk):
            copy = pltpu.make_async_copy(
                ref.at[pl.ds(start + i, chunk)], fetched.at[pl.ds(filled, chunk)], sems.at[filled]
            )
            copy.start()
            for k in range(chunk):
                work.append((at + i + k, fetched, filled + k, None if k else copy))
            filled += chunk
    if arrivals == 1:
        sources, per_source, width = imported_refs[0].shape
        flat = imported_refs[0][...].reshape(sources * per_source, width)
        swapped = 0
    else:
        sources = arrivals
        per_source, width = imported_refs[0].shape
        pieces = [ref[0] if i == 1 else ref[...] for i, ref in enumerate(imported_refs)]
        flat = jnp.concatenate(pieces, axis=0)
        swapped = lax.axis_index("box")
    boxes = picks_ref.shape[0]
    slots = sources * capacity
    stride = terms.shape[1] // share
    tiles = stride // LANES
    arrived = sources * per_source
    shape = (share * slots, arrived)
    row = iota(shape, 0)
    slot = mod(row, slots)
    origin = (
        (div(slot, capacity) ^ swapped) * per_source
        + (group * share + div(row, slots)) * capacity
        + mod(slot, capacity)
    )
    order = jnp.where(origin == iota(shape, 1), 1.0, 0.0).astype(jnp.bfloat16)
    ordered = jnp.dot(order, flat, preferred_element_type=jnp.float32).astype(jnp.bfloat16)
    for o, ref, i, copy in work:
        if copy is not None:
            copy.wait()
        term = jnp.dot(ordered, ref[i], preferred_element_type=jnp.float32)
        term = term.astype(jnp.bfloat16)
        for c in range(share):
            terms[o * slots : (o + 1) * slots, c * stride : c * stride + width] = term[
                c * slots : (c + 1) * slots
            ]
    total = jnp.dot(picks_ref[...], terms[...], preferred_element_type=jnp.float32)
    total = total.astype(out_ref.dtype)
    for c in range(share):
        out_ref[c] = total[:, c * stride : (c + 1) * stride]
        for t in range(tiles):
            at = (c * tiles + t) * LANES
            to = pl.ds(c * tiles + t, RIM, stride=share * tiles)
            edge_ref[0, to, :] = total[:RIM, at : at + LANES].astype(jnp.float32)
            edge_ref[1, to, :] = total[boxes - RIM :, at : at + LANES].astype(jnp.float32)


def field_call(imported, picks, ready, pending, share, capacity, group, dtype):
    width = imported[0].shape[-1]
    boxes, all_slots = picks.shape
    arrivals = len(imported)
    stride = round_up(width, LANES)
    fetched = sum(count for _, _, count, _ in pending)
    held = all_slots * share * stride * 2 + fetched * width * stride * 2
    return pl.pallas_call(
        functools.partial(
            field_kernel, share, capacity, group, arrivals,
            [at for _, at in ready], [entry[1:] for entry in pending],
        ),
        out_shape=[
            jax.ShapeDtypeStruct((share, boxes, stride), dtype),
            jax.ShapeDtypeStruct((2, RIM * share * (stride // LANES), LANES), jnp.float32),
        ],
        in_specs=[VMEM] * (arrivals + 1 + len(ready)) + [ANY] * len(pending),
        out_specs=[VMEM, VMEM],
        scratch_shapes=[
            pltpu.VMEM((all_slots, share * stride), jnp.bfloat16),
            pltpu.VMEM((max(fetched, 1), width, width), jnp.bfloat16),
            pltpu.SemaphoreType.DMA((max(fetched, 1),)),
        ],
        compiler_params=params(8 + held // (1 << 20)),
        cost_estimate=pl.CostEstimate(
            flops=2 * all_slots * share * width * (width + boxes),
            bytes_accessed=all_slots * share * stride * 2,
            transcendentals=0,
        ),
    )(
        *imported,
        picks,
        *[pltpu.with_memory_space_constraint(array, pltpu.VMEM) for array, _ in ready],
        *[pltpu.with_memory_space_constraint(array, pltpu.HBM) for array, *_ in pending],
    )


def edge_kernel(share, code_ref, lane_ref, *refs):
    edge_refs, (first_ref, second_ref, rows_ref, lanes_ref) = refs[:-4], refs[-4:]
    total = edge_refs[0][...]
    for ref in edge_refs[1:]:
        total = total + ref[...].astype(jnp.bfloat16).astype(jnp.float32)
    total = total.astype(jnp.bfloat16).astype(jnp.float32)
    even = mod(lax.axis_index("box"), 2) == 0
    first_ref[...] = jnp.where(even, total[1], total[0])
    second_ref[...] = jnp.where(even, total[0], total[1])
    patches, _, points = code_ref.shape
    per_box = total.shape[1] // RIM
    tiles = per_box // share
    row = iota((rows_ref.shape[1], points), 0)
    row_code = div(row, per_box) * tiles + mod(row, tiles)
    lane = iota((LANES, points), 0)
    for p in range(patches):
        rows_ref[p] = jnp.where(row_code == code_ref[p], 1.0, 0.0).astype(jnp.bfloat16)
        lanes_ref[p] = jnp.where(lane == lane_ref[p], 1.0, 0.0).astype(jnp.bfloat16)


def edge_call(code, lane, share, *edges):
    patches, _, points = code.shape
    side = edges[0].shape[1:]
    return pl.pallas_call(
        functools.partial(edge_kernel, share),
        out_shape=[
            jax.ShapeDtypeStruct(side, jnp.float32),
            jax.ShapeDtypeStruct(side, jnp.float32),
            pltpu.VMEM((patches, SPAN * side[0] // RIM, points), jnp.bfloat16),
            pltpu.VMEM((patches, LANES, points), jnp.bfloat16),
        ],
        in_specs=[VMEM] * (2 + len(edges)),
        out_specs=[VMEM] * 4,
        compiler_params=params(4),
        cost_estimate=pl.CostEstimate(flops=10**10, bytes_accessed=0, transcendentals=0),
    )(code, lane, *edges)


def order_patches(spans_ref, order_ref, boxes):
    patches = spans_ref.shape[0] // 2
    count = jnp.int32(0)
    for wanted in (True, False):
        for p in range(patches):
            reaches = (spans_ref[p] < RIM) | (spans_ref[patches + p] >= boxes + RIM)
            order_ref[count] = p
            count = count + jnp.where(reaches == wanted, 1, 0)
        if wanted:
            first = count
    return first


def patch_batch(
    chosen, spans_ref, code_ref, lane_ref, rows_ref, lanes_ref, ext, inverses_ref, spread, share, boxes
):
    points = code_ref.shape[2]
    per_box = ext.shape[0] // (boxes + 2 * RIM)
    tiles = per_box // share
    window = SPAN * per_box
    places, products = [], []
    row = iota((window, LANES), 0)
    row_code = div(row, per_box) * tiles + mod(row, tiles)
    for p in chosen:
        start = jnp.minimum(spans_ref[p], boxes + 2 * RIM - SPAN) * per_box
        places.append(pl.ds(pl.multiple_of(start, 8), window))
        held = ext[places[-1], :]
        values = []
        for at in range(0, points, LANES):
            code = code_ref[p, :, at : at + LANES]
            lane = jnp.broadcast_to(lane_ref[p, :, at : at + LANES], (window, LANES))
            found = jnp.take_along_axis(held, lane, axis=1)
            found = jnp.where(row_code == code, found, 0.0)
            found = jnp.sum(found.reshape(SPAN, per_box, LANES), axis=0)
            values.append(jnp.sum(found.reshape(share, tiles, LANES), axis=1))
        values = jnp.concatenate(values, axis=1).astype(jnp.bfloat16)
        product = jnp.dot(values, inverses_ref[p], preferred_element_type=jnp.float32)
        products.append(product)
    for p, place, product in zip(chosen, places, products):
        product = jnp.concatenate(
            [jnp.broadcast_to(product[c : c + 1], (tiles, points)) for c in range(share)], axis=0
        ).astype(jnp.bfloat16)
        left = rows_ref[p] * jnp.concatenate([product] * SPAN, axis=0)
        placed = lax.dot_general(left, lanes_ref[p], NT, preferred_element_type=jnp.float32)
        spread[place, :] = spread[place, :] + placed


def batch_size(patches):
    return 2 if patches % 2 == 0 else 1


def early_kernel(
    spans_ref, code_ref, lane_ref, own_ref, received_ref, inverses_ref, first_ref, second_ref,
    rows_in, lanes_in,
    ext, spread, first_out, second_out, order_ref,
):
    share, boxes, stride = own_ref.shape
    tiles = stride // LANES
    per_box = share * tiles
    rim = RIM * per_box
    end = rim + boxes * per_box
    patches = code_ref.shape[0]
    even = mod(lax.axis_index("box"), 2) == 0
    first = first_ref[...]
    second = second_ref[...]
    spread[...] = jnp.zeros_like(spread)
    ext[:rim, :] = jnp.where(even, second, first)
    ext[end:, :] = jnp.where(even, first, second)
    for c in range(share):
        for t in range(tiles):
            part = own_ref[c, :, t * LANES : (t + 1) * LANES]
            for r in range(received_ref.shape[0]):
                part = part + received_ref[r, c, :, t * LANES : (t + 1) * LANES].astype(jnp.float32)
            part = part.astype(jnp.bfloat16).astype(jnp.float32)
            ext[pl.ds(rim + c * tiles + t, boxes, stride=per_box), :] = part
    batch = batch_size(patches)
    reaching = order_patches(spans_ref, order_ref, boxes)

    def step(i, carry):
        chosen = [order_ref[i * batch + k] for k in range(batch)]
        patch_batch(
            chosen, spans_ref, code_ref, lane_ref, rows_in, lanes_in, ext, inverses_ref, spread,
            share, boxes,
        )
        return carry

    lax.fori_loop(0, div(reaching + batch - 1, batch), step, 0)
    low = spread[:rim, :]
    high = spread[end:, :]
    first_out[...] = jnp.where(even, high, low)
    second_out[...] = jnp.where(even, low, high)


def late_kernel(
    spans_ref, code_ref, lane_ref, ext, early_ref, inverses_ref, rows_in, lanes_in,
    field_ref, corrected_ref, rows_ref, spread, order_ref,
):
    share, width, boxes = field_ref.shape
    per_box = ext.shape[0] // (boxes + 2 * RIM)
    tiles = per_box // share
    rim = RIM * per_box
    end = rim + boxes * per_box
    patches = code_ref.shape[0]
    spread[...] = early_ref[...]
    batch = batch_size(patches)
    reaching = order_patches(spans_ref, order_ref, boxes)

    begin = div(reaching + batch - 1, batch) * batch
    for size in (2 * batch, batch):

        def step(i, carry, size=size, begin=begin):
            chosen = [order_ref[begin + i * size + k] for k in range(size)]
            patch_batch(
                chosen, spans_ref, code_ref, lane_ref, rows_in, lanes_in, ext, inverses_ref, spread,
                share, boxes,
            )
            return carry

        steps = div(patches - begin, size)
        lax.fori_loop(0, steps, step, 0)
        begin = begin + steps * size
    for c in range(share):
        for t in range(tiles):
            at = pl.ds(rim + c * tiles + t, boxes, stride=per_box)
            last = min(width - t * LANES, LANES)
            own = ext[at, :]
            total = own + spread[at, :]
            to = slice(t * LANES, t * LANES + last)
            field_ref[c, to, :] = own.T[:last].astype(field_ref.dtype)
            corrected_ref[c, to, :] = total.T[:last].astype(corrected_ref.dtype)
    rows_ref[:rim] = ext[rim : 2 * rim, :] + spread[rim : 2 * rim, :]
    rows_ref[rim:] = ext[end - rim : end, :] + spread[end - rim : end, :]


def finish_kernel(first_ref, second_ref, rows_ref, corrected_ref, out_ref):
    share, width, boxes = corrected_ref.shape
    rim = rows_ref.shape[0] // 2
    per_box = rim // RIM
    tiles = per_box // share
    even = mod(lax.axis_index("box"), 2) == 0
    first = first_ref[...]
    second = second_ref[...]
    low = rows_ref[:rim] + jnp.where(even, second, first)
    high = rows_ref[rim:] + jnp.where(even, first, second)
    rows = jnp.concatenate([low, high], axis=0)
    point = mod(iota(rows.shape, 0), tiles) * LANES + iota(rows.shape, 1)
    rows = jnp.where(point < width, rows, 0.0).T.astype(jnp.bfloat16)
    shape = (2 * rim, per_box * boxes)
    row = iota(shape, 0)
    box = div(mod(row, rim), per_box) + jnp.where(row < rim, 0, boxes - RIM)
    target = mod(row, per_box) * boxes + box
    place = jnp.where(target == iota(shape, 1), 1.0, 0.0).astype(jnp.bfloat16)
    placed = jnp.dot(rows, place, preferred_element_type=jnp.float32)
    box = iota((LANES, boxes), 1)
    edge = (box < RIM) | (box >= boxes - RIM)
    for c in range(share):
        for t in range(tiles):
            last = min(width - t * LANES, LANES)
            at = (c * tiles + t) * boxes
            to = slice(t * LANES, t * LANES + last)
            kept = corrected_ref[c, to, :].astype(jnp.float32)
            out_ref[c, to, :] = jnp.where(
                edge[:last], placed[:last, at : at + boxes], kept
            ).astype(out_ref.dtype)


def swap_sides(first, second):
    count = lax.axis_size("box")

    def moves(start):
        pairs = [(i, i + 1) for i in range(start, count - 1, 2)]
        return pairs + [(b, a) for a, b in pairs]

    return lax.ppermute(first, "box", moves(0)), lax.ppermute(second, "box", moves(1))


def body(density, export_ids, list_slot, translations, patch_points, inverses):
    boxes, total_cols, width = density.shape
    inner, outer = handled_groups()
    share = total_cols // (inner * outer)
    capacity = export_ids.shape[2]
    sources = export_ids.shape[1]
    patches, points = patch_points.shape
    stride = round_up(width, LANES)
    tiles = stride // LANES
    per_box = share * tiles
    places = [(h, k) for h in range(outer) for k in range(inner)]

    others = []
    for i in range(1, inner):
        moves = [(h * inner + (k + i) % inner, h * inner + k) for h, k in places]
        others.append(lax.ppermute(translations, "col", moves))

    swaps = sources <= 16 and sources & (sources - 1) == 0
    local_ops = translations.shape[0]
    early = EARLY_OPS if swaps else 0
    load = local_ops - early if swaps else 0
    outgoing = pick_call(export_ids, density, translations, share, swaps, early)
    ready = []
    if early:
        *outgoing, first_ops = outgoing
        ready.append((first_ops, 0))
    if swaps:
        imported = swap_blocks(outgoing)
    else:
        imported = [lax.all_to_all(outgoing[0], "box", split_axis=0, concat_axis=0, tiled=True)]

    _, *later = lax.optimization_barrier(
        (outgoing[-1], list_slot.T, patch_points, translations)
    )
    picks, code, lane, spans, *loaded = prepare_call(*later, load, sources * capacity, tiles)
    arrived = [(other, (i + 1) * local_ops) for i, other in enumerate(others)]
    pending = []
    if swaps:
        ready += [(array, early) for array in loaded] + arrived
    else:
        pending = [(array, 0, local_ops, at) for array, at in [(translations, 0)] + arrived]
    parts, edges = [], []
    for j in range(1, outer):
        part, edge = field_call(
            imported, picks, ready, pending, share, capacity, j, jnp.bfloat16
        )
        moves = [(h * inner + k, ((h + j) % outer) * inner + k) for h, k in places]
        edges.append(lax.ppermute(edge, "col", moves))
        parts.append(lax.ppermute(part, "col", moves))
    own, edge = field_call(imported, picks, ready, pending, share, capacity, 0, jnp.float32)
    first, second, *masks = edge_call(code, lane, share, edge, *edges)
    first, second = swap_sides(first, second)
    received = jnp.stack(parts)

    ext_rows = (boxes + 2 * RIM) * per_box
    rim = RIM * per_box
    side = jax.ShapeDtypeStruct((rim, LANES), jnp.float32)
    ext, early, first, second = pl.pallas_call(
        early_kernel,
        out_shape=[
            pltpu.VMEM((ext_rows, LANES), jnp.float32),
            pltpu.VMEM((ext_rows, LANES), jnp.float32),
            side,
            side,
        ],
        in_specs=[SMEM] + [VMEM] * 9,
        out_specs=[VMEM] * 4,
        scratch_shapes=[pltpu.SMEM((patches + 1,), jnp.int32)],
        compiler_params=params(10),
    )(spans, code, lane, own, received, inverses, first, second, *masks)
    first, second = swap_sides(first, second)

    field_t, corrected_t, rows = pl.pallas_call(
        late_kernel,
        out_shape=[
            jax.ShapeDtypeStruct((share, width, boxes), jnp.bfloat16),
            pltpu.VMEM((share, width, boxes), jnp.bfloat16),
            pltpu.VMEM((2 * rim, LANES), jnp.float32),
        ],
        in_specs=[SMEM] + [VMEM] * 7,
        out_specs=[VMEM] * 3,
        scratch_shapes=[
            pltpu.VMEM((ext_rows, LANES), jnp.float32),
            pltpu.SMEM((patches + 1,), jnp.int32),
        ],
        compiler_params=params(10),
        cost_estimate=pl.CostEstimate(
            flops=2 * patches * share * points * points,
            bytes_accessed=patches * points * points * 2,
            transcendentals=0,
        ),
    )(spans, code, lane, ext, early, inverses, *masks)

    corrected_t = pl.pallas_call(
        finish_kernel,
        out_shape=jax.ShapeDtypeStruct(corrected_t.shape, corrected_t.dtype),
        in_specs=[VMEM] * 4,
        out_specs=VMEM,
        compiler_params=params(8),
    )(first, second, rows, corrected_t)
    return jnp.transpose(field_t, (2, 0, 1)), jnp.transpose(corrected_t, (2, 0, 1))


def solution(mesh):
    return jax.shard_map(
        body,
        mesh=mesh,
        in_specs=(
            P("box", None, None),
            P("box", None, None),
            P("box", None),
            P("col", None, None),
            P("box", None),
            P("box", None, None),
        ),
        out_specs=(P("box", "col", None), P("box", "col", None)),
        check_vma=False,
    )
```

```python
import functools

import jax
import jax.numpy as jnp
from jax import lax
from jax.experimental import pallas as pl
from jax.experimental.pallas import tpu as pltpu
from jax.sharding import PartitionSpec as P

RIM = 2
SPAN = 8
EARLY_OPS = 4
LANES = 128
NT = (((1,), (1,)), ((), ()))
ANY = pl.BlockSpec(memory_space=pl.ANY)
VMEM = pl.BlockSpec(memory_space=pltpu.VMEM)
SMEM = pl.BlockSpec(memory_space=pltpu.SMEM)


def round_up(n, m):
    return -(-n // m) * m


def params(limit):
    return pltpu.CompilerParams(vmem_limit_bytes=limit << 20)


def iota(shape, dim):
    return lax.broadcasted_iota(jnp.int32, shape, dim)


def div(x, n):
    if n & (n - 1) == 0:
        return x >> (n.bit_length() - 1)
    return lax.div(x, jnp.int32(n))


def mod(x, n):
    if n & (n - 1) == 0:
        return x & (n - 1)
    return lax.rem(x, jnp.int32(n))


def handled_groups():
    groups = lax.axis_size("col")
    inner = 2 if groups % 2 == 0 else 1
    return inner, groups // inner


def pick_kernel(share, swaps, load, ids_hbm, density_ref, operators_hbm, *rest):
    out_refs, (ids_ref, block, sems) = rest[:-3], rest[-3:]
    if load:
        *out_refs, operators_ref = out_refs
    capacity, dests = ids_ref.shape
    cols, width, boxes = block.shape
    inner, outer = handled_groups()
    col = lax.axis_index("col")
    ids_copy = pltpu.make_async_copy(ids_hbm, ids_ref, sems.at[outer])
    ids_copy.start()
    copies = []
    for j in range(outer):
        group = mod(div(col, inner) + j, outer) * inner + mod(col, inner)
        copy = pltpu.make_async_copy(
            density_ref.at[pl.ds(group * share, share)],
            block.at[pl.ds(j * share, share)],
            sems.at[j],
        )
        copy.start()
        copies.append(copy)
    if load:
        operators_copy = pltpu.make_async_copy(
            operators_hbm.at[pl.ds(0, load)], operators_ref, sems.at[outer + 1]
        )
        operators_copy.start()
    ids_copy.wait()
    rows = dests * cols * capacity
    row = iota((rows, boxes), 0)
    dest = div(row, cols * capacity)
    if swaps:
        dest = dest ^ lax.axis_index("box")
    pair = dest * capacity + mod(row, capacity)
    column = mod(div(row, capacity), cols)

    def place(k, wanted):
        return jnp.where(pair == k, ids_ref[mod(k, capacity), div(k, capacity)], wanted)

    wanted = jnp.full((rows, boxes), -1, jnp.int32)
    if dests * capacity <= 64:
        for k in range(dests * capacity):
            wanted = place(jnp.int32(k), wanted)
    else:
        wanted = lax.fori_loop(0, dests * capacity, place, wanted)
    hit = wanted == iota((rows, boxes), 1)
    for copy in copies:
        copy.wait()
    total = jnp.zeros((rows, width), jnp.float32)
    for c in range(cols):
        chosen = jnp.where(hit & (column == c), 1.0, 0.0).astype(jnp.bfloat16)
        total = total + lax.dot_general(
            chosen, block[c], NT, preferred_element_type=jnp.float32
        )
    total = total.astype(out_refs[0].dtype).reshape(dests, cols * capacity, width)
    if not swaps:
        out_refs[0][...] = total
        return
    for k, ref in enumerate(out_refs[:-1]):
        ref[...] = total[2 * k]
        out_refs[-1][k] = total[2 * k + 1]
    if load:
        operators_copy.wait()


def pick_call(export_ids, density, translations, share, swaps, load):
    boxes, _, width = density.shape
    _, sources, capacity = export_ids.shape
    _, outer = handled_groups()
    block = (outer * share * capacity, width)
    if swaps:
        shapes = [block] * (sources // 2) + [(sources // 2,) + block]
    else:
        shapes = [(sources,) + block]
    return pl.pallas_call(
        functools.partial(pick_kernel, share, swaps, load),
        out_shape=[jax.ShapeDtypeStruct(shape, density.dtype) for shape in shapes]
        + [pltpu.VMEM((load,) + translations.shape[1:], translations.dtype)] * (load > 0),
        in_specs=[ANY] * 3,
        out_specs=[VMEM] * (len(shapes) + (load > 0)),
        scratch_shapes=[
            pltpu.SMEM((capacity, sources), jnp.int32),
            pltpu.VMEM((outer * share, width, boxes), density.dtype),
            pltpu.SemaphoreType.DMA((outer + 2,)),
        ],
        compiler_params=params(8),
    )(
        pltpu.with_memory_space_constraint(export_ids[0].T, pltpu.HBM),
        pltpu.with_memory_space_constraint(jnp.transpose(density, (1, 2, 0)), pltpu.HBM),
        pltpu.with_memory_space_constraint(translations, pltpu.HBM),
    )


def swap_blocks(outgoing):
    *keeps, send = outgoing
    count = lax.axis_size("box")

    def swap(x, mask):
        return lax.ppermute(x, "box", [(i, i ^ mask) for i in range(count)])

    received = swap(send, 1)
    blocks = [keeps[0], received]
    for k in range(1, len(keeps)):
        blocks += [swap(keeps[k], 2 * k), swap(received[k], 2 * k)]
    return blocks


def prepare_kernel(
    slots, tiles, width, local_ops, slots_hbm, points_hbm, operators_hbm,
    picks_ref, code_ref, lane_ref, spans_ref, *rest
):
    *operators_refs, slots_ref, points_ref, hot, sems = rest
    copies = [
        pltpu.make_async_copy(slots_hbm, slots_ref, sems.at[0]),
        pltpu.make_async_copy(points_hbm, points_ref, sems.at[1]),
    ]
    for ref in operators_refs:
        part = operators_hbm.at[pl.ds(local_ops - ref.shape[0], ref.shape[0])]
        copies.append(pltpu.make_async_copy(part, ref, sems.at[2]))
    for copy in copies:
        copy.start()
    copies[0].wait()
    boxes = slots_ref.shape[1]
    patches = code_ref.shape[0]
    inner, outer = handled_groups()
    col = lax.axis_index("col")
    for half in range(inner):
        first = (div(col, inner) * inner + mod(col + half, inner)) * local_ops
        wanted = slots_ref[pl.ds(first, local_ops), :]
        for o in range(local_ops):
            picked = iota((slots, boxes), 0) == wanted[o : o + 1, :]
            at = (half * local_ops + o) * slots
            hot[at : at + slots, :] = jnp.where(picked, 1.0, 0.0).astype(jnp.bfloat16)
    picks_ref[...] = hot[...].T
    copies[1].wait()
    local = points_ref[...] - (lax.axis_index("box") * boxes - RIM) * width
    at_box = ((local.astype(jnp.float32) + 0.5) * (1.0 / width)).astype(jnp.int32)
    at_point = local - at_box * width
    lowest = jnp.min(at_box, axis=1, keepdims=True)
    highest = jnp.max(at_box, axis=1, keepdims=True)
    start = jnp.minimum(lowest, boxes + 2 * RIM - SPAN)
    code = (at_box - start) * tiles + div(at_point, LANES)
    lane = mod(at_point, LANES)
    for p in range(patches):
        code_ref[p] = code[p : p + 1]
        lane_ref[p] = lane[p : p + 1]
        spans_ref[p] = jnp.min(lowest[p : p + 1])
        spans_ref[patches + p] = jnp.min(highest[p : p + 1])
    for copy in copies[2:]:
        copy.wait()


def prepare_call(slots_t, patch_points, translations, load, slots, tiles):
    local_ops, width, _ = translations.shape
    inner, _ = handled_groups()
    boxes = slots_t.shape[1]
    patches, points = patch_points.shape
    all_slots = inner * local_ops * slots
    keep = pltpu.VMEM if load else jax.ShapeDtypeStruct
    return pl.pallas_call(
        functools.partial(prepare_kernel, slots, tiles, width, local_ops),
        out_shape=[
            keep((boxes, all_slots), jnp.bfloat16),
            keep((patches, 1, points), jnp.int32),
            keep((patches, 1, points), jnp.int32),
            jax.ShapeDtypeStruct((2 * patches,), jnp.int32),
        ]
        + [pltpu.VMEM((load, width, width), translations.dtype)] * (load > 0),
        in_specs=[ANY] * 3,
        out_specs=[VMEM] * 3 + [SMEM] + [VMEM] * (load > 0),
        scratch_shapes=[
            pltpu.VMEM(slots_t.shape, slots_t.dtype),
            pltpu.VMEM(patch_points.shape, patch_points.dtype),
            pltpu.VMEM((all_slots, boxes), jnp.bfloat16),
            pltpu.SemaphoreType.DMA((3,)),
        ],
        compiler_params=params(8),
    )(
        pltpu.with_memory_space_constraint(slots_t, pltpu.HBM),
        pltpu.with_memory_space_constraint(patch_points, pltpu.HBM),
        pltpu.with_memory_space_constraint(translations, pltpu.HBM),
    )


def field_kernel(share, capacity, group, arrivals, ready, pending, *refs):
    imported_refs, picks_ref, rest = refs[:arrivals], refs[arrivals], refs[arrivals + 1 :]
    *operator_refs, out_ref, edge_ref, terms, fetched, sems = rest
    ready_refs, pending_refs = operator_refs[: len(ready)], operator_refs[len(ready) :]
    work = [(at + i, ref, i, None) for at, ref in zip(ready, ready_refs) for i in range(ref.shape[0])]
    filled = 0
    for (start, count, at), ref in zip(pending, pending_refs):
        chunk = 4 if count % 4 == 0 else 1
        for i in range(0, count, chunk):
            copy = pltpu.make_async_copy(
                ref.at[pl.ds(start + i, chunk)], fetched.at[pl.ds(filled, chunk)], sems.at[filled]
            )
            copy.start()
            for k in range(chunk):
                work.append((at + i + k, fetched, filled + k, None if k else copy))
            filled += chunk
    if arrivals == 1:
        sources, per_source, width = imported_refs[0].shape
        flat = imported_refs[0][...].reshape(sources * per_source, width)
        swapped = 0
    else:
        sources = arrivals
        per_source, width = imported_refs[0].shape
        pieces = [ref[0] if i == 1 else ref[...] for i, ref in enumerate(imported_refs)]
        flat = jnp.concatenate(pieces, axis=0)
        swapped = lax.axis_index("box")
    boxes = picks_ref.shape[0]
    slots = sources * capacity
    stride = terms.shape[1] // share
    tiles = stride // LANES
    arrived = sources * per_source
    shape = (share * slots, arrived)
    row = iota(shape, 0)
    slot = mod(row, slots)
    origin = (
        (div(slot, capacity) ^ swapped) * per_source
        + (group * share + div(row, slots)) * capacity
        + mod(slot, capacity)
    )
    order = jnp.where(origin == iota(shape, 1), 1.0, 0.0).astype(jnp.bfloat16)
    ordered = jnp.dot(order, flat, preferred_element_type=jnp.float32).astype(jnp.bfloat16)
    for o, ref, i, copy in work:
        if copy is not None:
            copy.wait()
        term = jnp.dot(ordered, ref[i], preferred_element_type=jnp.float32)
        term = term.astype(jnp.bfloat16)
        for c in range(share):
            terms[o * slots : (o + 1) * slots, c * stride : c * stride + width] = term[
                c * slots : (c + 1) * slots
            ]
    total = jnp.dot(picks_ref[...], terms[...], preferred_element_type=jnp.float32)
    total = total.astype(out_ref.dtype)
    for c in range(share):
        out_ref[c] = total[:, c * stride : (c + 1) * stride]
        for t in range(tiles):
            at = (c * tiles + t) * LANES
            to = pl.ds(c * tiles + t, RIM, stride=share * tiles)
            edge_ref[0, to, :] = total[:RIM, at : at + LANES].astype(jnp.float32)
            edge_ref[1, to, :] = total[boxes - RIM :, at : at + LANES].astype(jnp.float32)


def field_call(imported, picks, ready, pending, share, capacity, group, dtype):
    width = imported[0].shape[-1]
    boxes, all_slots = picks.shape
    arrivals = len(imported)
    stride = round_up(width, LANES)
    fetched = sum(count for _, _, count, _ in pending)
    held = all_slots * share * stride * 2 + fetched * width * stride * 2
    return pl.pallas_call(
        functools.partial(
            field_kernel, share, capacity, group, arrivals,
            [at for _, at in ready], [entry[1:] for entry in pending],
        ),
        out_shape=[
            jax.ShapeDtypeStruct((share, boxes, stride), dtype),
            jax.ShapeDtypeStruct((2, RIM * share * (stride // LANES), LANES), jnp.float32),
        ],
        in_specs=[VMEM] * (arrivals + 1 + len(ready)) + [ANY] * len(pending),
        out_specs=[VMEM, VMEM],
        scratch_shapes=[
            pltpu.VMEM((all_slots, share * stride), jnp.bfloat16),
            pltpu.VMEM((max(fetched, 1), width, width), jnp.bfloat16),
            pltpu.SemaphoreType.DMA((max(fetched, 1),)),
        ],
        compiler_params=params(8 + held // (1 << 20)),
        cost_estimate=pl.CostEstimate(
            flops=2 * all_slots * share * width * (width + boxes),
            bytes_accessed=all_slots * share * stride * 2,
            transcendentals=0,
        ),
    )(
        *imported,
        picks,
        *[pltpu.with_memory_space_constraint(array, pltpu.VMEM) for array, _ in ready],
        *[pltpu.with_memory_space_constraint(array, pltpu.HBM) for array, *_ in pending],
    )


def edge_kernel(share, code_ref, lane_ref, *refs):
    edge_refs, (first_ref, second_ref, rows_ref, lanes_ref) = refs[:-4], refs[-4:]
    total = edge_refs[0][...]
    for ref in edge_refs[1:]:
        total = total + ref[...].astype(jnp.bfloat16).astype(jnp.float32)
    total = total.astype(jnp.bfloat16).astype(jnp.float32)
    even = mod(lax.axis_index("box"), 2) == 0
    first_ref[...] = jnp.where(even, total[1], total[0])
    second_ref[...] = jnp.where(even, total[0], total[1])
    patches, _, points = code_ref.shape
    per_box = total.shape[1] // RIM
    tiles = per_box // share
    row = iota((rows_ref.shape[1], points), 0)
    row_code = div(row, per_box) * tiles + mod(row, tiles)
    lane = iota((LANES, points), 0)
    for p in range(patches):
        rows_ref[p] = jnp.where(row_code == code_ref[p], 1.0, 0.0).astype(jnp.bfloat16)
        lanes_ref[p] = jnp.where(lane == lane_ref[p], 1.0, 0.0).astype(jnp.bfloat16)


def edge_call(code, lane, share, *edges):
    patches, _, points = code.shape
    side = edges[0].shape[1:]
    return pl.pallas_call(
        functools.partial(edge_kernel, share),
        out_shape=[
            jax.ShapeDtypeStruct(side, jnp.float32),
            jax.ShapeDtypeStruct(side, jnp.float32),
            pltpu.VMEM((patches, SPAN * side[0] // RIM, points), jnp.bfloat16),
            pltpu.VMEM((patches, LANES, points), jnp.bfloat16),
        ],
        in_specs=[VMEM] * (2 + len(edges)),
        out_specs=[VMEM] * 4,
        compiler_params=params(4),
        cost_estimate=pl.CostEstimate(flops=10**10, bytes_accessed=0, transcendentals=0),
    )(code, lane, *edges)


def order_patches(spans_ref, order_ref, boxes):
    patches = spans_ref.shape[0] // 2
    count = jnp.int32(0)
    for wanted in (True, False):
        for p in range(patches):
            reaches = (spans_ref[p] < RIM) | (spans_ref[patches + p] >= boxes + RIM)
            order_ref[count] = p
            count = count + jnp.where(reaches == wanted, 1, 0)
        if wanted:
            first = count
    return first


def patch_batch(
    chosen, spans_ref, code_ref, lane_ref, rows_ref, lanes_ref, ext, inverses_ref, spread, share, boxes
):
    points = code_ref.shape[2]
    per_box = ext.shape[0] // (boxes + 2 * RIM)
    tiles = per_box // share
    window = SPAN * per_box
    places, products = [], []
    row = iota((window, LANES), 0)
    row_code = div(row, per_box) * tiles + mod(row, tiles)
    for p in chosen:
        start = jnp.minimum(spans_ref[p], boxes + 2 * RIM - SPAN) * per_box
        places.append(pl.ds(pl.multiple_of(start, 8), window))
        held = ext[places[-1], :]
        values = []
        for at in range(0, points, LANES):
            code = code_ref[p, :, at : at + LANES]
            lane = jnp.broadcast_to(lane_ref[p, :, at : at + LANES], (window, LANES))
            found = jnp.take_along_axis(held, lane, axis=1)
            found = jnp.where(row_code == code, found, 0.0)
            found = jnp.sum(found.reshape(SPAN, per_box, LANES), axis=0)
            values.append(jnp.sum(found.reshape(share, tiles, LANES), axis=1))
        values = jnp.concatenate(values, axis=1).astype(jnp.bfloat16)
        product = jnp.dot(values, inverses_ref[p], preferred_element_type=jnp.float32)
        products.append(product)
    for p, place, product in zip(chosen, places, products):
        product = jnp.concatenate(
            [jnp.broadcast_to(product[c : c + 1], (tiles, points)) for c in range(share)], axis=0
        ).astype(jnp.bfloat16)
        left = rows_ref[p] * jnp.concatenate([product] * SPAN, axis=0)
        placed = lax.dot_general(left, lanes_ref[p], NT, preferred_element_type=jnp.float32)
        spread[place, :] = spread[place, :] + placed


def batch_size(patches):
    return 2 if patches % 2 == 0 else 1


def early_kernel(
    spans_ref, code_ref, lane_ref, own_ref, received_ref, inverses_ref, first_ref, second_ref,
    rows_in, lanes_in,
    ext, spread, first_out, second_out, order_ref,
):
    share, boxes, stride = own_ref.shape
    tiles = stride // LANES
    per_box = share * tiles
    rim = RIM * per_box
    end = rim + boxes * per_box
    patches = code_ref.shape[0]
    even = mod(lax.axis_index("box"), 2) == 0
    first = first_ref[...]
    second = second_ref[...]
    spread[...] = jnp.zeros_like(spread)
    ext[:rim, :] = jnp.where(even, second, first)
    ext[end:, :] = jnp.where(even, first, second)
    for c in range(share):
        for t in range(tiles):
            part = own_ref[c, :, t * LANES : (t + 1) * LANES]
            for r in range(received_ref.shape[0]):
                part = part + received_ref[r, c, :, t * LANES : (t + 1) * LANES].astype(jnp.float32)
            part = part.astype(jnp.bfloat16).astype(jnp.float32)
            ext[pl.ds(rim + c * tiles + t, boxes, stride=per_box), :] = part
    batch = batch_size(patches)
    reaching = order_patches(spans_ref, order_ref, boxes)

    def step(i, carry):
        chosen = [order_ref[i * batch + k] for k in range(batch)]
        patch_batch(
            chosen, spans_ref, code_ref, lane_ref, rows_in, lanes_in, ext, inverses_ref, spread,
            share, boxes,
        )
        return carry

    lax.fori_loop(0, div(reaching + batch - 1, batch), step, 0)
    low = spread[:rim, :]
    high = spread[end:, :]
    first_out[...] = jnp.where(even, high, low)
    second_out[...] = jnp.where(even, low, high)


def late_kernel(
    spans_ref, code_ref, lane_ref, ext, early_ref, inverses_ref, rows_in, lanes_in,
    field_hbm, corrected_ref, rows_ref, spread, field_ref, order_ref, sem,
):
    share, width, boxes = field_ref.shape
    per_box = ext.shape[0] // (boxes + 2 * RIM)
    tiles = per_box // share
    rim = RIM * per_box
    end = rim + boxes * per_box
    patches = code_ref.shape[0]
    for c in range(share):
        for t in range(tiles):
            own = ext[pl.ds(rim + c * tiles + t, boxes, stride=per_box), :]
            last = min(width - t * LANES, LANES)
            field_ref[c, t * LANES : t * LANES + last, :] = own.T[:last].astype(field_ref.dtype)
    field_copy = pltpu.make_async_copy(field_ref, field_hbm, sem)
    field_copy.start()
    spread[...] = early_ref[...]
    batch = batch_size(patches)
    reaching = order_patches(spans_ref, order_ref, boxes)

    begin = div(reaching + batch - 1, batch) * batch
    for size in (2 * batch, batch):

        def step(i, carry, size=size, begin=begin):
            chosen = [order_ref[begin + i * size + k] for k in range(size)]
            patch_batch(
                chosen, spans_ref, code_ref, lane_ref, rows_in, lanes_in, ext, inverses_ref, spread,
                share, boxes,
            )
            return carry

        steps = div(patches - begin, size)
        lax.fori_loop(0, steps, step, 0)
        begin = begin + steps * size
    for c in range(share):
        for t in range(tiles):
            at = pl.ds(rim + c * tiles + t, boxes, stride=per_box)
            last = min(width - t * LANES, LANES)
            total = ext[at, :] + spread[at, :]
            to = slice(t * LANES, t * LANES + last)
            corrected_ref[c, to, :] = total.T[:last].astype(corrected_ref.dtype)
    rows_ref[:rim] = ext[rim : 2 * rim, :] + spread[rim : 2 * rim, :]
    rows_ref[rim:] = ext[end - rim : end, :] + spread[end - rim : end, :]
    field_copy.wait()


def finish_kernel(first_ref, second_ref, rows_ref, corrected_ref, out_hbm, out_ref, sems):
    share, width, boxes = corrected_ref.shape
    rim = rows_ref.shape[0] // 2
    per_box = rim // RIM
    tiles = per_box // share
    even = mod(lax.axis_index("box"), 2) == 0
    first = first_ref[...]
    second = second_ref[...]
    low = rows_ref[:rim] + jnp.where(even, second, first)
    high = rows_ref[rim:] + jnp.where(even, first, second)
    rows = jnp.concatenate([low, high], axis=0)
    point = mod(iota(rows.shape, 0), tiles) * LANES + iota(rows.shape, 1)
    rows = jnp.where(point < width, rows, 0.0).T.astype(jnp.bfloat16)
    shape = (2 * rim, per_box * boxes)
    row = iota(shape, 0)
    box = div(mod(row, rim), per_box) + jnp.where(row < rim, 0, boxes - RIM)
    target = mod(row, per_box) * boxes + box
    place = jnp.where(target == iota(shape, 1), 1.0, 0.0).astype(jnp.bfloat16)
    placed = jnp.dot(rows, place, preferred_element_type=jnp.float32)
    box = iota((LANES, boxes), 1)
    edge = (box < RIM) | (box >= boxes - RIM)
    for c in range(share):
        for t in range(tiles):
            last = min(width - t * LANES, LANES)
            at = (c * tiles + t) * boxes
            to = slice(t * LANES, t * LANES + last)
            kept = corrected_ref[c, to, :].astype(jnp.float32)
            out_ref[c, to, :] = jnp.where(
                edge[:last], placed[:last, at : at + boxes], kept
            ).astype(out_ref.dtype)
        pltpu.make_async_copy(out_ref.at[c], out_hbm.at[c], sems.at[c]).start()
    for c in range(share):
        pltpu.make_async_copy(out_ref.at[c], out_hbm.at[c], sems.at[c]).wait()


def swap_sides(first, second):
    count = lax.axis_size("box")

    def moves(start):
        pairs = [(i, i + 1) for i in range(start, count - 1, 2)]
        return pairs + [(b, a) for a, b in pairs]

    return lax.ppermute(first, "box", moves(0)), lax.ppermute(second, "box", moves(1))


def body(density, export_ids, list_slot, translations, patch_points, inverses):
    boxes, total_cols, width = density.shape
    inner, outer = handled_groups()
    share = total_cols // (inner * outer)
    capacity = export_ids.shape[2]
    sources = export_ids.shape[1]
    patches, points = patch_points.shape
    stride = round_up(width, LANES)
    tiles = stride // LANES
    per_box = share * tiles
    places = [(h, k) for h in range(outer) for k in range(inner)]

    others = []
    for i in range(1, inner):
        moves = [(h * inner + (k + i) % inner, h * inner + k) for h, k in places]
        others.append(lax.ppermute(translations, "col", moves))

    swaps = sources <= 16 and sources & (sources - 1) == 0
    local_ops = translations.shape[0]
    early = EARLY_OPS if swaps else 0
    load = local_ops - early if swaps else 0
    outgoing = pick_call(export_ids, density, translations, share, swaps, early)
    ready = []
    if early:
        *outgoing, first_ops = outgoing
        ready.append((first_ops, 0))
    if swaps:
        imported = swap_blocks(outgoing)
    else:
        imported = [lax.all_to_all(outgoing[0], "box", split_axis=0, concat_axis=0, tiled=True)]

    _, *later = lax.optimization_barrier(
        (outgoing[-1], list_slot.T, patch_points, translations)
    )
    picks, code, lane, spans, *loaded = prepare_call(*later, load, sources * capacity, tiles)
    arrived = [(other, (i + 1) * local_ops) for i, other in enumerate(others)]
    pending = []
    if swaps:
        ready += [(array, early) for array in loaded] + arrived
    else:
        pending = [(array, 0, local_ops, at) for array, at in [(translations, 0)] + arrived]
    parts, edges = [], []
    for j in range(1, outer):
        part, edge = field_call(
            imported, picks, ready, pending, share, capacity, j, jnp.bfloat16
        )
        moves = [(h * inner + k, ((h + j) % outer) * inner + k) for h, k in places]
        edges.append(lax.ppermute(edge, "col", moves))
        parts.append(lax.ppermute(part, "col", moves))
    own, edge = field_call(imported, picks, ready, pending, share, capacity, 0, jnp.float32)
    first, second, *masks = edge_call(code, lane, share, edge, *edges)
    first, second = swap_sides(first, second)
    received = jnp.stack(parts)

    ext_rows = (boxes + 2 * RIM) * per_box
    rim = RIM * per_box
    side = jax.ShapeDtypeStruct((rim, LANES), jnp.float32)
    ext, early, first, second = pl.pallas_call(
        early_kernel,
        out_shape=[
            pltpu.VMEM((ext_rows, LANES), jnp.float32),
            pltpu.VMEM((ext_rows, LANES), jnp.float32),
            side,
            side,
        ],
        in_specs=[SMEM] + [VMEM] * 9,
        out_specs=[VMEM] * 4,
        scratch_shapes=[pltpu.SMEM((patches + 1,), jnp.int32)],
        compiler_params=params(10),
    )(spans, code, lane, own, received, inverses, first, second, *masks)
    first, second = swap_sides(first, second)

    field_t, corrected_t, rows = pl.pallas_call(
        late_kernel,
        out_shape=[
            jax.ShapeDtypeStruct((share, width, boxes), jnp.bfloat16),
            pltpu.VMEM((share, width, boxes), jnp.bfloat16),
            pltpu.VMEM((2 * rim, LANES), jnp.float32),
        ],
        in_specs=[SMEM] + [VMEM] * 7,
        out_specs=[ANY, VMEM, VMEM],
        scratch_shapes=[
            pltpu.VMEM((ext_rows, LANES), jnp.float32),
            pltpu.VMEM((share, width, boxes), jnp.bfloat16),
            pltpu.SMEM((patches + 1,), jnp.int32),
            pltpu.SemaphoreType.DMA,
        ],
        compiler_params=params(10),
        cost_estimate=pl.CostEstimate(
            flops=2 * patches * share * points * points,
            bytes_accessed=patches * points * points * 2,
            transcendentals=0,
        ),
    )(spans, code, lane, ext, early, inverses, *masks)

    corrected_t = pl.pallas_call(
        finish_kernel,
        out_shape=jax.ShapeDtypeStruct(corrected_t.shape, corrected_t.dtype),
        in_specs=[VMEM] * 4,
        out_specs=ANY,
        scratch_shapes=[
            pltpu.VMEM(corrected_t.shape, corrected_t.dtype),
            pltpu.SemaphoreType.DMA((share,)),
        ],
        compiler_params=params(8),
    )(first, second, rows, corrected_t)
    return jnp.transpose(field_t, (2, 0, 1)), jnp.transpose(corrected_t, (2, 0, 1))


def solution(mesh):
    return jax.shard_map(
        body,
        mesh=mesh,
        in_specs=(
            P("box", None, None),
            P("box", None, None),
            P("box", None),
            P("col", None, None),
            P("box", None),
            P("box", None, None),
        ),
        out_specs=(P("box", "col", None), P("box", "col", None)),
        check_vma=False,
    )
```

```python
import functools

import jax
import jax.numpy as jnp
from jax import lax
from jax.experimental import pallas as pl
from jax.experimental.pallas import tpu as pltpu
from jax.sharding import PartitionSpec as P

RIM = 2
SPAN = 8
EARLY_OPS = 4
LANES = 128
NT = (((1,), (1,)), ((), ()))
ANY = pl.BlockSpec(memory_space=pl.ANY)
VMEM = pl.BlockSpec(memory_space=pltpu.VMEM)
SMEM = pl.BlockSpec(memory_space=pltpu.SMEM)


def round_up(n, m):
    return -(-n // m) * m


def params(limit):
    return pltpu.CompilerParams(vmem_limit_bytes=limit << 20)


def iota(shape, dim):
    return lax.broadcasted_iota(jnp.int32, shape, dim)


def div(x, n):
    if n & (n - 1) == 0:
        return x >> (n.bit_length() - 1)
    return lax.div(x, jnp.int32(n))


def mod(x, n):
    if n & (n - 1) == 0:
        return x & (n - 1)
    return lax.rem(x, jnp.int32(n))


def handled_groups():
    groups = lax.axis_size("col")
    inner = 2 if groups % 2 == 0 else 1
    return inner, groups // inner


def pick_kernel(share, swaps, load, ids_hbm, density_ref, operators_hbm, *rest):
    out_refs, (ids_ref, block, sems) = rest[:-3], rest[-3:]
    if load:
        *out_refs, operators_ref = out_refs
    capacity, dests = ids_ref.shape
    cols, width, boxes = block.shape
    inner, outer = handled_groups()
    col = lax.axis_index("col")
    ids_copy = pltpu.make_async_copy(ids_hbm, ids_ref, sems.at[outer])
    ids_copy.start()
    copies = []
    for j in range(outer):
        group = mod(div(col, inner) + j, outer) * inner + mod(col, inner)
        copy = pltpu.make_async_copy(
            density_ref.at[pl.ds(group * share, share)],
            block.at[pl.ds(j * share, share)],
            sems.at[j],
        )
        copy.start()
        copies.append(copy)
    if load:
        operators_copy = pltpu.make_async_copy(
            operators_hbm.at[pl.ds(0, load)], operators_ref, sems.at[outer + 1]
        )
        operators_copy.start()
    ids_copy.wait()
    rows = dests * cols * capacity
    row = iota((rows, boxes), 0)
    dest = div(row, cols * capacity)
    if swaps:
        dest = dest ^ lax.axis_index("box")
    pair = dest * capacity + mod(row, capacity)
    column = mod(div(row, capacity), cols)

    def place(k, wanted):
        return jnp.where(pair == k, ids_ref[mod(k, capacity), div(k, capacity)], wanted)

    wanted = jnp.full((rows, boxes), -1, jnp.int32)
    if dests * capacity <= 64:
        for k in range(dests * capacity):
            wanted = place(jnp.int32(k), wanted)
    else:
        wanted = lax.fori_loop(0, dests * capacity, place, wanted)
    hit = wanted == iota((rows, boxes), 1)
    for copy in copies:
        copy.wait()
    total = jnp.zeros((rows, width), jnp.float32)
    for c in range(cols):
        chosen = jnp.where(hit & (column == c), 1.0, 0.0).astype(jnp.bfloat16)
        total = total + lax.dot_general(
            chosen, block[c], NT, preferred_element_type=jnp.float32
        )
    total = total.astype(out_refs[0].dtype).reshape(dests, cols * capacity, width)
    if not swaps:
        out_refs[0][...] = total
        return
    for k, ref in enumerate(out_refs[:-1]):
        ref[...] = total[2 * k]
        out_refs[-1][k] = total[2 * k + 1]
    if load:
        operators_copy.wait()


def pick_call(export_ids, density, translations, share, swaps, load):
    boxes, _, width = density.shape
    _, sources, capacity = export_ids.shape
    _, outer = handled_groups()
    block = (outer * share * capacity, width)
    if swaps:
        shapes = [block] * (sources // 2) + [(sources // 2,) + block]
    else:
        shapes = [(sources,) + block]
    return pl.pallas_call(
        functools.partial(pick_kernel, share, swaps, load),
        out_shape=[jax.ShapeDtypeStruct(shape, density.dtype) for shape in shapes]
        + [pltpu.VMEM((load,) + translations.shape[1:], translations.dtype)] * (load > 0),
        in_specs=[ANY] * 3,
        out_specs=[VMEM] * (len(shapes) + (load > 0)),
        scratch_shapes=[
            pltpu.SMEM((capacity, sources), jnp.int32),
            pltpu.VMEM((outer * share, width, boxes), density.dtype),
            pltpu.SemaphoreType.DMA((outer + 2,)),
        ],
        compiler_params=params(8),
    )(
        pltpu.with_memory_space_constraint(export_ids[0].T, pltpu.HBM),
        pltpu.with_memory_space_constraint(jnp.transpose(density, (1, 2, 0)), pltpu.HBM),
        pltpu.with_memory_space_constraint(translations, pltpu.HBM),
    )


def swap_blocks(outgoing):
    *keeps, send = outgoing
    count = lax.axis_size("box")

    def swap(x, mask):
        return lax.ppermute(x, "box", [(i, i ^ mask) for i in range(count)])

    received = swap(send, 1)
    blocks = [keeps[0], received]
    for k in range(1, len(keeps)):
        blocks += [swap(keeps[k], 2 * k), swap(received[k], 2 * k)]
    return blocks


def prepare_kernel(
    slots, tiles, width, local_ops, slots_hbm, points_hbm, operators_hbm,
    picks_ref, code_ref, lane_ref, spans_ref, *rest
):
    *operators_refs, slots_ref, points_ref, hot, sems = rest
    copies = [
        pltpu.make_async_copy(slots_hbm, slots_ref, sems.at[0]),
        pltpu.make_async_copy(points_hbm, points_ref, sems.at[1]),
    ]
    for ref in operators_refs:
        part = operators_hbm.at[pl.ds(local_ops - ref.shape[0], ref.shape[0])]
        copies.append(pltpu.make_async_copy(part, ref, sems.at[2]))
    for copy in copies:
        copy.start()
    copies[0].wait()
    boxes = slots_ref.shape[1]
    patches = code_ref.shape[0]
    inner, outer = handled_groups()
    col = lax.axis_index("col")
    for half in range(inner):
        first = (div(col, inner) * inner + mod(col + half, inner)) * local_ops
        wanted = slots_ref[pl.ds(first, local_ops), :]
        for o in range(local_ops):
            picked = iota((slots, boxes), 0) == wanted[o : o + 1, :]
            at = (half * local_ops + o) * slots
            hot[at : at + slots, :] = jnp.where(picked, 1.0, 0.0).astype(jnp.bfloat16)
    picks_ref[...] = hot[...].T
    copies[1].wait()
    local = points_ref[...] - (lax.axis_index("box") * boxes - RIM) * width
    at_box = ((local.astype(jnp.float32) + 0.5) * (1.0 / width)).astype(jnp.int32)
    at_point = local - at_box * width
    lowest = jnp.min(at_box, axis=1, keepdims=True)
    highest = jnp.max(at_box, axis=1, keepdims=True)
    start = jnp.minimum(lowest, boxes + 2 * RIM - SPAN)
    code = (at_box - start) * tiles + div(at_point, LANES)
    lane = mod(at_point, LANES)
    for p in range(patches):
        code_ref[p] = code[p : p + 1]
        lane_ref[p] = lane[p : p + 1]
        spans_ref[p] = jnp.min(lowest[p : p + 1])
        spans_ref[patches + p] = jnp.min(highest[p : p + 1])
    for copy in copies[2:]:
        copy.wait()


def prepare_call(slots_t, patch_points, translations, load, slots, tiles):
    local_ops, width, _ = translations.shape
    inner, _ = handled_groups()
    boxes = slots_t.shape[1]
    patches, points = patch_points.shape
    all_slots = inner * local_ops * slots
    keep = pltpu.VMEM if load else jax.ShapeDtypeStruct
    return pl.pallas_call(
        functools.partial(prepare_kernel, slots, tiles, width, local_ops),
        out_shape=[
            keep((boxes, all_slots), jnp.bfloat16),
            keep((patches, 1, points), jnp.int32),
            keep((patches, 1, points), jnp.int32),
            jax.ShapeDtypeStruct((2 * patches,), jnp.int32),
        ]
        + [pltpu.VMEM((load, width, width), translations.dtype)] * (load > 0),
        in_specs=[ANY] * 3,
        out_specs=[VMEM] * 3 + [SMEM] + [VMEM] * (load > 0),
        scratch_shapes=[
            pltpu.VMEM(slots_t.shape, slots_t.dtype),
            pltpu.VMEM(patch_points.shape, patch_points.dtype),
            pltpu.VMEM((all_slots, boxes), jnp.bfloat16),
            pltpu.SemaphoreType.DMA((3,)),
        ],
        compiler_params=params(8),
    )(
        pltpu.with_memory_space_constraint(slots_t, pltpu.HBM),
        pltpu.with_memory_space_constraint(patch_points, pltpu.HBM),
        pltpu.with_memory_space_constraint(translations, pltpu.HBM),
    )


def field_kernel(share, capacity, group, arrivals, ready, pending, *refs):
    imported_refs, picks_ref, rest = refs[:arrivals], refs[arrivals], refs[arrivals + 1 :]
    *operator_refs, out_ref, edge_ref, terms, fetched, sems = rest
    ready_refs, pending_refs = operator_refs[: len(ready)], operator_refs[len(ready) :]
    work = [(at + i, ref, i, None) for at, ref in zip(ready, ready_refs) for i in range(ref.shape[0])]
    filled = 0
    for (start, count, at), ref in zip(pending, pending_refs):
        chunk = 4 if count % 4 == 0 else 1
        for i in range(0, count, chunk):
            copy = pltpu.make_async_copy(
                ref.at[pl.ds(start + i, chunk)], fetched.at[pl.ds(filled, chunk)], sems.at[filled]
            )
            copy.start()
            for k in range(chunk):
                work.append((at + i + k, fetched, filled + k, None if k else copy))
            filled += chunk
    if arrivals == 1:
        sources, per_source, width = imported_refs[0].shape
        flat = imported_refs[0][...].reshape(sources * per_source, width)
        swapped = 0
    else:
        sources = arrivals
        per_source, width = imported_refs[0].shape
        pieces = [ref[0] if i == 1 else ref[...] for i, ref in enumerate(imported_refs)]
        flat = jnp.concatenate(pieces, axis=0)
        swapped = lax.axis_index("box")
    boxes = picks_ref.shape[0]
    slots = sources * capacity
    stride = terms.shape[1] // share
    tiles = stride // LANES
    arrived = sources * per_source
    shape = (share * slots, arrived)
    row = iota(shape, 0)
    slot = mod(row, slots)
    origin = (
        (div(slot, capacity) ^ swapped) * per_source
        + (group * share + div(row, slots)) * capacity
        + mod(slot, capacity)
    )
    order = jnp.where(origin == iota(shape, 1), 1.0, 0.0).astype(jnp.bfloat16)
    ordered = jnp.dot(order, flat, preferred_element_type=jnp.float32).astype(jnp.bfloat16)
    for o, ref, i, copy in work:
        if copy is not None:
            copy.wait()
        term = jnp.dot(ordered, ref[i], preferred_element_type=jnp.float32)
        term = term.astype(jnp.bfloat16)
        for c in range(share):
            terms[o * slots : (o + 1) * slots, c * stride : c * stride + width] = term[
                c * slots : (c + 1) * slots
            ]
    total = jnp.dot(picks_ref[...], terms[...], preferred_element_type=jnp.float32)
    if out_ref.shape[0] != share:
        total = total.astype(out_ref.dtype).astype(jnp.float32)
        for at, part in enumerate(pack_columns(total, share, tiles, width)):
            out_ref[at] = part.astype(out_ref.dtype)
    for c in range(share):
        if out_ref.shape[0] == share:
            out_ref[c] = total[:, c * stride : (c + 1) * stride].astype(out_ref.dtype)
        for t in range(tiles):
            at = (c * tiles + t) * LANES
            to = pl.ds(c * tiles + t, RIM, stride=share * tiles)
            edge_ref[0, to, :] = total[:RIM, at : at + LANES]
            edge_ref[1, to, :] = total[boxes - RIM :, at : at + LANES]


def pack_columns(total, share, tiles, width):
    last = width - (tiles - 1) * LANES
    blocks, tails = [], []
    for c in range(share):
        for t in range(tiles):
            at = (c * tiles + t) * LANES
            if t < tiles - 1:
                blocks.append(total[:, at : at + LANES])
            else:
                tails.append(total[:, at : at + last])
    rest = -(share * last) % LANES
    if rest:
        tails.append(jnp.zeros((total.shape[0], rest), total.dtype))
    tails = jnp.concatenate(tails, axis=1)
    return blocks + [tails[:, at : at + LANES] for at in range(0, tails.shape[1], LANES)]


def packed_blocks(share, tiles, width):
    last = width - (tiles - 1) * LANES
    return share * (tiles - 1) + round_up(share * last, LANES) // LANES


def unpack_columns(blocks, share, tiles, width):
    last = width - (tiles - 1) * LANES
    full = share * (tiles - 1)
    tails = jnp.concatenate(blocks[full:], axis=1)
    blank = jnp.zeros((tails.shape[0], LANES - last), tails.dtype)
    columns = []
    for c in range(share):
        tail = tails[:, c * last : (c + 1) * last]
        if last < LANES:
            tail = jnp.concatenate([tail, blank], axis=1)
        columns.append(blocks[c * (tiles - 1) : (c + 1) * (tiles - 1)] + [tail])
    return columns


def field_call(imported, picks, ready, pending, share, capacity, group, dtype):
    width = imported[0].shape[-1]
    boxes, all_slots = picks.shape
    arrivals = len(imported)
    stride = round_up(width, LANES)
    shape = (share, boxes, stride)
    if dtype == jnp.bfloat16:
        shape = (packed_blocks(share, stride // LANES, width), boxes, LANES)
    fetched = sum(count for _, _, count, _ in pending)
    held = all_slots * share * stride * 2 + fetched * width * stride * 2
    return pl.pallas_call(
        functools.partial(
            field_kernel, share, capacity, group, arrivals,
            [at for _, at in ready], [entry[1:] for entry in pending],
        ),
        out_shape=[
            jax.ShapeDtypeStruct(shape, dtype),
            jax.ShapeDtypeStruct((2, RIM * share * (stride // LANES), LANES), jnp.float32),
        ],
        in_specs=[VMEM] * (arrivals + 1 + len(ready)) + [ANY] * len(pending),
        out_specs=[VMEM, VMEM],
        scratch_shapes=[
            pltpu.VMEM((all_slots, share * stride), jnp.bfloat16),
            pltpu.VMEM((max(fetched, 1), width, width), jnp.bfloat16),
            pltpu.SemaphoreType.DMA((max(fetched, 1),)),
        ],
        compiler_params=params(8 + held // (1 << 20)),
        cost_estimate=pl.CostEstimate(
            flops=2 * all_slots * share * width * (width + boxes),
            bytes_accessed=all_slots * share * stride * 2,
            transcendentals=0,
        ),
    )(
        *imported,
        picks,
        *[pltpu.with_memory_space_constraint(array, pltpu.VMEM) for array, _ in ready],
        *[pltpu.with_memory_space_constraint(array, pltpu.HBM) for array, *_ in pending],
    )


def edge_kernel(share, code_ref, lane_ref, *refs):
    edge_refs, (first_ref, second_ref, rows_ref, lanes_ref) = refs[:-4], refs[-4:]
    total = edge_refs[0][...]
    for ref in edge_refs[1:]:
        total = total + ref[...].astype(jnp.bfloat16).astype(jnp.float32)
    total = total.astype(jnp.bfloat16).astype(jnp.float32)
    even = mod(lax.axis_index("box"), 2) == 0
    first_ref[...] = jnp.where(even, total[1], total[0])
    second_ref[...] = jnp.where(even, total[0], total[1])
    patches, _, points = code_ref.shape
    per_box = total.shape[1] // RIM
    tiles = per_box // share
    row = iota((rows_ref.shape[1], points), 0)
    row_code = div(row, per_box) * tiles + mod(row, tiles)
    lane = iota((LANES, points), 0)
    for p in range(patches):
        rows_ref[p] = jnp.where(row_code == code_ref[p], 1.0, 0.0).astype(jnp.bfloat16)
        lanes_ref[p] = jnp.where(lane == lane_ref[p], 1.0, 0.0).astype(jnp.bfloat16)


def edge_call(code, lane, share, *edges):
    patches, _, points = code.shape
    side = edges[0].shape[1:]
    return pl.pallas_call(
        functools.partial(edge_kernel, share),
        out_shape=[
            jax.ShapeDtypeStruct(side, jnp.float32),
            jax.ShapeDtypeStruct(side, jnp.float32),
            pltpu.VMEM((patches, SPAN * side[0] // RIM, points), jnp.bfloat16),
            pltpu.VMEM((patches, LANES, points), jnp.bfloat16),
        ],
        in_specs=[VMEM] * (2 + len(edges)),
        out_specs=[VMEM] * 4,
        compiler_params=params(4),
        cost_estimate=pl.CostEstimate(flops=10**10, bytes_accessed=0, transcendentals=0),
    )(code, lane, *edges)


def order_patches(spans_ref, order_ref, boxes):
    patches = spans_ref.shape[0] // 2
    count = jnp.int32(0)
    for wanted in (True, False):
        for p in range(patches):
            reaches = (spans_ref[p] < RIM) | (spans_ref[patches + p] >= boxes + RIM)
            order_ref[count] = p
            count = count + jnp.where(reaches == wanted, 1, 0)
        if wanted:
            first = count
    return first


def patch_batch(
    chosen, spans_ref, code_ref, lane_ref, rows_ref, lanes_ref, ext, inverses_ref, spread, share, boxes
):
    points = code_ref.shape[2]
    per_box = ext.shape[0] // (boxes + 2 * RIM)
    tiles = per_box // share
    window = SPAN * per_box
    places, products = [], []
    row = iota((window, LANES), 0)
    row_code = div(row, per_box) * tiles + mod(row, tiles)
    for p in chosen:
        start = jnp.minimum(spans_ref[p], boxes + 2 * RIM - SPAN) * per_box
        places.append(pl.ds(pl.multiple_of(start, 8), window))
        held = ext[places[-1], :]
        values = []
        for at in range(0, points, LANES):
            code = code_ref[p, :, at : at + LANES]
            lane = jnp.broadcast_to(lane_ref[p, :, at : at + LANES], (window, LANES))
            found = jnp.take_along_axis(held, lane, axis=1)
            found = jnp.where(row_code == code, found, 0.0)
            found = jnp.sum(found.reshape(SPAN, per_box, LANES), axis=0)
            values.append(jnp.sum(found.reshape(share, tiles, LANES), axis=1))
        values = jnp.concatenate(values, axis=1).astype(jnp.bfloat16)
        product = jnp.dot(values, inverses_ref[p], preferred_element_type=jnp.float32)
        products.append(product)
    for p, place, product in zip(chosen, places, products):
        product = jnp.concatenate(
            [jnp.broadcast_to(product[c : c + 1], (tiles, points)) for c in range(share)], axis=0
        ).astype(jnp.bfloat16)
        left = rows_ref[p] * jnp.concatenate([product] * SPAN, axis=0)
        placed = lax.dot_general(left, lanes_ref[p], NT, preferred_element_type=jnp.float32)
        spread[place, :] = spread[place, :] + placed


def batch_size(patches):
    return 2 if patches % 2 == 0 else 1


def early_kernel(
    width, spans_ref, code_ref, lane_ref, own_ref, received_ref, inverses_ref, first_ref, second_ref,
    rows_in, lanes_in,
    ext, spread, first_out, second_out, order_ref,
):
    share, boxes, stride = own_ref.shape
    tiles = stride // LANES
    per_box = share * tiles
    rim = RIM * per_box
    end = rim + boxes * per_box
    patches = code_ref.shape[0]
    even = mod(lax.axis_index("box"), 2) == 0
    first = first_ref[...]
    second = second_ref[...]
    spread[...] = jnp.zeros_like(spread)
    ext[:rim, :] = jnp.where(even, second, first)
    ext[end:, :] = jnp.where(even, first, second)
    received = []
    for r in range(received_ref.shape[0]):
        blocks = [received_ref[r, k].astype(jnp.float32) for k in range(received_ref.shape[1])]
        received.append(unpack_columns(blocks, share, tiles, width))
    for c in range(share):
        for t in range(tiles):
            part = own_ref[c, :, t * LANES : (t + 1) * LANES]
            for columns in received:
                part = part + columns[c][t]
            part = part.astype(jnp.bfloat16).astype(jnp.float32)
            ext[pl.ds(rim + c * tiles + t, boxes, stride=per_box), :] = part
    batch = batch_size(patches)
    reaching = order_patches(spans_ref, order_ref, boxes)

    def step(i, carry):
        chosen = [order_ref[i * batch + k] for k in range(batch)]
        patch_batch(
            chosen, spans_ref, code_ref, lane_ref, rows_in, lanes_in, ext, inverses_ref, spread,
            share, boxes,
        )
        return carry

    lax.fori_loop(0, div(reaching + batch - 1, batch), step, 0)
    low = spread[:rim, :]
    high = spread[end:, :]
    first_out[...] = jnp.where(even, high, low)
    second_out[...] = jnp.where(even, low, high)


def late_kernel(
    spans_ref, code_ref, lane_ref, ext, early_ref, inverses_ref, rows_in, lanes_in,
    field_hbm, corrected_ref, rows_ref, spread, field_ref, order_ref, sem,
):
    share, width, boxes = field_ref.shape
    per_box = ext.shape[0] // (boxes + 2 * RIM)
    tiles = per_box // share
    rim = RIM * per_box
    end = rim + boxes * per_box
    patches = code_ref.shape[0]
    for c in range(share):
        for t in range(tiles):
            own = ext[pl.ds(rim + c * tiles + t, boxes, stride=per_box), :]
            last = min(width - t * LANES, LANES)
            field_ref[c, t * LANES : t * LANES + last, :] = own.T[:last].astype(field_ref.dtype)
    field_copy = pltpu.make_async_copy(field_ref, field_hbm, sem)
    field_copy.start()
    spread[...] = early_ref[...]
    batch = batch_size(patches)
    reaching = order_patches(spans_ref, order_ref, boxes)

    begin = div(reaching + batch - 1, batch) * batch
    for size in (2 * batch, batch):

        def step(i, carry, size=size, begin=begin):
            chosen = [order_ref[begin + i * size + k] for k in range(size)]
            patch_batch(
                chosen, spans_ref, code_ref, lane_ref, rows_in, lanes_in, ext, inverses_ref, spread,
                share, boxes,
            )
            return carry

        steps = div(patches - begin, size)
        lax.fori_loop(0, steps, step, 0)
        begin = begin + steps * size
    for c in range(share):
        for t in range(tiles):
            at = pl.ds(rim + c * tiles + t, boxes, stride=per_box)
            last = min(width - t * LANES, LANES)
            total = ext[at, :] + spread[at, :]
            to = slice(t * LANES, t * LANES + last)
            corrected_ref[c, to, :] = total.T[:last].astype(corrected_ref.dtype)
    rows_ref[:rim] = ext[rim : 2 * rim, :] + spread[rim : 2 * rim, :]
    rows_ref[rim:] = ext[end - rim : end, :] + spread[end - rim : end, :]
    field_copy.wait()


def finish_kernel(first_ref, second_ref, rows_ref, corrected_ref, out_hbm, out_ref, sems):
    share, width, boxes = corrected_ref.shape
    rim = rows_ref.shape[0] // 2
    per_box = rim // RIM
    tiles = per_box // share
    even = mod(lax.axis_index("box"), 2) == 0
    first = first_ref[...]
    second = second_ref[...]
    low = rows_ref[:rim] + jnp.where(even, second, first)
    high = rows_ref[rim:] + jnp.where(even, first, second)
    rows = jnp.concatenate([low, high], axis=0)
    point = mod(iota(rows.shape, 0), tiles) * LANES + iota(rows.shape, 1)
    rows = jnp.where(point < width, rows, 0.0).T.astype(jnp.bfloat16)
    shape = (2 * rim, per_box * boxes)
    row = iota(shape, 0)
    box = div(mod(row, rim), per_box) + jnp.where(row < rim, 0, boxes - RIM)
    target = mod(row, per_box) * boxes + box
    place = jnp.where(target == iota(shape, 1), 1.0, 0.0).astype(jnp.bfloat16)
    placed = jnp.dot(rows, place, preferred_element_type=jnp.float32)
    box = iota((LANES, boxes), 1)
    edge = (box < RIM) | (box >= boxes - RIM)
    for c in range(share):
        for t in range(tiles):
            last = min(width - t * LANES, LANES)
            at = (c * tiles + t) * boxes
            to = slice(t * LANES, t * LANES + last)
            kept = corrected_ref[c, to, :].astype(jnp.float32)
            out_ref[c, to, :] = jnp.where(
                edge[:last], placed[:last, at : at + boxes], kept
            ).astype(out_ref.dtype)
        pltpu.make_async_copy(out_ref.at[c], out_hbm.at[c], sems.at[c]).start()
    for c in range(share):
        pltpu.make_async_copy(out_ref.at[c], out_hbm.at[c], sems.at[c]).wait()


def swap_sides(first, second):
    count = lax.axis_size("box")

    def moves(start):
        pairs = [(i, i + 1) for i in range(start, count - 1, 2)]
        return pairs + [(b, a) for a, b in pairs]

    return lax.ppermute(first, "box", moves(0)), lax.ppermute(second, "box", moves(1))


def body(density, export_ids, list_slot, translations, patch_points, inverses):
    boxes, total_cols, width = density.shape
    inner, outer = handled_groups()
    share = total_cols // (inner * outer)
    capacity = export_ids.shape[2]
    sources = export_ids.shape[1]
    patches, points = patch_points.shape
    stride = round_up(width, LANES)
    tiles = stride // LANES
    per_box = share * tiles
    places = [(h, k) for h in range(outer) for k in range(inner)]

    others = []
    for i in range(1, inner):
        moves = [(h * inner + (k + i) % inner, h * inner + k) for h, k in places]
        others.append(lax.ppermute(translations, "col", moves))

    swaps = sources <= 16 and sources & (sources - 1) == 0
    local_ops = translations.shape[0]
    early = EARLY_OPS if swaps else 0
    load = local_ops - early if swaps else 0
    outgoing = pick_call(export_ids, density, translations, share, swaps, early)
    ready = []
    if early:
        *outgoing, first_ops = outgoing
        ready.append((first_ops, 0))
    if swaps:
        imported = swap_blocks(outgoing)
    else:
        imported = [lax.all_to_all(outgoing[0], "box", split_axis=0, concat_axis=0, tiled=True)]

    _, *later = lax.optimization_barrier(
        (outgoing[-1], list_slot.T, patch_points, translations)
    )
    picks, code, lane, spans, *loaded = prepare_call(*later, load, sources * capacity, tiles)
    arrived = [(other, (i + 1) * local_ops) for i, other in enumerate(others)]
    pending = []
    if swaps:
        ready += [(array, early) for array in loaded] + arrived
    else:
        pending = [(array, 0, local_ops, at) for array, at in [(translations, 0)] + arrived]
    parts, edges = [], []
    for j in range(1, outer):
        part, edge = field_call(
            imported, picks, ready, pending, share, capacity, j, jnp.bfloat16
        )
        moves = [(h * inner + k, ((h + j) % outer) * inner + k) for h, k in places]
        edges.append(lax.ppermute(edge, "col", moves))
        parts.append(lax.ppermute(part, "col", moves))
    own, edge = field_call(imported, picks, ready, pending, share, capacity, 0, jnp.float32)
    first, second, *masks = edge_call(code, lane, share, edge, *edges)
    first, second = swap_sides(first, second)
    received = jnp.stack(parts)

    ext_rows = (boxes + 2 * RIM) * per_box
    rim = RIM * per_box
    side = jax.ShapeDtypeStruct((rim, LANES), jnp.float32)
    ext, early, first, second = pl.pallas_call(
        functools.partial(early_kernel, width),
        out_shape=[
            pltpu.VMEM((ext_rows, LANES), jnp.float32),
            pltpu.VMEM((ext_rows, LANES), jnp.float32),
            side,
            side,
        ],
        in_specs=[SMEM] + [VMEM] * 9,
        out_specs=[VMEM] * 4,
        scratch_shapes=[pltpu.SMEM((patches + 1,), jnp.int32)],
        compiler_params=params(10),
    )(spans, code, lane, own, received, inverses, first, second, *masks)
    first, second = swap_sides(first, second)

    field_t, corrected_t, rows = pl.pallas_call(
        late_kernel,
        out_shape=[
            jax.ShapeDtypeStruct((share, width, boxes), jnp.bfloat16),
            pltpu.VMEM((share, width, boxes), jnp.bfloat16),
            pltpu.VMEM((2 * rim, LANES), jnp.float32),
        ],
        in_specs=[SMEM] + [VMEM] * 7,
        out_specs=[ANY, VMEM, VMEM],
        scratch_shapes=[
            pltpu.VMEM((ext_rows, LANES), jnp.float32),
            pltpu.VMEM((share, width, boxes), jnp.bfloat16),
            pltpu.SMEM((patches + 1,), jnp.int32),
            pltpu.SemaphoreType.DMA,
        ],
        compiler_params=params(10),
        cost_estimate=pl.CostEstimate(
            flops=2 * patches * share * points * points,
            bytes_accessed=patches * points * points * 2,
            transcendentals=0,
        ),
    )(spans, code, lane, ext, early, inverses, *masks)

    corrected_t = pl.pallas_call(
        finish_kernel,
        out_shape=jax.ShapeDtypeStruct(corrected_t.shape, corrected_t.dtype),
        in_specs=[VMEM] * 4,
        out_specs=ANY,
        scratch_shapes=[
            pltpu.VMEM(corrected_t.shape, corrected_t.dtype),
            pltpu.SemaphoreType.DMA((share,)),
        ],
        compiler_params=params(8),
    )(first, second, rows, corrected_t)
    return jnp.transpose(field_t, (2, 0, 1)), jnp.transpose(corrected_t, (2, 0, 1))


def solution(mesh):
    return jax.shard_map(
        body,
        mesh=mesh,
        in_specs=(
            P("box", None, None),
            P("box", None, None),
            P("box", None),
            P("col", None, None),
            P("box", None),
            P("box", None, None),
        ),
        out_specs=(P("box", "col", None), P("box", "col", None)),
        check_vma=False,
    )
```

```python
import functools

import jax
import jax.numpy as jnp
from jax import lax
from jax.experimental import pallas as pl
from jax.experimental.pallas import tpu as pltpu
from jax.sharding import PartitionSpec as P

RIM = 2
SPAN = 8
EARLY_OPS = 4
LANES = 128
NT = (((1,), (1,)), ((), ()))
ANY = pl.BlockSpec(memory_space=pl.ANY)
VMEM = pl.BlockSpec(memory_space=pltpu.VMEM)
SMEM = pl.BlockSpec(memory_space=pltpu.SMEM)


def round_up(n, m):
    return -(-n // m) * m


def params(limit):
    return pltpu.CompilerParams(vmem_limit_bytes=limit << 20)


def iota(shape, dim):
    return lax.broadcasted_iota(jnp.int32, shape, dim)


def div(x, n):
    if n & (n - 1) == 0:
        return x >> (n.bit_length() - 1)
    return lax.div(x, jnp.int32(n))


def mod(x, n):
    if n & (n - 1) == 0:
        return x & (n - 1)
    return lax.rem(x, jnp.int32(n))


def handled_groups():
    groups = lax.axis_size("col")
    inner = 2 if groups % 2 == 0 else 1
    return inner, groups // inner


def pick_kernel(share, swaps, load, ids_hbm, density_ref, operators_hbm, *rest):
    out_refs, (ids_ref, block, sems) = rest[:-3], rest[-3:]
    if load:
        *out_refs, operators_ref = out_refs
    capacity, dests = ids_ref.shape
    cols, width, boxes = block.shape
    inner, outer = handled_groups()
    col = lax.axis_index("col")
    ids_copy = pltpu.make_async_copy(ids_hbm, ids_ref, sems.at[outer])
    ids_copy.start()
    copies = []
    for j in range(outer):
        group = mod(div(col, inner) + j, outer) * inner + mod(col, inner)
        copy = pltpu.make_async_copy(
            density_ref.at[pl.ds(group * share, share)],
            block.at[pl.ds(j * share, share)],
            sems.at[j],
        )
        copy.start()
        copies.append(copy)
    if load:
        operators_copy = pltpu.make_async_copy(
            operators_hbm.at[pl.ds(0, load)], operators_ref, sems.at[outer + 1]
        )
        operators_copy.start()
    ids_copy.wait()
    rows = dests * cols * capacity
    row = iota((rows, boxes), 0)
    dest = div(row, cols * capacity)
    if swaps:
        dest = dest ^ lax.axis_index("box")
    pair = dest * capacity + mod(row, capacity)
    column = mod(div(row, capacity), cols)

    def place(k, wanted):
        return jnp.where(pair == k, ids_ref[mod(k, capacity), div(k, capacity)], wanted)

    wanted = jnp.full((rows, boxes), -1, jnp.int32)
    if dests * capacity <= 64:
        for k in range(dests * capacity):
            wanted = place(jnp.int32(k), wanted)
    else:
        wanted = lax.fori_loop(0, dests * capacity, place, wanted)
    hit = wanted == iota((rows, boxes), 1)
    for copy in copies:
        copy.wait()
    total = jnp.zeros((rows, width), jnp.float32)
    for c in range(cols):
        chosen = jnp.where(hit & (column == c), 1.0, 0.0).astype(jnp.bfloat16)
        total = total + lax.dot_general(
            chosen, block[c], NT, preferred_element_type=jnp.float32
        )
    total = total.astype(out_refs[0].dtype).reshape(dests, cols * capacity, width)
    if not swaps:
        out_refs[0][...] = total
        return
    out_refs[0][...] = total[0]
    out_refs[1][...] = total[1]
    for k, ref in enumerate(out_refs[2:], 1):
        ref[...] = total[2 * k : 2 * k + 2]
    if load:
        operators_copy.wait()


def pick_call(export_ids, density, translations, share, swaps, load):
    boxes, _, width = density.shape
    _, sources, capacity = export_ids.shape
    _, outer = handled_groups()
    block = (outer * share * capacity, width)
    if swaps:
        shapes = [block] * 2 + [(2,) + block] * (sources // 2 - 1)
    else:
        shapes = [(sources,) + block]
    return pl.pallas_call(
        functools.partial(pick_kernel, share, swaps, load),
        out_shape=[jax.ShapeDtypeStruct(shape, density.dtype) for shape in shapes]
        + [pltpu.VMEM((load,) + translations.shape[1:], translations.dtype)] * (load > 0),
        in_specs=[ANY] * 3,
        out_specs=[VMEM] * (len(shapes) + (load > 0)),
        scratch_shapes=[
            pltpu.SMEM((capacity, sources), jnp.int32),
            pltpu.VMEM((outer * share, width, boxes), density.dtype),
            pltpu.SemaphoreType.DMA((outer + 2,)),
        ],
        compiler_params=params(8),
    )(
        pltpu.with_memory_space_constraint(export_ids[0].T, pltpu.HBM),
        pltpu.with_memory_space_constraint(jnp.transpose(density, (1, 2, 0)), pltpu.HBM),
        pltpu.with_memory_space_constraint(translations, pltpu.HBM),
    )


def swap_mask(x, mask):
    count = lax.axis_size("box")
    return lax.ppermute(x, "box", [(i, i ^ mask) for i in range(count)])


def swap_far(outgoing):
    return [swap_mask(pair, 2 * k) for k, pair in enumerate(outgoing[2:], 1)]


def swap_near(outgoing, pairs, prepared):
    blocks = [outgoing[0], swap_mask(outgoing[1], 1)]
    for pair in pairs:
        second, prepared = lax.optimization_barrier((pair[1], prepared))
        blocks += [pair, swap_mask(second, 1)]
    return blocks, prepared


def prepare_kernel(
    slots, tiles, width, local_ops, slots_hbm, points_hbm, operators_hbm,
    picks_ref, code_ref, lane_ref, spans_ref, *rest
):
    *operators_refs, slots_ref, points_ref, hot, sems = rest
    copies = [
        pltpu.make_async_copy(slots_hbm, slots_ref, sems.at[0]),
        pltpu.make_async_copy(points_hbm, points_ref, sems.at[1]),
    ]
    for ref in operators_refs:
        part = operators_hbm.at[pl.ds(local_ops - ref.shape[0], ref.shape[0])]
        copies.append(pltpu.make_async_copy(part, ref, sems.at[2]))
    for copy in copies:
        copy.start()
    copies[0].wait()
    boxes = slots_ref.shape[1]
    patches = code_ref.shape[0]
    inner, outer = handled_groups()
    col = lax.axis_index("col")
    for half in range(inner):
        first = (div(col, inner) * inner + mod(col + half, inner)) * local_ops
        wanted = slots_ref[pl.ds(first, local_ops), :]
        for o in range(local_ops):
            picked = iota((slots, boxes), 0) == wanted[o : o + 1, :]
            at = (half * local_ops + o) * slots
            hot[at : at + slots, :] = jnp.where(picked, 1.0, 0.0).astype(jnp.bfloat16)
    picks_ref[...] = hot[...].T
    copies[1].wait()
    local = points_ref[...] - (lax.axis_index("box") * boxes - RIM) * width
    at_box = ((local.astype(jnp.float32) + 0.5) * (1.0 / width)).astype(jnp.int32)
    at_point = local - at_box * width
    lowest = jnp.min(at_box, axis=1, keepdims=True)
    highest = jnp.max(at_box, axis=1, keepdims=True)
    start = jnp.minimum(lowest, boxes + 2 * RIM - SPAN)
    code = (at_box - start) * tiles + div(at_point, LANES)
    lane = mod(at_point, LANES)
    for p in range(patches):
        code_ref[p] = code[p : p + 1]
        lane_ref[p] = lane[p : p + 1]
        spans_ref[p] = jnp.min(lowest[p : p + 1])
        spans_ref[patches + p] = jnp.min(highest[p : p + 1])
    for copy in copies[2:]:
        copy.wait()


def prepare_call(slots_t, patch_points, translations, load, slots, tiles):
    local_ops, width, _ = translations.shape
    inner, _ = handled_groups()
    boxes = slots_t.shape[1]
    patches, points = patch_points.shape
    all_slots = inner * local_ops * slots
    keep = pltpu.VMEM if load else jax.ShapeDtypeStruct
    return pl.pallas_call(
        functools.partial(prepare_kernel, slots, tiles, width, local_ops),
        out_shape=[
            keep((boxes, all_slots), jnp.bfloat16),
            keep((patches, 1, points), jnp.int32),
            keep((patches, 1, points), jnp.int32),
            jax.ShapeDtypeStruct((2 * patches,), jnp.int32),
        ]
        + [pltpu.VMEM((load, width, width), translations.dtype)] * (load > 0),
        in_specs=[ANY] * 3,
        out_specs=[VMEM] * 3 + [SMEM] + [VMEM] * (load > 0),
        scratch_shapes=[
            pltpu.VMEM(slots_t.shape, slots_t.dtype),
            pltpu.VMEM(patch_points.shape, patch_points.dtype),
            pltpu.VMEM((all_slots, boxes), jnp.bfloat16),
            pltpu.SemaphoreType.DMA((3,)),
        ],
        compiler_params=params(8),
    )(
        pltpu.with_memory_space_constraint(slots_t, pltpu.HBM),
        pltpu.with_memory_space_constraint(patch_points, pltpu.HBM),
        pltpu.with_memory_space_constraint(translations, pltpu.HBM),
    )


def field_kernel(share, capacity, group, arrivals, ready, pending, *refs):
    imported_refs, picks_ref, rest = refs[:arrivals], refs[arrivals], refs[arrivals + 1 :]
    *operator_refs, out_ref, edge_ref, terms, fetched, sems = rest
    ready_refs, pending_refs = operator_refs[: len(ready)], operator_refs[len(ready) :]
    work = [(at + i, ref, i, None) for at, ref in zip(ready, ready_refs) for i in range(ref.shape[0])]
    filled = 0
    for (start, count, at), ref in zip(pending, pending_refs):
        chunk = 4 if count % 4 == 0 else 1
        for i in range(0, count, chunk):
            copy = pltpu.make_async_copy(
                ref.at[pl.ds(start + i, chunk)], fetched.at[pl.ds(filled, chunk)], sems.at[filled]
            )
            copy.start()
            for k in range(chunk):
                work.append((at + i + k, fetched, filled + k, None if k else copy))
            filled += chunk
    if arrivals == 1:
        sources, per_source, width = imported_refs[0].shape
        flat = imported_refs[0][...].reshape(sources * per_source, width)
        swapped = 0
    else:
        sources = arrivals
        per_source, width = imported_refs[0].shape
        pieces = [ref[0] if len(ref.shape) == 3 else ref[...] for ref in imported_refs]
        flat = jnp.concatenate(pieces, axis=0)
        swapped = lax.axis_index("box")
    boxes = picks_ref.shape[0]
    slots = sources * capacity
    stride = terms.shape[1] // share
    tiles = stride // LANES
    arrived = sources * per_source
    shape = (share * slots, arrived)
    row = iota(shape, 0)
    slot = mod(row, slots)
    origin = (
        (div(slot, capacity) ^ swapped) * per_source
        + (group * share + div(row, slots)) * capacity
        + mod(slot, capacity)
    )
    order = jnp.where(origin == iota(shape, 1), 1.0, 0.0).astype(jnp.bfloat16)
    ordered = jnp.dot(order, flat, preferred_element_type=jnp.float32).astype(jnp.bfloat16)
    for o, ref, i, copy in work:
        if copy is not None:
            copy.wait()
        term = jnp.dot(ordered, ref[i], preferred_element_type=jnp.float32)
        term = term.astype(jnp.bfloat16)
        for c in range(share):
            terms[o * slots : (o + 1) * slots, c * stride : c * stride + width] = term[
                c * slots : (c + 1) * slots
            ]
    total = jnp.dot(picks_ref[...], terms[...], preferred_element_type=jnp.float32)
    total = total.astype(out_ref.dtype)
    for c in range(share):
        out_ref[c] = total[:, c * stride : (c + 1) * stride]
        for t in range(tiles):
            at = (c * tiles + t) * LANES
            to = pl.ds(c * tiles + t, RIM, stride=share * tiles)
            edge_ref[0, to, :] = total[:RIM, at : at + LANES].astype(jnp.float32)
            edge_ref[1, to, :] = total[boxes - RIM :, at : at + LANES].astype(jnp.float32)


def field_call(imported, picks, ready, pending, share, capacity, group, dtype):
    width = imported[0].shape[-1]
    boxes, all_slots = picks.shape
    arrivals = len(imported)
    stride = round_up(width, LANES)
    fetched = sum(count for _, _, count, _ in pending)
    held = all_slots * share * stride * 2 + fetched * width * stride * 2
    return pl.pallas_call(
        functools.partial(
            field_kernel, share, capacity, group, arrivals,
            [at for _, at in ready], [entry[1:] for entry in pending],
        ),
        out_shape=[
            jax.ShapeDtypeStruct((share, boxes, stride), dtype),
            jax.ShapeDtypeStruct((2, RIM * share * (stride // LANES), LANES), jnp.float32),
        ],
        in_specs=[VMEM] * (arrivals + 1 + len(ready)) + [ANY] * len(pending),
        out_specs=[VMEM, VMEM],
        scratch_shapes=[
            pltpu.VMEM((all_slots, share * stride), jnp.bfloat16),
            pltpu.VMEM((max(fetched, 1), width, width), jnp.bfloat16),
            pltpu.SemaphoreType.DMA((max(fetched, 1),)),
        ],
        compiler_params=params(8 + held // (1 << 20)),
        cost_estimate=pl.CostEstimate(
            flops=2 * all_slots * share * width * (width + boxes),
            bytes_accessed=all_slots * share * stride * 2,
            transcendentals=0,
        ),
    )(
        *imported,
        picks,
        *[pltpu.with_memory_space_constraint(array, pltpu.VMEM) for array, _ in ready],
        *[pltpu.with_memory_space_constraint(array, pltpu.HBM) for array, *_ in pending],
    )


def edge_kernel(share, code_ref, lane_ref, *refs):
    edge_refs, (first_ref, second_ref, rows_ref, lanes_ref) = refs[:-4], refs[-4:]
    total = edge_refs[0][...]
    for ref in edge_refs[1:]:
        total = total + ref[...].astype(jnp.bfloat16).astype(jnp.float32)
    total = total.astype(jnp.bfloat16).astype(jnp.float32)
    even = mod(lax.axis_index("box"), 2) == 0
    first_ref[...] = jnp.where(even, total[1], total[0])
    second_ref[...] = jnp.where(even, total[0], total[1])
    patches, _, points = code_ref.shape
    per_box = total.shape[1] // RIM
    tiles = per_box // share
    row = iota((rows_ref.shape[1], points), 0)
    row_code = div(row, per_box) * tiles + mod(row, tiles)
    lane = iota((LANES, points), 0)
    for p in range(patches):
        rows_ref[p] = jnp.where(row_code == code_ref[p], 1.0, 0.0).astype(jnp.bfloat16)
        lanes_ref[p] = jnp.where(lane == lane_ref[p], 1.0, 0.0).astype(jnp.bfloat16)


def edge_call(code, lane, share, *edges):
    patches, _, points = code.shape
    side = edges[0].shape[1:]
    return pl.pallas_call(
        functools.partial(edge_kernel, share),
        out_shape=[
            jax.ShapeDtypeStruct(side, jnp.float32),
            jax.ShapeDtypeStruct(side, jnp.float32),
            pltpu.VMEM((patches, SPAN * side[0] // RIM, points), jnp.bfloat16),
            pltpu.VMEM((patches, LANES, points), jnp.bfloat16),
        ],
        in_specs=[VMEM] * (2 + len(edges)),
        out_specs=[VMEM] * 4,
        compiler_params=params(4),
        cost_estimate=pl.CostEstimate(flops=10**10, bytes_accessed=0, transcendentals=0),
    )(code, lane, *edges)


def order_patches(spans_ref, order_ref, boxes):
    patches = spans_ref.shape[0] // 2
    count = jnp.int32(0)
    for wanted in (True, False):
        for p in range(patches):
            reaches = (spans_ref[p] < RIM) | (spans_ref[patches + p] >= boxes + RIM)
            order_ref[count] = p
            count = count + jnp.where(reaches == wanted, 1, 0)
        if wanted:
            first = count
    return first


def patch_batch(
    chosen, spans_ref, code_ref, lane_ref, rows_ref, lanes_ref, ext, inverses_ref, spread, share, boxes
):
    points = code_ref.shape[2]
    per_box = ext.shape[0] // (boxes + 2 * RIM)
    tiles = per_box // share
    window = SPAN * per_box
    places, products = [], []
    row = iota((window, LANES), 0)
    row_code = div(row, per_box) * tiles + mod(row, tiles)
    for p in chosen:
        start = jnp.minimum(spans_ref[p], boxes + 2 * RIM - SPAN) * per_box
        places.append(pl.ds(pl.multiple_of(start, 8), window))
        held = ext[places[-1], :]
        values = []
        for at in range(0, points, LANES):
            code = code_ref[p, :, at : at + LANES]
            lane = jnp.broadcast_to(lane_ref[p, :, at : at + LANES], (window, LANES))
            found = jnp.take_along_axis(held, lane, axis=1)
            found = jnp.where(row_code == code, found, 0.0)
            found = jnp.sum(found.reshape(SPAN, per_box, LANES), axis=0)
            values.append(jnp.sum(found.reshape(share, tiles, LANES), axis=1))
        values = jnp.concatenate(values, axis=1).astype(jnp.bfloat16)
        product = jnp.dot(values, inverses_ref[p], preferred_element_type=jnp.float32)
        products.append(product)
    for p, place, product in zip(chosen, places, products):
        product = jnp.concatenate(
            [jnp.broadcast_to(product[c : c + 1], (tiles, points)) for c in range(share)], axis=0
        ).astype(jnp.bfloat16)
        left = rows_ref[p] * jnp.concatenate([product] * SPAN, axis=0)
        placed = lax.dot_general(left, lanes_ref[p], NT, preferred_element_type=jnp.float32)
        spread[place, :] = spread[place, :] + placed


def batch_size(patches):
    return 2 if patches % 2 == 0 else 1


def early_kernel(
    spans_ref, code_ref, lane_ref, own_ref, received_ref, inverses_ref, first_ref, second_ref,
    rows_in, lanes_in,
    ext, spread, first_out, second_out, order_ref,
):
    share, boxes, stride = own_ref.shape
    tiles = stride // LANES
    per_box = share * tiles
    rim = RIM * per_box
    end = rim + boxes * per_box
    patches = code_ref.shape[0]
    even = mod(lax.axis_index("box"), 2) == 0
    first = first_ref[...]
    second = second_ref[...]
    spread[...] = jnp.zeros_like(spread)
    ext[:rim, :] = jnp.where(even, second, first)
    ext[end:, :] = jnp.where(even, first, second)
    for c in range(share):
        for t in range(tiles):
            part = own_ref[c, :, t * LANES : (t + 1) * LANES]
            for r in range(received_ref.shape[0]):
                part = part + received_ref[r, c, :, t * LANES : (t + 1) * LANES].astype(jnp.float32)
            part = part.astype(jnp.bfloat16).astype(jnp.float32)
            ext[pl.ds(rim + c * tiles + t, boxes, stride=per_box), :] = part
    batch = batch_size(patches)
    reaching = order_patches(spans_ref, order_ref, boxes)

    def step(i, carry):
        chosen = [order_ref[i * batch + k] for k in range(batch)]
        patch_batch(
            chosen, spans_ref, code_ref, lane_ref, rows_in, lanes_in, ext, inverses_ref, spread,
            share, boxes,
        )
        return carry

    lax.fori_loop(0, div(reaching + batch - 1, batch), step, 0)
    low = spread[:rim, :]
    high = spread[end:, :]
    first_out[...] = jnp.where(even, high, low)
    second_out[...] = jnp.where(even, low, high)


def late_kernel(
    spans_ref, code_ref, lane_ref, ext, early_ref, inverses_ref, rows_in, lanes_in,
    field_hbm, corrected_ref, rows_ref, spread, field_ref, order_ref, sem,
):
    share, width, boxes = field_ref.shape
    per_box = ext.shape[0] // (boxes + 2 * RIM)
    tiles = per_box // share
    rim = RIM * per_box
    end = rim + boxes * per_box
    patches = code_ref.shape[0]
    for c in range(share):
        for t in range(tiles):
            own = ext[pl.ds(rim + c * tiles + t, boxes, stride=per_box), :]
            last = min(width - t * LANES, LANES)
            field_ref[c, t * LANES : t * LANES + last, :] = own.T[:last].astype(field_ref.dtype)
    field_copy = pltpu.make_async_copy(field_ref, field_hbm, sem)
    field_copy.start()
    spread[...] = early_ref[...]
    batch = batch_size(patches)
    reaching = order_patches(spans_ref, order_ref, boxes)

    begin = div(reaching + batch - 1, batch) * batch
    for size in (2 * batch, batch):

        def step(i, carry, size=size, begin=begin):
            chosen = [order_ref[begin + i * size + k] for k in range(size)]
            patch_batch(
                chosen, spans_ref, code_ref, lane_ref, rows_in, lanes_in, ext, inverses_ref, spread,
                share, boxes,
            )
            return carry

        steps = div(patches - begin, size)
        lax.fori_loop(0, steps, step, 0)
        begin = begin + steps * size
    for c in range(share):
        for t in range(tiles):
            at = pl.ds(rim + c * tiles + t, boxes, stride=per_box)
            last = min(width - t * LANES, LANES)
            total = ext[at, :] + spread[at, :]
            to = slice(t * LANES, t * LANES + last)
            corrected_ref[c, to, :] = total.T[:last].astype(corrected_ref.dtype)
    rows_ref[:rim] = ext[rim : 2 * rim, :] + spread[rim : 2 * rim, :]
    rows_ref[rim:] = ext[end - rim : end, :] + spread[end - rim : end, :]
    field_copy.wait()


def finish_kernel(first_ref, second_ref, rows_ref, corrected_ref, out_hbm, out_ref, sems):
    share, width, boxes = corrected_ref.shape
    rim = rows_ref.shape[0] // 2
    per_box = rim // RIM
    tiles = per_box // share
    even = mod(lax.axis_index("box"), 2) == 0
    first = first_ref[...]
    second = second_ref[...]
    low = rows_ref[:rim] + jnp.where(even, second, first)
    high = rows_ref[rim:] + jnp.where(even, first, second)
    rows = jnp.concatenate([low, high], axis=0)
    point = mod(iota(rows.shape, 0), tiles) * LANES + iota(rows.shape, 1)
    rows = jnp.where(point < width, rows, 0.0).T.astype(jnp.bfloat16)
    shape = (2 * rim, per_box * boxes)
    row = iota(shape, 0)
    box = div(mod(row, rim), per_box) + jnp.where(row < rim, 0, boxes - RIM)
    target = mod(row, per_box) * boxes + box
    place = jnp.where(target == iota(shape, 1), 1.0, 0.0).astype(jnp.bfloat16)
    placed = jnp.dot(rows, place, preferred_element_type=jnp.float32)
    box = iota((LANES, boxes), 1)
    edge = (box < RIM) | (box >= boxes - RIM)
    for c in range(share):
        for t in range(tiles):
            last = min(width - t * LANES, LANES)
            at = (c * tiles + t) * boxes
            to = slice(t * LANES, t * LANES + last)
            kept = corrected_ref[c, to, :].astype(jnp.float32)
            out_ref[c, to, :] = jnp.where(
                edge[:last], placed[:last, at : at + boxes], kept
            ).astype(out_ref.dtype)
        pltpu.make_async_copy(out_ref.at[c], out_hbm.at[c], sems.at[c]).start()
    for c in range(share):
        pltpu.make_async_copy(out_ref.at[c], out_hbm.at[c], sems.at[c]).wait()


def swap_sides(first, second):
    count = lax.axis_size("box")

    def moves(start):
        pairs = [(i, i + 1) for i in range(start, count - 1, 2)]
        return pairs + [(b, a) for a, b in pairs]

    return lax.ppermute(first, "box", moves(0)), lax.ppermute(second, "box", moves(1))


def body(density, export_ids, list_slot, translations, patch_points, inverses):
    boxes, total_cols, width = density.shape
    inner, outer = handled_groups()
    share = total_cols // (inner * outer)
    capacity = export_ids.shape[2]
    sources = export_ids.shape[1]
    patches, points = patch_points.shape
    stride = round_up(width, LANES)
    tiles = stride // LANES
    per_box = share * tiles
    places = [(h, k) for h in range(outer) for k in range(inner)]

    others = []
    for i in range(1, inner):
        moves = [(h * inner + (k + i) % inner, h * inner + k) for h, k in places]
        others.append(lax.ppermute(translations, "col", moves))

    swaps = sources <= 16 and sources & (sources - 1) == 0
    local_ops = translations.shape[0]
    early = EARLY_OPS if swaps else 0
    load = local_ops - early if swaps else 0
    outgoing = pick_call(export_ids, density, translations, share, swaps, early)
    ready = []
    if early:
        *outgoing, first_ops = outgoing
        ready.append((first_ops, 0))
    if swaps:
        pairs = swap_far(outgoing)
    else:
        imported = [lax.all_to_all(outgoing[0], "box", split_axis=0, concat_axis=0, tiled=True)]

    _, *later = lax.optimization_barrier(
        (outgoing[-1], list_slot.T, patch_points, translations)
    )
    prepared = list(prepare_call(*later, load, sources * capacity, tiles))
    if swaps:
        imported, prepared[3] = swap_near(outgoing, pairs, prepared[3])
    picks, code, lane, spans, *loaded = prepared
    arrived = [(other, (i + 1) * local_ops) for i, other in enumerate(others)]
    pending = []
    if swaps:
        ready += [(array, early) for array in loaded] + arrived
    else:
        pending = [(array, 0, local_ops, at) for array, at in [(translations, 0)] + arrived]
    parts, edges = [], []
    for j in range(1, outer):
        part, edge = field_call(
            imported, picks, ready, pending, share, capacity, j, jnp.bfloat16
        )
        moves = [(h * inner + k, ((h + j) % outer) * inner + k) for h, k in places]
        edges.append(lax.ppermute(edge, "col", moves))
        parts.append(lax.ppermute(part, "col", moves))
    own, edge = field_call(imported, picks, ready, pending, share, capacity, 0, jnp.float32)
    first, second, *masks = edge_call(code, lane, share, edge, *edges)
    first, second = swap_sides(first, second)
    received = jnp.stack(parts)

    ext_rows = (boxes + 2 * RIM) * per_box
    rim = RIM * per_box
    side = jax.ShapeDtypeStruct((rim, LANES), jnp.float32)
    ext, early, first, second = pl.pallas_call(
        early_kernel,
        out_shape=[
            pltpu.VMEM((ext_rows, LANES), jnp.float32),
            pltpu.VMEM((ext_rows, LANES), jnp.float32),
            side,
            side,
        ],
        in_specs=[SMEM] + [VMEM] * 9,
        out_specs=[VMEM] * 4,
        scratch_shapes=[pltpu.SMEM((patches + 1,), jnp.int32)],
        compiler_params=params(10),
    )(spans, code, lane, own, received, inverses, first, second, *masks)
    first, second = swap_sides(first, second)

    field_t, corrected_t, rows = pl.pallas_call(
        late_kernel,
        out_shape=[
            jax.ShapeDtypeStruct((share, width, boxes), jnp.bfloat16),
            pltpu.VMEM((share, width, boxes), jnp.bfloat16),
            pltpu.VMEM((2 * rim, LANES), jnp.float32),
        ],
        in_specs=[SMEM] + [VMEM] * 7,
        out_specs=[ANY, VMEM, VMEM],
        scratch_shapes=[
            pltpu.VMEM((ext_rows, LANES), jnp.float32),
            pltpu.VMEM((share, width, boxes), jnp.bfloat16),
            pltpu.SMEM((patches + 1,), jnp.int32),
            pltpu.SemaphoreType.DMA,
        ],
        compiler_params=params(10),
        cost_estimate=pl.CostEstimate(
            flops=2 * patches * share * points * points,
            bytes_accessed=patches * points * points * 2,
            transcendentals=0,
        ),
    )(spans, code, lane, ext, early, inverses, *masks)

    corrected_t = pl.pallas_call(
        finish_kernel,
        out_shape=jax.ShapeDtypeStruct(corrected_t.shape, corrected_t.dtype),
        in_specs=[VMEM] * 4,
        out_specs=ANY,
        scratch_shapes=[
            pltpu.VMEM(corrected_t.shape, corrected_t.dtype),
            pltpu.SemaphoreType.DMA((share,)),
        ],
        compiler_params=params(8),
    )(first, second, rows, corrected_t)
    return jnp.transpose(field_t, (2, 0, 1)), jnp.transpose(corrected_t, (2, 0, 1))


def solution(mesh):
    return jax.shard_map(
        body,
        mesh=mesh,
        in_specs=(
            P("box", None, None),
            P("box", None, None),
            P("box", None),
            P("col", None, None),
            P("box", None),
            P("box", None, None),
        ),
        out_specs=(P("box", "col", None), P("box", "col", None)),
        check_vma=False,
    )
```

```python
import functools

import jax
import jax.numpy as jnp
from jax import lax
from jax.experimental import pallas as pl
from jax.experimental.pallas import tpu as pltpu
from jax.sharding import PartitionSpec as P

RIM = 2
SPAN = 8
EARLY_OPS = 4
LANES = 128
NT = (((1,), (1,)), ((), ()))
ANY = pl.BlockSpec(memory_space=pl.ANY)
VMEM = pl.BlockSpec(memory_space=pltpu.VMEM)
SMEM = pl.BlockSpec(memory_space=pltpu.SMEM)


def round_up(n, m):
    return -(-n // m) * m


def params(limit):
    return pltpu.CompilerParams(vmem_limit_bytes=limit << 20)


def iota(shape, dim):
    return lax.broadcasted_iota(jnp.int32, shape, dim)


def div(x, n):
    if n & (n - 1) == 0:
        return x >> (n.bit_length() - 1)
    return lax.div(x, jnp.int32(n))


def mod(x, n):
    if n & (n - 1) == 0:
        return x & (n - 1)
    return lax.rem(x, jnp.int32(n))


def handled_groups():
    groups = lax.axis_size("col")
    inner = 2 if groups % 2 == 0 else 1
    return inner, groups // inner


def pick_kernel(share, swaps, load, ids_hbm, density_ref, operators_hbm, *rest):
    out_refs, (ids_ref, block, sems) = rest[:-3], rest[-3:]
    if load:
        *out_refs, operators_ref = out_refs
    capacity, dests = ids_ref.shape
    cols, width, boxes = block.shape
    inner, outer = handled_groups()
    col = lax.axis_index("col")
    ids_copy = pltpu.make_async_copy(ids_hbm, ids_ref, sems.at[outer])
    ids_copy.start()
    copies = []
    for j in range(outer):
        group = mod(div(col, inner) + j, outer) * inner + mod(col, inner)
        copy = pltpu.make_async_copy(
            density_ref.at[pl.ds(group * share, share)],
            block.at[pl.ds(j * share, share)],
            sems.at[j],
        )
        copy.start()
        copies.append(copy)
    if load:
        operators_copy = pltpu.make_async_copy(
            operators_hbm.at[pl.ds(0, load)], operators_ref, sems.at[outer + 1]
        )
        operators_copy.start()
    ids_copy.wait()
    rows = dests * cols * capacity
    row = iota((rows, boxes), 0)
    dest = div(row, cols * capacity)
    if swaps:
        dest = dest ^ lax.axis_index("box")
    pair = dest * capacity + mod(row, capacity)
    column = mod(div(row, capacity), cols)

    def place(k, wanted):
        return jnp.where(pair == k, ids_ref[mod(k, capacity), div(k, capacity)], wanted)

    wanted = jnp.full((rows, boxes), -1, jnp.int32)
    if dests * capacity <= 64:
        for k in range(dests * capacity):
            wanted = place(jnp.int32(k), wanted)
    else:
        wanted = lax.fori_loop(0, dests * capacity, place, wanted)
    hit = wanted == iota((rows, boxes), 1)
    for copy in copies:
        copy.wait()
    total = jnp.zeros((rows, width), jnp.float32)
    for c in range(cols):
        chosen = jnp.where(hit & (column == c), 1.0, 0.0).astype(jnp.bfloat16)
        total = total + lax.dot_general(
            chosen, block[c], NT, preferred_element_type=jnp.float32
        )
    total = total.astype(out_refs[0].dtype).reshape(dests, cols * capacity, width)
    if not swaps:
        out_refs[0][...] = total
        return
    for k, ref in enumerate(out_refs[:-1]):
        ref[...] = total[2 * k]
        out_refs[-1][k] = total[2 * k + 1]
    if load:
        operators_copy.wait()


def pick_call(export_ids, density, translations, share, swaps, load):
    boxes, _, width = density.shape
    _, sources, capacity = export_ids.shape
    _, outer = handled_groups()
    block = (outer * share * capacity, width)
    if swaps:
        shapes = [block] * (sources // 2) + [(sources // 2,) + block]
    else:
        shapes = [(sources,) + block]
    return pl.pallas_call(
        functools.partial(pick_kernel, share, swaps, load),
        out_shape=[jax.ShapeDtypeStruct(shape, density.dtype) for shape in shapes]
        + [pltpu.VMEM((load,) + translations.shape[1:], translations.dtype)] * (load > 0),
        in_specs=[ANY] * 3,
        out_specs=[VMEM] * (len(shapes) + (load > 0)),
        scratch_shapes=[
            pltpu.SMEM((capacity, sources), jnp.int32),
            pltpu.VMEM((outer * share, width, boxes), density.dtype),
            pltpu.SemaphoreType.DMA((outer + 2,)),
        ],
        compiler_params=params(8),
    )(
        pltpu.with_memory_space_constraint(export_ids[0].T, pltpu.HBM),
        pltpu.with_memory_space_constraint(jnp.transpose(density, (1, 2, 0)), pltpu.HBM),
        pltpu.with_memory_space_constraint(translations, pltpu.HBM),
    )


def swap_blocks(outgoing):
    *keeps, send = outgoing
    count = lax.axis_size("box")

    def swap(x, mask):
        return lax.ppermute(x, "box", [(i, i ^ mask) for i in range(count)])

    received = swap(send, 1)
    blocks = [keeps[0], received]
    for k in range(1, len(keeps)):
        blocks += [swap(keeps[k], 2 * k), swap(received[k], 2 * k)]
    return blocks


def prepare_kernel(
    slots, tiles, width, local_ops, slots_hbm, points_hbm, operators_hbm,
    picks_ref, code_ref, lane_ref, spans_ref, *rest
):
    *operators_refs, slots_ref, points_ref, hot, sems = rest
    copies = [
        pltpu.make_async_copy(slots_hbm, slots_ref, sems.at[0]),
        pltpu.make_async_copy(points_hbm, points_ref, sems.at[1]),
    ]
    for ref in operators_refs:
        part = operators_hbm.at[pl.ds(local_ops - ref.shape[0], ref.shape[0])]
        copies.append(pltpu.make_async_copy(part, ref, sems.at[2]))
    for copy in copies:
        copy.start()
    copies[0].wait()
    boxes = slots_ref.shape[1]
    patches = code_ref.shape[0]
    inner, outer = handled_groups()
    col = lax.axis_index("col")
    for half in range(inner):
        first = (div(col, inner) * inner + mod(col + half, inner)) * local_ops
        wanted = slots_ref[pl.ds(first, local_ops), :]
        for o in range(local_ops):
            picked = iota((slots, boxes), 0) == wanted[o : o + 1, :]
            at = (half * local_ops + o) * slots
            hot[at : at + slots, :] = jnp.where(picked, 1.0, 0.0).astype(jnp.bfloat16)
    picks_ref[...] = hot[...].T
    copies[1].wait()
    local = points_ref[...] - (lax.axis_index("box") * boxes - RIM) * width
    at_box = ((local.astype(jnp.float32) + 0.5) * (1.0 / width)).astype(jnp.int32)
    at_point = local - at_box * width
    lowest = jnp.min(at_box, axis=1, keepdims=True)
    highest = jnp.max(at_box, axis=1, keepdims=True)
    start = jnp.minimum(lowest, boxes + 2 * RIM - SPAN)
    code = (at_box - start) * tiles + div(at_point, LANES)
    lane = mod(at_point, LANES)
    for p in range(patches):
        code_ref[p] = code[p : p + 1]
        lane_ref[p] = lane[p : p + 1]
        spans_ref[p] = jnp.min(lowest[p : p + 1])
        spans_ref[patches + p] = jnp.min(highest[p : p + 1])
    for copy in copies[2:]:
        copy.wait()


def prepare_call(slots_t, patch_points, translations, load, slots, tiles):
    local_ops, width, _ = translations.shape
    inner, _ = handled_groups()
    boxes = slots_t.shape[1]
    patches, points = patch_points.shape
    all_slots = inner * local_ops * slots
    keep = pltpu.VMEM if load else jax.ShapeDtypeStruct
    return pl.pallas_call(
        functools.partial(prepare_kernel, slots, tiles, width, local_ops),
        out_shape=[
            keep((boxes, all_slots), jnp.bfloat16),
            keep((patches, 1, points), jnp.int32),
            keep((patches, 1, points), jnp.int32),
            jax.ShapeDtypeStruct((2 * patches,), jnp.int32),
        ]
        + [pltpu.VMEM((load, width, width), translations.dtype)] * (load > 0),
        in_specs=[ANY] * 3,
        out_specs=[VMEM] * 3 + [SMEM] + [VMEM] * (load > 0),
        scratch_shapes=[
            pltpu.VMEM(slots_t.shape, slots_t.dtype),
            pltpu.VMEM(patch_points.shape, patch_points.dtype),
            pltpu.VMEM((all_slots, boxes), jnp.bfloat16),
            pltpu.SemaphoreType.DMA((3,)),
        ],
        compiler_params=params(8),
    )(
        pltpu.with_memory_space_constraint(slots_t, pltpu.HBM),
        pltpu.with_memory_space_constraint(patch_points, pltpu.HBM),
        pltpu.with_memory_space_constraint(translations, pltpu.HBM),
    )


def field_kernel(share, capacity, group, arrivals, ready, pending, *refs):
    imported_refs, picks_ref, rest = refs[:arrivals], refs[arrivals], refs[arrivals + 1 :]
    *operator_refs, out_ref, edge_ref, terms, fetched, sems = rest
    ready_refs, pending_refs = operator_refs[: len(ready)], operator_refs[len(ready) :]
    work = [(at + i, ref, i, None) for at, ref in zip(ready, ready_refs) for i in range(ref.shape[0])]
    filled = 0
    for (start, count, at), ref in zip(pending, pending_refs):
        chunk = 4 if count % 4 == 0 else 1
        for i in range(0, count, chunk):
            copy = pltpu.make_async_copy(
                ref.at[pl.ds(start + i, chunk)], fetched.at[pl.ds(filled, chunk)], sems.at[filled]
            )
            copy.start()
            for k in range(chunk):
                work.append((at + i + k, fetched, filled + k, None if k else copy))
            filled += chunk
    if arrivals == 1:
        sources, per_source, width = imported_refs[0].shape
        flat = imported_refs[0][...].reshape(sources * per_source, width)
        swapped = 0
    else:
        sources = arrivals
        per_source, width = imported_refs[0].shape
        pieces = [ref[0] if i == 1 else ref[...] for i, ref in enumerate(imported_refs)]
        flat = jnp.concatenate(pieces, axis=0)
        swapped = lax.axis_index("box")
    boxes = picks_ref.shape[0]
    slots = sources * capacity
    stride = terms.shape[1] // share
    tiles = stride // LANES
    arrived = sources * per_source
    shape = (share * slots, arrived)
    row = iota(shape, 0)
    slot = mod(row, slots)
    origin = (
        (div(slot, capacity) ^ swapped) * per_source
        + (group * share + div(row, slots)) * capacity
        + mod(slot, capacity)
    )
    order = jnp.where(origin == iota(shape, 1), 1.0, 0.0).astype(jnp.bfloat16)
    ordered = jnp.dot(order, flat, preferred_element_type=jnp.float32).astype(jnp.bfloat16)
    for o, ref, i, copy in work:
        if copy is not None:
            copy.wait()
        term = jnp.dot(ordered, ref[i], preferred_element_type=jnp.float32)
        term = term.astype(jnp.bfloat16)
        for c in range(share):
            terms[o * slots : (o + 1) * slots, c * stride : c * stride + width] = term[
                c * slots : (c + 1) * slots
            ]
    total = jnp.dot(picks_ref[...], terms[...], preferred_element_type=jnp.float32)
    total = total.astype(out_ref.dtype)
    for c in range(share):
        out_ref[c] = total[:, c * stride : (c + 1) * stride]
        for t in range(tiles):
            at = (c * tiles + t) * LANES
            to = pl.ds(c * tiles + t, RIM, stride=share * tiles)
            edge_ref[0, to, :] = total[:RIM, at : at + LANES].astype(jnp.float32)
            edge_ref[1, to, :] = total[boxes - RIM :, at : at + LANES].astype(jnp.float32)


def field_call(imported, picks, ready, pending, share, capacity, group, dtype):
    width = imported[0].shape[-1]
    boxes, all_slots = picks.shape
    arrivals = len(imported)
    stride = round_up(width, LANES)
    fetched = sum(count for _, _, count, _ in pending)
    held = all_slots * share * stride * 2 + fetched * width * stride * 2
    return pl.pallas_call(
        functools.partial(
            field_kernel, share, capacity, group, arrivals,
            [at for _, at in ready], [entry[1:] for entry in pending],
        ),
        out_shape=[
            jax.ShapeDtypeStruct((share, boxes, stride), dtype),
            jax.ShapeDtypeStruct((2, RIM * share * (stride // LANES), LANES), jnp.float32),
        ],
        in_specs=[VMEM] * (arrivals + 1 + len(ready)) + [ANY] * len(pending),
        out_specs=[VMEM, VMEM],
        scratch_shapes=[
            pltpu.VMEM((all_slots, share * stride), jnp.bfloat16),
            pltpu.VMEM((max(fetched, 1), width, width), jnp.bfloat16),
            pltpu.SemaphoreType.DMA((max(fetched, 1),)),
        ],
        compiler_params=params(8 + held // (1 << 20)),
        cost_estimate=pl.CostEstimate(
            flops=2 * all_slots * share * width * (width + boxes),
            bytes_accessed=all_slots * share * stride * 2,
            transcendentals=0,
        ),
    )(
        *imported,
        picks,
        *[pltpu.with_memory_space_constraint(array, pltpu.VMEM) for array, _ in ready],
        *[pltpu.with_memory_space_constraint(array, pltpu.HBM) for array, *_ in pending],
    )


def edge_kernel(share, code_ref, lane_ref, *refs):
    edge_refs, (first_ref, second_ref, rows_ref, lanes_ref) = refs[:-4], refs[-4:]
    total = edge_refs[0][...]
    for ref in edge_refs[1:]:
        total = total + ref[...].astype(jnp.bfloat16).astype(jnp.float32)
    total = total.astype(jnp.bfloat16).astype(jnp.float32)
    even = mod(lax.axis_index("box"), 2) == 0
    first_ref[...] = jnp.where(even, total[1], total[0])
    second_ref[...] = jnp.where(even, total[0], total[1])
    patches, _, points = code_ref.shape
    per_box = total.shape[1] // RIM
    tiles = per_box // share
    row = iota((rows_ref.shape[1], points), 0)
    row_code = div(row, per_box) * tiles + mod(row, tiles)
    lane = iota((LANES, points), 0)
    for p in range(patches):
        rows_ref[p] = jnp.where(row_code == code_ref[p], 1.0, 0.0).astype(jnp.bfloat16)
        lanes_ref[p] = jnp.where(lane == lane_ref[p], 1.0, 0.0).astype(jnp.bfloat16)


def edge_call(code, lane, share, *edges):
    patches, _, points = code.shape
    side = edges[0].shape[1:]
    return pl.pallas_call(
        functools.partial(edge_kernel, share),
        out_shape=[
            jax.ShapeDtypeStruct(side, jnp.float32),
            jax.ShapeDtypeStruct(side, jnp.float32),
            pltpu.VMEM((patches, SPAN * side[0] // RIM, points), jnp.bfloat16),
            pltpu.VMEM((patches, LANES, points), jnp.bfloat16),
        ],
        in_specs=[VMEM] * (2 + len(edges)),
        out_specs=[VMEM] * 4,
        compiler_params=params(4),
        cost_estimate=pl.CostEstimate(flops=10**10, bytes_accessed=0, transcendentals=0),
    )(code, lane, *edges)


def order_patches(spans_ref, order_ref, boxes):
    patches = spans_ref.shape[0] // 2
    count = jnp.int32(0)
    for wanted in (True, False):
        for p in range(patches):
            reaches = (spans_ref[p] < RIM) | (spans_ref[patches + p] >= boxes + RIM)
            order_ref[count] = p
            count = count + jnp.where(reaches == wanted, 1, 0)
        if wanted:
            first = count
    return first


def patch_batch(
    chosen, spans_ref, code_ref, lane_ref, rows_ref, lanes_ref, ext, inverses_ref, spread, share, boxes
):
    points = code_ref.shape[2]
    per_box = ext.shape[0] // (boxes + 2 * RIM)
    tiles = per_box // share
    window = SPAN * per_box
    places, products = [], []
    row = iota((window, LANES), 0)
    row_code = div(row, per_box) * tiles + mod(row, tiles)
    for p in chosen:
        start = jnp.minimum(spans_ref[p], boxes + 2 * RIM - SPAN) * per_box
        places.append(pl.ds(pl.multiple_of(start, 8), window))
        held = ext[places[-1], :]
        values = []
        for at in range(0, points, LANES):
            code = code_ref[p, :, at : at + LANES]
            lane = jnp.broadcast_to(lane_ref[p, :, at : at + LANES], (window, LANES))
            found = jnp.take_along_axis(held, lane, axis=1)
            found = jnp.where(row_code == code, found, 0.0)
            found = jnp.sum(found.reshape(SPAN, per_box, LANES), axis=0)
            values.append(jnp.sum(found.reshape(share, tiles, LANES), axis=1))
        values = jnp.concatenate(values, axis=1).astype(jnp.bfloat16)
        product = jnp.dot(values, inverses_ref[p], preferred_element_type=jnp.float32)
        products.append(product)
    for p, place, product in zip(chosen, places, products):
        product = jnp.concatenate(
            [jnp.broadcast_to(product[c : c + 1], (tiles, points)) for c in range(share)], axis=0
        ).astype(jnp.bfloat16)
        left = rows_ref[p] * jnp.concatenate([product] * SPAN, axis=0)
        placed = lax.dot_general(left, lanes_ref[p], NT, preferred_element_type=jnp.float32)
        spread[place, :] = spread[place, :] + placed


def batch_size(patches):
    return 2 if patches % 2 == 0 else 1


def early_kernel(
    spans_ref, code_ref, lane_ref, own_ref, received_ref, inverses_ref, first_ref, second_ref,
    rows_in, lanes_in,
    ext, spread, first_out, second_out, order_ref,
):
    share, boxes, stride = own_ref.shape
    tiles = stride // LANES
    per_box = share * tiles
    rim = RIM * per_box
    end = rim + boxes * per_box
    patches = code_ref.shape[0]
    even = mod(lax.axis_index("box"), 2) == 0
    first = first_ref[...]
    second = second_ref[...]
    spread[...] = jnp.zeros_like(spread)
    ext[:rim, :] = jnp.where(even, second, first)
    ext[end:, :] = jnp.where(even, first, second)
    for c in range(share):
        for t in range(tiles):
            part = own_ref[c, :, t * LANES : (t + 1) * LANES]
            for r in range(received_ref.shape[0]):
                part = part + received_ref[r, c, :, t * LANES : (t + 1) * LANES].astype(jnp.float32)
            part = part.astype(jnp.bfloat16).astype(jnp.float32)
            ext[pl.ds(rim + c * tiles + t, boxes, stride=per_box), :] = part
    batch = batch_size(patches)
    reaching = order_patches(spans_ref, order_ref, boxes)

    def step(i, carry):
        chosen = [order_ref[i * batch + k] for k in range(batch)]
        patch_batch(
            chosen, spans_ref, code_ref, lane_ref, rows_in, lanes_in, ext, inverses_ref, spread,
            share, boxes,
        )
        return carry

    lax.fori_loop(0, div(reaching + batch - 1, batch), step, 0)
    low = spread[:rim, :]
    high = spread[end:, :]
    first_out[...] = jnp.where(even, high, low)
    second_out[...] = jnp.where(even, low, high)


def late_kernel(
    spans_ref, code_ref, lane_ref, ext, early_ref, inverses_ref, rows_in, lanes_in,
    field_hbm, corrected_ref, rows_ref, spread, field_ref, order_ref, sem,
):
    share, width, boxes = field_ref.shape
    per_box = ext.shape[0] // (boxes + 2 * RIM)
    tiles = per_box // share
    rim = RIM * per_box
    end = rim + boxes * per_box
    patches = code_ref.shape[0]
    for c in range(share):
        for t in range(tiles):
            own = ext[pl.ds(rim + c * tiles + t, boxes, stride=per_box), :]
            last = min(width - t * LANES, LANES)
            field_ref[c, t * LANES : t * LANES + last, :] = own.T[:last].astype(field_ref.dtype)
    field_copy = pltpu.make_async_copy(field_ref, field_hbm, sem)
    field_copy.start()
    spread[...] = early_ref[...]
    batch = batch_size(patches)
    reaching = order_patches(spans_ref, order_ref, boxes)

    begin = div(reaching + batch - 1, batch) * batch
    for size in (3 * batch, batch):

        def step(i, carry, size=size, begin=begin):
            chosen = [order_ref[begin + i * size + k] for k in range(size)]
            patch_batch(
                chosen, spans_ref, code_ref, lane_ref, rows_in, lanes_in, ext, inverses_ref, spread,
                share, boxes,
            )
            return carry

        steps = div(patches - begin, size)
        lax.fori_loop(0, steps, step, 0)
        begin = begin + steps * size
    for c in range(share):
        for t in range(tiles):
            at = pl.ds(rim + c * tiles + t, boxes, stride=per_box)
            last = min(width - t * LANES, LANES)
            total = ext[at, :] + spread[at, :]
            to = slice(t * LANES, t * LANES + last)
            corrected_ref[c, to, :] = total.T[:last].astype(corrected_ref.dtype)
    rows_ref[:rim] = ext[rim : 2 * rim, :] + spread[rim : 2 * rim, :]
    rows_ref[rim:] = ext[end - rim : end, :] + spread[end - rim : end, :]
    field_copy.wait()


def finish_kernel(first_ref, second_ref, rows_ref, corrected_ref, out_hbm, out_ref, sems):
    share, width, boxes = corrected_ref.shape
    rim = rows_ref.shape[0] // 2
    per_box = rim // RIM
    tiles = per_box // share
    even = mod(lax.axis_index("box"), 2) == 0
    first = first_ref[...]
    second = second_ref[...]
    low = rows_ref[:rim] + jnp.where(even, second, first)
    high = rows_ref[rim:] + jnp.where(even, first, second)
    rows = jnp.concatenate([low, high], axis=0)
    point = mod(iota(rows.shape, 0), tiles) * LANES + iota(rows.shape, 1)
    rows = jnp.where(point < width, rows, 0.0).T.astype(jnp.bfloat16)
    shape = (2 * rim, per_box * boxes)
    row = iota(shape, 0)
    box = div(mod(row, rim), per_box) + jnp.where(row < rim, 0, boxes - RIM)
    target = mod(row, per_box) * boxes + box
    place = jnp.where(target == iota(shape, 1), 1.0, 0.0).astype(jnp.bfloat16)
    placed = jnp.dot(rows, place, preferred_element_type=jnp.float32)
    box = iota((LANES, boxes), 1)
    edge = (box < RIM) | (box >= boxes - RIM)
    for c in range(share):
        for t in range(tiles):
            last = min(width - t * LANES, LANES)
            at = (c * tiles + t) * boxes
            to = slice(t * LANES, t * LANES + last)
            kept = corrected_ref[c, to, :].astype(jnp.float32)
            out_ref[c, to, :] = jnp.where(
                edge[:last], placed[:last, at : at + boxes], kept
            ).astype(out_ref.dtype)
        pltpu.make_async_copy(out_ref.at[c], out_hbm.at[c], sems.at[c]).start()
    for c in range(share):
        pltpu.make_async_copy(out_ref.at[c], out_hbm.at[c], sems.at[c]).wait()


def swap_sides(first, second):
    count = lax.axis_size("box")

    def moves(start):
        pairs = [(i, i + 1) for i in range(start, count - 1, 2)]
        return pairs + [(b, a) for a, b in pairs]

    return lax.ppermute(first, "box", moves(0)), lax.ppermute(second, "box", moves(1))


def body(density, export_ids, list_slot, translations, patch_points, inverses):
    boxes, total_cols, width = density.shape
    inner, outer = handled_groups()
    share = total_cols // (inner * outer)
    capacity = export_ids.shape[2]
    sources = export_ids.shape[1]
    patches, points = patch_points.shape
    stride = round_up(width, LANES)
    tiles = stride // LANES
    per_box = share * tiles
    places = [(h, k) for h in range(outer) for k in range(inner)]

    others = []
    for i in range(1, inner):
        moves = [(h * inner + (k + i) % inner, h * inner + k) for h, k in places]
        others.append(lax.ppermute(translations, "col", moves))

    swaps = sources <= 16 and sources & (sources - 1) == 0
    local_ops = translations.shape[0]
    early = EARLY_OPS if swaps else 0
    load = local_ops - early if swaps else 0
    outgoing = pick_call(export_ids, density, translations, share, swaps, early)
    ready = []
    if early:
        *outgoing, first_ops = outgoing
        ready.append((first_ops, 0))
    if swaps:
        imported = swap_blocks(outgoing)
    else:
        imported = [lax.all_to_all(outgoing[0], "box", split_axis=0, concat_axis=0, tiled=True)]

    _, *later = lax.optimization_barrier(
        (outgoing[-1], list_slot.T, patch_points, translations)
    )
    picks, code, lane, spans, *loaded = prepare_call(*later, load, sources * capacity, tiles)
    arrived = [(other, (i + 1) * local_ops) for i, other in enumerate(others)]
    pending = []
    if swaps:
        ready += [(array, early) for array in loaded] + arrived
    else:
        pending = [(array, 0, local_ops, at) for array, at in [(translations, 0)] + arrived]
    parts, edges = [], []
    for j in range(1, outer):
        part, edge = field_call(
            imported, picks, ready, pending, share, capacity, j, jnp.bfloat16
        )
        moves = [(h * inner + k, ((h + j) % outer) * inner + k) for h, k in places]
        edges.append(lax.ppermute(edge, "col", moves))
        parts.append(lax.ppermute(part, "col", moves))
    own, edge = field_call(imported, picks, ready, pending, share, capacity, 0, jnp.float32)
    first, second, *masks = edge_call(code, lane, share, edge, *edges)
    first, second = swap_sides(first, second)
    received = jnp.stack(parts)

    ext_rows = (boxes + 2 * RIM) * per_box
    rim = RIM * per_box
    side = jax.ShapeDtypeStruct((rim, LANES), jnp.float32)
    ext, early, first, second = pl.pallas_call(
        early_kernel,
        out_shape=[
            pltpu.VMEM((ext_rows, LANES), jnp.float32),
            pltpu.VMEM((ext_rows, LANES), jnp.float32),
            side,
            side,
        ],
        in_specs=[SMEM] + [VMEM] * 9,
        out_specs=[VMEM] * 4,
        scratch_shapes=[pltpu.SMEM((patches + 1,), jnp.int32)],
        compiler_params=params(10),
    )(spans, code, lane, own, received, inverses, first, second, *masks)
    first, second = swap_sides(first, second)

    field_t, corrected_t, rows = pl.pallas_call(
        late_kernel,
        out_shape=[
            jax.ShapeDtypeStruct((share, width, boxes), jnp.bfloat16),
            pltpu.VMEM((share, width, boxes), jnp.bfloat16),
            pltpu.VMEM((2 * rim, LANES), jnp.float32),
        ],
        in_specs=[SMEM] + [VMEM] * 7,
        out_specs=[ANY, VMEM, VMEM],
        scratch_shapes=[
            pltpu.VMEM((ext_rows, LANES), jnp.float32),
            pltpu.VMEM((share, width, boxes), jnp.bfloat16),
            pltpu.SMEM((patches + 1,), jnp.int32),
            pltpu.SemaphoreType.DMA,
        ],
        compiler_params=params(10),
        cost_estimate=pl.CostEstimate(
            flops=2 * patches * share * points * points,
            bytes_accessed=patches * points * points * 2,
            transcendentals=0,
        ),
    )(spans, code, lane, ext, early, inverses, *masks)

    corrected_t = pl.pallas_call(
        finish_kernel,
        out_shape=jax.ShapeDtypeStruct(corrected_t.shape, corrected_t.dtype),
        in_specs=[VMEM] * 4,
        out_specs=ANY,
        scratch_shapes=[
            pltpu.VMEM(corrected_t.shape, corrected_t.dtype),
            pltpu.SemaphoreType.DMA((share,)),
        ],
        compiler_params=params(8),
    )(first, second, rows, corrected_t)
    return jnp.transpose(field_t, (2, 0, 1)), jnp.transpose(corrected_t, (2, 0, 1))


def solution(mesh):
    return jax.shard_map(
        body,
        mesh=mesh,
        in_specs=(
            P("box", None, None),
            P("box", None, None),
            P("box", None),
            P("col", None, None),
            P("box", None),
            P("box", None, None),
        ),
        out_specs=(P("box", "col", None), P("box", "col", None)),
        check_vma=False,
    )
```
